32 devices in a mesh: tile: 8 (over z, y), grp: 4 (over x, core).
Axes of the slice: x: 2, y: 2, z: 4, core: 2. Of those that a mesh axis runs over, the one named last changes fastest.
Arguments:
- velocity: float32 [3, 64, 256, 512], P(None, 'grp', 'tile'), may hold values from -6 to 6
- modes: float32 [128, 98304], P(None, ('tile', 'grp')), may hold values from -6 to 6
- mode_weights: float32 [128], replicated, may hold values from 1 to 10
- history: float32 [63, 98304], P(None, ('tile', 'grp')), may hold values from -6 to 6
- slab_ids: int32 [32768], P(('tile', 'grp')), may hold values from 0 to 262143
- snap_steps: int32 [64], replicated, may hold values from 0 to 63, each once
Outputs:
- advanced: float32 [3, 64, 256, 512], P(None, 'grp', 'tile')
- basis: float32 [192, 98304], P(None, ('tile', 'grp'))
- factor: float32 [192, 192], replicated
The draws below stay inside these ranges and needn't reach their ends.
Inputs may be any that keep to these rules, and one draw needn't show every extreme that they name: `slab_ids`: each id is a cell of the owning device's block. `snap_steps`: each step index appears once.
All inputs are finite; a program needn't handle non-finite values.
Results may differ from the reference program's by a relative error of at most 0.000098.
Values sent between devices are 32-bit elements; how exact they have to be, the bound alone decides.
No kernel may reach another device: no remote copies, remote signals or barrier semaphores. Data moves between devices by JAX's collectives and lax.ppermute only.
A program may use at most 320 MiB of HBM per device.

```python
import math
import jax
import jax.numpy as jnp
from jax import lax

CX = 16
CY = 32
CZ = 512
SLAB_DEV = 1024
MODES = 128
SNAPS = 64
NX = 64
NY = 256
SLAB = 32768
ROWS = 98304
N_TILE = 8
N_GRP = 4
DEVICES = 32


def touch_ends(values, rng, smallest, top_value):
    shape = values.shape
    place = [jax.random.randint(jax.random.fold_in(rng, axis), (), 0, shape[axis]) for axis in range(len(shape))]
    values = values.at[tuple(place)].set(smallest)
    longest = shape.index(max(shape))
    place[longest] = (place[longest] + 1) % shape[longest]
    return values.at[tuple(place)].set(top_value)


def steps_of(stream_key, dims, split, least, largest):
    gain = 1.0
    for axis_at, parts in split:
        heights = jax.random.uniform(jax.random.fold_in(jax.random.fold_in(stream_key, 6), axis_at), (parts,), jnp.float32, least / len(split), largest / len(split))
        gain = gain * jnp.repeat(jnp.exp(heights), dims[axis_at] // parts).reshape((-1,) + (1,) * (len(dims) - 1 - axis_at))
    return gain


def bell_draw(stream_key, shape, scale, reach, cuts=(), kind=jnp.bfloat16):
    level = steps_of(stream_key, shape, cuts, -0.22, 0.18) if cuts else 1.0
    drawn = jax.random.normal(stream_key, shape, jnp.float32) * scale * level
    return jnp.minimum(jnp.maximum(drawn, -reach), reach).astype(kind)


def setup_inputs(seed: int = 0) -> dict:
    streams_of = jax.random.split(jax.random.key(seed), 7)
    return {
        "velocity": bell_draw(streams_of[0], (3, NX, NY, CZ), 1.0, 6.0, ((1, 4), (2, 8)), jnp.float32),
        "modes": bell_draw(streams_of[1], (MODES, ROWS), 1.0, 6.0, ((1, 32),), jnp.float32),
        "mode_weights": jnp.clip(jnp.exp(jax.random.uniform(streams_of[2], (MODES,), jnp.float32, math.log(1.0), math.log(10.0))), 1.0, 10.0),
        "history": bell_draw(streams_of[3], (SNAPS - 1, ROWS), 1.0, 6.0, ((1, 32),), jnp.float32),
        "slab_ids": touch_ends(jax.random.randint(streams_of[4], (SLAB,), 0, CX * CY * CZ), jax.random.fold_in(streams_of[4], 1), 0, (CX * CY * CZ) - 1).astype(jnp.int32),
        "snap_steps": jax.random.permutation(streams_of[5], SNAPS).astype(jnp.int32),
    }


time_step = 0.1
viscosity = 0.5

def advance(padded):
    center = padded[:, 1:-1, 1:-1, :]
    x_plus = padded[:, 2:, 1:-1, :]
    x_minus = padded[:, :-2, 1:-1, :]
    y_plus = padded[:, 1:-1, 2:, :]
    y_minus = padded[:, 1:-1, :-2, :]
    z_plus = jnp.roll(center, -1, axis=3)
    z_minus = jnp.roll(center, 1, axis=3)
    laplace = x_plus + x_minus + y_plus + y_minus + z_plus + z_minus - 6.0 * center
    carried = center[0:1] * (0.5 * (x_plus - x_minus)) + center[1:2] * (0.5 * (y_plus - y_minus)) + center[2:3] * (0.5 * (z_plus - z_minus))
    return center + time_step * (viscosity * laplace - carried)

def reference(velocity, modes, mode_weights, history, slab_ids, snap_steps):
    field = velocity
    for step in range(2):
        padded = jnp.pad(field, ((0, 0), (1, 1), (1, 1), (0, 0)), mode='wrap')
        field = advance(padded)
    blocks = field.reshape(3, N_GRP, CX, N_TILE, CY, CZ).transpose(3, 1, 0, 2, 4, 5)
    blocks = blocks.reshape(DEVICES, 3, CX * CY * CZ)
    ids = slab_ids.reshape(DEVICES, 1, SLAB_DEV).astype(jnp.int32)
    ids = jnp.broadcast_to(ids, (DEVICES, 3, SLAB_DEV))
    sample = jnp.take_along_axis(blocks, ids, axis=2).reshape(1, ROWS)
    stacked = jnp.concatenate([history, sample], axis=0)
    snapshots = jnp.take(stacked, snap_steps.astype(jnp.int32), axis=0)
    combined = jnp.concatenate([mode_weights[:, None] * modes, snapshots], axis=0)
    gram = jnp.dot(combined, combined.T, precision=lax.Precision.HIGHEST)
    lower = jnp.linalg.cholesky(gram)
    root = jnp.sqrt(jnp.float32(ROWS))
    basis = lax.linalg.triangular_solve(lower, combined, left_side=True, lower=True) * root
    factor = lower.T / root
    return (field, basis, factor)
```

```python
import functools
import math

import jax
import jax.numpy as jnp
from jax import lax
from jax.experimental import pallas as pl
from jax.experimental.pallas import tpu as pltpu
from jax.sharding import PartitionSpec as P

time_step = 0.1
viscosity = 0.5
HIGHEST = lax.Precision.HIGHEST
LANES = 128
GROUP = 16


def in_hbm(array):
    return pltpu.with_memory_space_constraint(array, pltpu.HBM)


def in_vmem(array):
    return pltpu.with_memory_space_constraint(array, pltpu.VMEM)


def dot(a, b, ca=1, cb=0):
    return lax.dot_general(
        a, b, (((ca,), (cb,)), ((), ())), precision=HIGHEST, preferred_element_type=jnp.float32
    )


def faces_kernel(velocity_ref, xlow_ref, xhigh_ref, ylow_ref, yhigh_ref, low, high, sems):
    nx, ny = velocity_ref.shape[1:3]
    copies = [
        pltpu.make_async_copy(velocity_ref.at[:, 0:2], xlow_ref, sems.at[0]),
        pltpu.make_async_copy(velocity_ref.at[:, nx - 2 : nx], xhigh_ref, sems.at[1]),
        pltpu.make_async_copy(velocity_ref.at[:, :, 0:8, :], low, sems.at[2]),
        pltpu.make_async_copy(velocity_ref.at[:, :, ny - 8 : ny, :], high, sems.at[3]),
    ]
    for copy in copies:
        copy.start()
    copies[2].wait()
    ylow_ref[...] = low[:, :, 0:2, :]
    copies[3].wait()
    yhigh_ref[...] = high[:, :, 6:8, :]
    copies[0].wait()
    copies[1].wait()


def faces(velocity):
    comps, nx, ny, nz = velocity.shape
    hbm = pl.BlockSpec(memory_space=pl.ANY)
    vmem = pl.BlockSpec(memory_space=pltpu.VMEM)
    across_x = pltpu.VMEM((comps, 2, ny, nz), jnp.float32)
    across_y = pltpu.VMEM((comps, nx, 2, nz), jnp.float32)
    return pl.pallas_call(
        faces_kernel,
        in_specs=[hbm],
        out_specs=[vmem, vmem, vmem, vmem],
        out_shape=[across_x, across_x, across_y, across_y],
        scratch_shapes=[
            pltpu.VMEM((comps, nx, 8, nz), jnp.float32),
            pltpu.VMEM((comps, nx, 8, nz), jnp.float32),
            pltpu.SemaphoreType.DMA((4,)),
        ],
        compiler_params=pltpu.CompilerParams(vmem_limit_bytes=16 * 2**20),
        name="faces",
    )(in_hbm(velocity))


def corners_kernel(ylo_ref, yhi_ref, gram_ref, low_ref, high_ref):
    nx = ylo_ref.shape[1]
    for c in range(ylo_ref.shape[0]):
        low_ref[c, 0:1, :] = ylo_ref[c, 0, 1:2, :]
        low_ref[c, 1:2, :] = yhi_ref[c, 0, 0:1, :]
        high_ref[c, 0:1, :] = ylo_ref[c, nx - 1, 1:2, :]
        high_ref[c, 1:2, :] = yhi_ref[c, nx - 1, 0:1, :]


def corners(ylo, yhi, gram):
    comps, _, _, nz = ylo.shape
    vmem = pl.BlockSpec(memory_space=pltpu.VMEM)
    return pl.pallas_call(
        corners_kernel,
        in_specs=[vmem, vmem, pl.BlockSpec(memory_space=pl.ANY)],
        out_specs=[vmem, vmem],
        out_shape=[pltpu.VMEM((comps, 2, nz), jnp.float32)] * 2,
        compiler_params=pltpu.CompilerParams(vmem_limit_bytes=4 * 2**20),
        name="corners",
    )(in_vmem(ylo), in_vmem(yhi), in_vmem(gram))


def gram_kernel(steps_ref, w_ref, modes_ref, history_ref, gram_ref, snaps_ref):
    k = modes_ref.shape[0]
    count = snaps_ref.shape[0]
    last = count - 1
    for j in range(count):
        step = steps_ref[j]
        source = jnp.minimum(step, last - 1)
        row = history_ref[pl.ds(source, 1), :]
        snaps_ref[j : j + 1, :] = jnp.where(step == last, 0.0, row)
    modes = modes_ref[...]
    snaps = snaps_ref[...]
    wide = jnp.broadcast_to(w_ref[...], (k, k))
    tall = jnp.transpose(wide)
    gram_ref[0:k, 0:k] = dot(modes, modes, 1, 1) * wide * tall
    gram_ref[0:k, k:] = dot(modes, snaps, 1, 1) * tall[:, 0:count]
    gram_ref[k:, 0:k] = jnp.zeros((count, k), jnp.float32)
    gram_ref[k:, k:] = dot(snaps, snaps, 1, 1)


def early_gram(steps, weights, modes, history):
    k, width = modes.shape
    count = steps.shape[0]
    total = k + count
    return pl.pallas_call(
        gram_kernel,
        in_specs=[pl.BlockSpec(memory_space=pltpu.SMEM)] + [pl.BlockSpec(memory_space=pltpu.VMEM)] * 3,
        out_specs=[pl.BlockSpec(memory_space=pltpu.VMEM)] * 2,
        out_shape=[
            pltpu.VMEM((total, total), jnp.float32),
            pltpu.VMEM((count, width), jnp.float32),
        ],
        compiler_params=pltpu.CompilerParams(vmem_limit_bytes=24 * 2**20),
        cost_estimate=pl.CostEstimate(
            flops=12 * total * total * width, bytes_accessed=12 * total * width, transcendentals=0
        ),
        name="early_gram",
    )(in_vmem(steps), in_vmem(weights), in_vmem(modes), in_vmem(history))


def substep(src, dst, rows, src_x, dst_x, tiles, store):
    diff = time_step * viscosity
    adv = 0.5 * time_step
    for t in range(tiles):
        lo, hi = 8 * t, 8 * t + 8
        mid = [src[c, src_x, lo:hi, :] for c in range(3)]
        ax = [diff - adv * v for v in mid]
        bx = [diff + adv * v for v in mid]
        for c in range(3):
            v = mid[c]
            if lo == 0:
                y_minus = jnp.concatenate([src[c, src_x, rows - 1 : rows, :], src[c, src_x, 0:7, :]], axis=0)
            else:
                y_minus = src[c, src_x, lo - 1 : hi - 1, :]
            if hi == rows:
                y_plus = jnp.concatenate([src[c, src_x, lo + 1 : hi, :], src[c, src_x, 0:1, :]], axis=0)
            else:
                y_plus = src[c, src_x, lo + 1 : hi + 1, :]
            x_plus = src[c, src_x + 1, lo:hi, :]
            x_minus = src[c, src_x - 1, lo:hi, :]
            z_plus = pltpu.roll(v, v.shape[1] - 1, 1)
            z_minus = pltpu.roll(v, 1, 1)
            out = (1.0 - 6.0 * diff) * v
            out = out + ax[0] * x_plus + bx[0] * x_minus
            out = out + ax[1] * y_plus + bx[1] * y_minus
            out = out + ax[2] * z_plus + bx[2] * z_minus
            store(c, dst_x, lo, hi, out)


def field_kernel(
    ids_ref, steps_ref, core_ref, w_ref, velocity_ref, xlo_ref, xhi_ref, ylo_ref, yhi_ref, clo_ref, chi_ref,
    modes_ref, snaps_ref, gram_ref,
    advanced_ref, snaps_out_ref, mine_ref, other_ref,
    p0, p1, u2, flat, picked, packed, sem, out_sems,
):
    comps, nx, ny, nz = u2.shape
    rows = ny + 8
    inner = pltpu.make_async_copy(velocity_ref, p0.at[:, 2 : nx + 2, 0:ny, :], sem)
    inner.start()
    p0[:, 0:2, 0:ny, :] = xlo_ref[...]
    p0[:, nx + 2 : nx + 4, 0:ny, :] = xhi_ref[...]
    for c in range(comps):
        for x in range(nx):
            p0[c, x + 2, ny : ny + 2, :] = yhi_ref[c, x]
            p0[c, x + 2, rows - 2 : rows, :] = ylo_ref[c, x]
        p0[c, 1, rows - 1 : rows, :] = clo_ref[c, 0:1, :]
        p0[c, 1, ny : ny + 1, :] = clo_ref[c, 1:2, :]
        p0[c, nx + 2, rows - 1 : rows, :] = chi_ref[c, 0:1, :]
        p0[c, nx + 2, ny : ny + 1, :] = chi_ref[c, 1:2, :]
    inner.wait()

    def keep1(c, x, lo, hi, out):
        p1[c, x, lo:hi, :] = out

    tiles = nz // LANES

    def keep2(c, x, lo, hi, out):
        u2[c, x, lo:hi, :] = out
        for k in range(tiles):
            at = pl.multiple_of((k * nx + x) * ny + lo, 8)
            flat[c, pl.ds(at, 8), :] = out[:, k * LANES : (k + 1) * LANES]

    @pl.loop(0, nx + 2)
    def _(x):
        substep(p0, p1, rows, x + 1, x, rows // 8, keep1)

    def out_copy(x):
        return pltpu.make_async_copy(u2.at[:, x], advanced_ref.at[:, x], out_sems.at[x])

    @pl.loop(0, nx)
    def _(x):
        substep(p1, u2, rows, x + 1, x, ny // 8, keep2)
        out_copy(x).start()

    count = ids_ref.shape[0]
    lane = lax.broadcasted_iota(jnp.int32, (1, LANES), 1)

    @pl.loop(0, count // 8)
    def _(i):
        for k in range(8):
            cell = ids_ref[i * 8 + k]
            line = lax.shift_right_logical(cell, int(math.log2(LANES)))
            at = (line & (tiles - 1)) * (nx * ny) + lax.shift_right_logical(line, int(math.log2(tiles)))
            hit = lane == (cell & (LANES - 1))
            for c in range(comps):
                row = flat[c, pl.ds(at, 1), :]
                picked[c, pl.ds(i * 8 + k, 1), :] = jnp.where(hit, row, 0.0)

    ones = jnp.ones((8, LANES), jnp.float32)
    parts = [dot(ones, picked[c], 1, 1)[0:1] for c in range(comps)]
    sample = jnp.concatenate(parts, axis=1)

    snaps_count = steps_ref.shape[0]
    place = jnp.int32(0)
    for j in range(snaps_count):
        place = jnp.where(steps_ref[j] == snaps_count - 1, j, place)
    snaps_out_ref[...] = snaps_ref[...]
    snaps_out_ref[pl.ds(place, 1), :] = sample

    k = modes_ref.shape[0]
    half = snaps_count
    tall = jnp.transpose(jnp.broadcast_to(w_ref[...], (k, k)))
    with_modes = jnp.sum(modes_ref[...] * sample, axis=1, keepdims=True) * tall
    with_snaps = jnp.sum(snaps_out_ref[...] * sample, axis=1, keepdims=True)
    col = lax.broadcasted_iota(jnp.int32, (half, half), 1)
    row = lax.broadcasted_iota(jnp.int32, (half, half), 0)
    col_k = lax.broadcasted_iota(jnp.int32, (k, half), 1)
    cross = jnp.where(col_k == place, with_modes[:, 0:half], gram_ref[0:k, k:])
    splat = jnp.broadcast_to(with_snaps, (half, LANES))[:, 0:half]
    low = jnp.where(col == place, splat, gram_ref[k:, k:])
    low = jnp.where(row == place, jnp.transpose(splat), low)
    packed[0:half, 0:half] = gram_ref[0:half, half:k]
    packed[0:half, half:k] = cross[0:half]
    packed[half:k, 0:half] = gram_ref[half:k, half:k]
    packed[half:k, half:k] = cross[half:k]
    packed[k:, 0:half] = gram_ref[0:half, 0:half]
    packed[k:, half:k] = low
    part = mine_ref.shape[0]
    core = core_ref[0]
    mine_ref[...] = packed[pl.ds(pl.multiple_of(core * part, 8), part), :]
    other_ref[...] = packed[pl.ds(pl.multiple_of((1 - core) * part, 8), part), :]

    @pl.loop(0, nx)
    def _(x):
        out_copy(x).wait()


def field_call(ids, steps, core, weights, velocity, xlo, xhi, ylo, yhi, clo, chi, modes, snaps, gram):
    comps, nx, ny, nz = velocity.shape
    total = gram.shape[0]
    part = total // 2
    smem = pl.BlockSpec(memory_space=pltpu.SMEM)
    vmem = pl.BlockSpec(memory_space=pltpu.VMEM)
    hbm = pl.BlockSpec(memory_space=pl.ANY)
    return pl.pallas_call(
        field_kernel,
        in_specs=[smem, smem, smem, vmem, hbm] + [vmem] * 9,
        out_specs=[hbm, vmem, vmem, vmem],
        out_shape=[
            pltpu.HBM(velocity.shape, jnp.float32),
            pltpu.VMEM(snaps.shape, jnp.float32),
            pltpu.VMEM((part, LANES), jnp.float32),
            pltpu.VMEM((part, LANES), jnp.float32),
        ],
        scratch_shapes=[
            pltpu.VMEM((comps, nx + 4, ny + 8, nz), jnp.float32),
            pltpu.VMEM((comps, nx + 2, ny + 8, nz), jnp.float32),
            pltpu.VMEM((comps, nx, ny, nz), jnp.float32),
            pltpu.VMEM((comps, nx * ny * nz // LANES, LANES), jnp.float32),
            pltpu.VMEM((comps, ids.shape[0], LANES), jnp.float32),
            pltpu.VMEM((total, LANES), jnp.float32),
            pltpu.SemaphoreType.DMA,
            pltpu.SemaphoreType.DMA((nx,)),
        ],
        compiler_params=pltpu.CompilerParams(vmem_limit_bytes=26 * 2**20),
        cost_estimate=pl.CostEstimate(
            flops=60 * velocity.size, bytes_accessed=8 * velocity.size, transcendentals=0
        ),
        name="substeps_and_sample",
    )(
        in_vmem(ids), in_vmem(steps), core, in_vmem(weights), in_hbm(velocity), in_vmem(xlo), in_vmem(xhi),
        in_vmem(ylo), in_vmem(yhi), in_vmem(clo), in_vmem(chi), in_vmem(modes), in_vmem(snaps), in_vmem(gram),
    )


def eliminate(block):
    n = block.shape[0]
    eye = (
        lax.broadcasted_iota(jnp.int32, (n, n), 0) == lax.broadcasted_iota(jnp.int32, (n, n), 1)
    ).astype(jnp.float32)
    table = jnp.concatenate([block, eye], axis=1)
    width = table.shape[1]
    done = []
    base = 0
    for j in range(0, n, GROUP):
        first = (j // 8) * 8
        if first > base:
            done.append(table[: first - base])
            table = table[first - base :]
            base = first
        h = n - base
        rows = lax.broadcasted_iota(jnp.int32, (h, width), 0) + base
        spread = [jnp.broadcast_to(table[:, j + k : j + k + 1], (h, width)) for k in range(GROUP)]
        for k in range(GROUP):
            i = j + k - base
            ratio = jnp.where(rows > j + k, spread[k] * (1.0 / spread[k][i : i + 1, :]), 0.0)
            for l in range(k + 1, GROUP):
                spread[l] = spread[l] - ratio * spread[l][i : i + 1, :]
            table = table - ratio * table[i : i + 1, :]
    done.append(table)
    table = jnp.concatenate(done, axis=0)
    pivots = jnp.sum(table[:, :n] * eye, axis=1, keepdims=True)
    table = table * lax.rsqrt(pivots)
    upper = lax.broadcasted_iota(jnp.int32, (n, n), 1) >= lax.broadcasted_iota(jnp.int32, (n, n), 0)
    return jnp.where(upper, table[:, :n], 0.0), table[:, n:]


def basis_kernel(root, core_ref, w_ref, mine_ref, other_ref, modes_ref, snaps_ref, factor_ref, basis_ref, packed, inverse):
    total = factor_ref.shape[0]
    half = total // 3
    two = 2 * half

    @pl.when(pl.program_id(0) == 0)
    def _():
        part = mine_ref.shape[0]
        core = core_ref[0]
        packed[pl.ds(pl.multiple_of(core * part, 8), part), :] = mine_ref[...]
        packed[pl.ds(pl.multiple_of((1 - core) * part, 8), part), :] = other_ref[...]
        a00 = packed[two:, 0:half]
        a22 = packed[two:, half:two]
        u00, m00 = eliminate(a00)
        w0 = dot(m00, packed[0:half, :])
        w01, w02 = w0[:, 0:half], w0[:, half:two]
        a1 = packed[half:two, :] - dot(w01, w0, 0, 0)
        u11, m11 = eliminate(a1[:, 0:half])
        w12 = dot(m11, a1[:, half:two])
        a22 = a22 - dot(w02, w02, 0, 0) - dot(w12, w12, 0, 0)
        m10 = -dot(m11, dot(w01, m00, 0, 0))
        u22, m22 = eliminate(a22)
        m20 = -dot(m22, dot(w02, m00, 0, 0) + dot(w12, m10, 0, 0))
        m21 = -dot(m22, dot(w12, m11, 0, 0))
        zero = jnp.zeros((half, half), jnp.float32)
        scale = 1.0 / root
        factor_ref[0:half, 0:half] = u00 * scale
        factor_ref[0:half, half:two] = w01 * scale
        factor_ref[0:half, two:] = w02 * scale
        factor_ref[half:two, 0:half] = zero
        factor_ref[half:two, half:two] = u11 * scale
        factor_ref[half:two, two:] = w12 * scale
        factor_ref[two:, 0:half] = zero
        factor_ref[two:, half:two] = zero
        factor_ref[two:, two:] = u22 * scale
        wide = w_ref[...] * root
        inverse[0:half, 0:two] = jnp.concatenate([m00, zero], axis=1) * wide
        inverse[half:two, 0:two] = jnp.concatenate([m10, m11], axis=1) * wide
        inverse[two:, 0:two] = jnp.concatenate([m20, m21], axis=1) * wide
        inverse[0:half, two:total] = zero
        inverse[half:two, two:total] = zero
        inverse[two:, two:total] = m22 * root

    rows = jnp.concatenate([modes_ref[...], snaps_ref[...]], axis=0)
    basis_ref[...] = dot(inverse[:, 0:total], rows)


def basis_call(root, core, weights, mine, other, modes, snaps):
    k, width = modes.shape
    count = snaps.shape[0]
    total = k + count
    chunk = 512
    smem = pl.BlockSpec(memory_space=pltpu.SMEM)
    whole = lambda shape: pl.BlockSpec(shape, lambda i: (0, 0))
    return pl.pallas_call(
        functools.partial(basis_kernel, root),
        grid=(width // chunk,),
        in_specs=[
            smem,
            whole(weights.shape),
            whole(mine.shape),
            whole(other.shape),
            pl.BlockSpec((k, chunk), lambda i: (0, i)),
            pl.BlockSpec((count, chunk), lambda i: (0, i)),
        ],
        out_specs=[whole((total, total)), pl.BlockSpec((total, chunk), lambda i: (0, i))],
        out_shape=[
            jax.ShapeDtypeStruct((total, total), jnp.float32),
            jax.ShapeDtypeStruct((total, width), jnp.float32),
        ],
        scratch_shapes=[
            pltpu.VMEM((total, LANES), jnp.float32),
            pltpu.VMEM((total, 2 * LANES), jnp.float32),
        ],
        compiler_params=pltpu.CompilerParams(vmem_limit_bytes=24 * 2**20),
        cost_estimate=pl.CostEstimate(
            flops=12 * total * total * width, bytes_accessed=8 * total * width, transcendentals=0
        ),
        name="factor_and_basis",
    )(core, in_vmem(weights), in_vmem(mine), in_vmem(other), in_vmem(modes), in_vmem(snaps))


def ring(axis):
    count = lax.axis_size(axis)
    forward = [(i, (i + 1) % count) for i in range(count)]
    backward = [(i, (i - 1) % count) for i in range(count)]
    return forward, backward


def swap(axis, bit):
    return [(i, i ^ bit) for i in range(lax.axis_size(axis))]


def per_device(velocity, modes, mode_weights, history, slab_ids, snap_steps):
    xlow, xhigh, ylow, yhigh = faces(velocity)
    up, down = ring("grp")
    xlo = lax.ppermute(xhigh, "grp", up)
    xhi = lax.ppermute(xlow, "grp", down)
    up_y, down_y = ring("tile")
    ylo = lax.ppermute(yhigh, "tile", up_y)
    yhi = lax.ppermute(ylow, "tile", down_y)

    weights = mode_weights.reshape(1, -1)
    gram, snaps = early_gram(snap_steps, weights, modes, history)

    clow, chigh = corners(ylo, yhi, gram)
    clo = lax.ppermute(chigh, "grp", up)
    chi = lax.ppermute(clow, "grp", down)

    core = (lax.axis_index("grp") & 1).astype(jnp.int32).reshape(1)
    advanced, snaps, mine, other = field_call(
        slab_ids, snap_steps, core, weights, velocity, xlo, xhi, ylo, yhi, clo, chi, modes, snaps, gram
    )

    mine = mine + lax.ppermute(other, "grp", swap("grp", 1))
    for axis, first in (("grp", 2), ("tile", 1)):
        bit = first
        while bit < lax.axis_size(axis):
            mine = mine + lax.ppermute(mine, axis, swap(axis, bit))
            bit *= 2
    other = lax.ppermute(mine, "grp", swap("grp", 1))

    total_rows = modes.shape[1] * lax.axis_size("tile") * lax.axis_size("grp")
    root = math.sqrt(total_rows)
    factor, basis = basis_call(root, core, weights, mine, other, modes, snaps)
    return (advanced, basis, factor)


def solution(mesh):
    return jax.shard_map(
        per_device,
        mesh=mesh,
        in_specs=(
            P(None, "grp", "tile", None),
            P(None, ("tile", "grp")),
            P(),
            P(None, ("tile", "grp")),
            P(("tile", "grp")),
            P(),
        ),
        out_specs=(P(None, "grp", "tile", None), P(None, ("tile", "grp")), P()),
        check_vma=False,
    )
```

```python
import functools
import math

import jax
import jax.numpy as jnp
from jax import lax
from jax.experimental import pallas as pl
from jax.experimental.pallas import tpu as pltpu
from jax.sharding import PartitionSpec as P

time_step = 0.1
viscosity = 0.5
HIGHEST = lax.Precision.HIGHEST
LANES = 128
GROUP = 16


def in_hbm(array):
    return pltpu.with_memory_space_constraint(array, pltpu.HBM)


def in_vmem(array):
    return pltpu.with_memory_space_constraint(array, pltpu.VMEM)


def dot(a, b, ca=1, cb=0):
    return lax.dot_general(
        a, b, (((ca,), (cb,)), ((), ())), precision=HIGHEST, preferred_element_type=jnp.float32
    )


def faces_kernel(velocity_ref, ylow_ref, yhigh_ref, xlow_ref, xhigh_ref, sems):
    nx, ny = velocity_ref.shape[1:3]
    copies = [
        pltpu.make_async_copy(velocity_ref.at[:, :, 0:2, :], ylow_ref, sems.at[0]),
        pltpu.make_async_copy(velocity_ref.at[:, :, ny - 2 : ny, :], yhigh_ref, sems.at[1]),
        pltpu.make_async_copy(velocity_ref.at[:, 0:2], xlow_ref, sems.at[2]),
        pltpu.make_async_copy(velocity_ref.at[:, nx - 2 : nx], xhigh_ref, sems.at[3]),
    ]
    for copy in copies:
        copy.start()
    for copy in copies:
        copy.wait()


def faces(velocity):
    comps, nx, ny, nz = velocity.shape
    vmem = pl.BlockSpec(memory_space=pltpu.VMEM)
    across_x = pltpu.VMEM((comps, 2, ny, nz), jnp.float32)
    across_y = pltpu.VMEM((comps, nx, 2, nz), jnp.float32)
    return pl.pallas_call(
        faces_kernel,
        in_specs=[pl.BlockSpec(memory_space=pl.ANY)],
        out_specs=[vmem] * 4,
        out_shape=[across_y, across_y, across_x, across_x],
        scratch_shapes=[pltpu.SemaphoreType.DMA((4,))],
        compiler_params=pltpu.CompilerParams(vmem_limit_bytes=2 * 2**20),
        name="faces",
    )(in_hbm(velocity))


def corners_kernel(ylo_ref, yhi_ref, gram_ref, low_ref, high_ref):
    nx = ylo_ref.shape[1]
    for c in range(ylo_ref.shape[0]):
        low_ref[c, 0:1, :] = ylo_ref[c, 0, 1:2, :]
        low_ref[c, 1:2, :] = yhi_ref[c, 0, 0:1, :]
        high_ref[c, 0:1, :] = ylo_ref[c, nx - 1, 1:2, :]
        high_ref[c, 1:2, :] = yhi_ref[c, nx - 1, 0:1, :]


def corners(ylo, yhi, gram):
    comps, _, _, nz = ylo.shape
    vmem = pl.BlockSpec(memory_space=pltpu.VMEM)
    return pl.pallas_call(
        corners_kernel,
        in_specs=[vmem, vmem, pl.BlockSpec(memory_space=pl.ANY)],
        out_specs=[vmem, vmem],
        out_shape=[pltpu.VMEM((comps, 2, nz), jnp.float32)] * 2,
        compiler_params=pltpu.CompilerParams(vmem_limit_bytes=4 * 2**20),
        name="corners",
    )(in_vmem(ylo), in_vmem(yhi), in_vmem(gram))


def gram_kernel(steps_ref, w_ref, modes_ref, history_ref, gram_ref, snaps_ref):
    k = modes_ref.shape[0]
    count = snaps_ref.shape[0]
    last = count - 1
    for j in range(count):
        step = steps_ref[j]
        source = jnp.minimum(step, last - 1)
        row = history_ref[pl.ds(source, 1), :]
        snaps_ref[j : j + 1, :] = jnp.where(step == last, 0.0, row)
    modes = modes_ref[...]
    snaps = snaps_ref[...]
    wide = jnp.broadcast_to(w_ref[...], (k, k))
    tall = jnp.transpose(wide)
    gram_ref[0:k, 0:k] = dot(modes, modes, 1, 1) * wide * tall
    gram_ref[0:k, k:] = dot(modes, snaps, 1, 1) * tall[:, 0:count]
    gram_ref[k:, 0:k] = jnp.zeros((count, k), jnp.float32)
    gram_ref[k:, k:] = dot(snaps, snaps, 1, 1)


def early_gram(steps, weights, modes, history):
    k, width = modes.shape
    count = steps.shape[0]
    total = k + count
    return pl.pallas_call(
        gram_kernel,
        in_specs=[pl.BlockSpec(memory_space=pltpu.SMEM)] + [pl.BlockSpec(memory_space=pltpu.VMEM)] * 3,
        out_specs=[pl.BlockSpec(memory_space=pltpu.VMEM)] * 2,
        out_shape=[
            pltpu.VMEM((total, total), jnp.float32),
            pltpu.VMEM((count, width), jnp.float32),
        ],
        compiler_params=pltpu.CompilerParams(vmem_limit_bytes=10 * 2**20),
        cost_estimate=pl.CostEstimate(
            flops=12 * total * total * width, bytes_accessed=12 * total * width, transcendentals=0
        ),
        name="early_gram",
    )(in_vmem(steps), in_vmem(weights), in_vmem(modes), in_vmem(history))


def stencil(tile, which, inner, store):
    adv = 0.5 * time_step
    diff = time_step * viscosity
    sub = lax.broadcasted_iota(jnp.int32, tile(0, 0, 0).shape, 0)
    first, last = sub == 0, sub == 7
    for t in which:
        before, after = (t - 1) % (inner + 1), (t + 1) % (inner + 1)
        mid = [tile(0, c, t) for c in range(3)]
        scaled = [adv * v for v in mid]
        plus = [diff - v for v in scaled]
        minus = [diff + v for v in scaled]
        for c in range(3):
            v = mid[c]
            y_plus = jnp.where(last, pltpu.roll(tile(0, c, after), 7, 0), pltpu.roll(v, 7, 0))
            y_minus = jnp.where(first, pltpu.roll(tile(0, c, before), 1, 0), pltpu.roll(v, 1, 0))
            out = (1.0 - 6.0 * diff) * v
            out = out + plus[0] * tile(1, c, t) + minus[0] * tile(-1, c, t)
            out = out + plus[1] * y_plus + minus[1] * y_minus
            out = out + plus[2] * pltpu.roll(v, v.shape[1] - 1, 1) + minus[2] * pltpu.roll(v, 1, 1)
            store(c, t, out)


def field_kernel(
    velocity_ref, xlo_ref, xhi_ref, ylo_ref, yhi_ref,
    advanced_ref, p1, ends_ref, flat, ring_tile, u2, out_sems,
):
    comps, nx, ny, nz = velocity_ref.shape
    inner = ny // 8
    tiles = nz // LANES
    for c in range(comps):
        for x in range(nx):
            ring_tile[c, x, 0:2, :] = yhi_ref[c, x]
            ring_tile[c, x, 6:8, :] = ylo_ref[c, x]

    def first_layer(x, refs, layers, count):
        def tile(k, c, t):
            if t == inner:
                if isinstance(x, int) and not 0 <= x + k < nx:
                    return jnp.zeros((8, nz), jnp.float32)
                return ring_tile[c, x + k]
            return refs[k + 1][c, layers[k + 1], 8 * t : 8 * t + 8, :]

        def store(c, t, value):
            p1[c, x + 1, 8 * t : 8 * t + 8, :] = value

        stencil(tile, range(count), inner, store)

    vel = velocity_ref
    first_layer(-1, (xlo_ref, xlo_ref, vel), (0, 1, 0), inner)
    first_layer(0, (xlo_ref, vel, vel), (1, 0, 1), inner + 1)

    @pl.loop(1, nx - 1)
    def _(x):
        first_layer(x, (vel, vel, vel), (x - 1, x, x + 1), inner + 1)

    first_layer(nx - 1, (vel, vel, xhi_ref), (nx - 2, nx - 1, 0), inner + 1)
    first_layer(nx, (vel, xhi_ref, xhi_ref), (nx - 1, 0, 1), inner)

    def second_layer(x, out, layer):
        def tile(k, c, t):
            return p1[c, x + 1 + k, 8 * t : 8 * t + 8, :]

        def store(c, t, value):
            out[c, layer, 8 * t : 8 * t + 8, :] = value
            for k in range(tiles):
                at = pl.multiple_of((k * nx + x) * ny + 8 * t, 8)
                flat[c, pl.ds(at, 8), :] = value[:, k * LANES : (k + 1) * LANES]

        stencil(tile, range(inner), inner, store)

    def out_copy(x):
        return pltpu.make_async_copy(u2.at[:, x], advanced_ref.at[:, x], out_sems.at[x])

    @pl.loop(1, nx - 1)
    def _(x):
        second_layer(x, u2, x)
        out_copy(x).start()

    second_layer(0, ends_ref, 0)
    second_layer(nx - 1, ends_ref, 1)

    @pl.loop(1, nx - 1)
    def _(x):
        out_copy(x).wait()


def field_call(velocity, xlo, xhi, ylo, yhi):
    comps, nx, ny, nz = velocity.shape
    vmem = pl.BlockSpec(memory_space=pltpu.VMEM)
    return pl.pallas_call(
        field_kernel,
        in_specs=[vmem] * 5,
        out_specs=[pl.BlockSpec(memory_space=pl.ANY), vmem, vmem, vmem],
        out_shape=[
            pltpu.HBM(velocity.shape, jnp.float32),
            pltpu.VMEM((comps, nx + 2, ny + 8, nz), jnp.float32),
            pltpu.VMEM((comps, 2, ny, nz), jnp.float32),
            pltpu.VMEM((comps, nx * ny * nz // LANES, LANES), jnp.float32),
        ],
        scratch_shapes=[
            pltpu.VMEM((comps, nx, 8, nz), jnp.float32),
            pltpu.VMEM((comps, nx, ny, nz), jnp.float32),
            pltpu.SemaphoreType.DMA((nx,)),
        ],
        compiler_params=pltpu.CompilerParams(vmem_limit_bytes=8 * 2**20),
        cost_estimate=pl.CostEstimate(
            flops=60 * velocity.size, bytes_accessed=8 * velocity.size, transcendentals=0
        ),
        name="substeps",
    )(*(in_vmem(a) for a in (velocity, xlo, xhi, ylo, yhi)))


def sample_kernel(
    ids_ref, steps_ref, w_ref, xlo_ref, xhi_ref, clo_ref, chi_ref, own_lo_ref, own_hi_ref,
    p1, modes_ref, snaps_ref, gram_ref, advanced_in, ends_in, flat_in,
    advanced_ref, ends_ref, flat, snaps_out_ref, mine_ref, other_ref,
    fixed, picked, packed, sems,
):
    comps, _, ny, nz = xlo_ref.shape
    nx = flat.shape[1] * LANES // (ny * nz)
    inner = ny // 8
    tiles = nz // LANES
    sub = lax.broadcasted_iota(jnp.int32, (8, nz), 0)
    adv = 0.5 * time_step
    diff = time_step * viscosity

    def halo_tile(line, c):
        return jnp.where(sub == 0, line[c, 1:2, :], line[c, 0:1, :])

    for end, layer, mid, line, own in (
        (0, 0, xlo_ref.at[:, 1], clo_ref, own_lo_ref),
        (1, nx - 1, xhi_ref.at[:, 0], chi_ref, own_hi_ref),
    ):
        sign = 1.0 if end == 0 else -1.0
        outside = layer if end == 0 else layer + 2
        own_x = diff + sign * adv * halo_tile(own, 0)
        low_y = diff + adv * mid[1, 0:8, :]
        high_y = diff - adv * mid[1, ny - 8 : ny, :]
        for c in range(comps):
            corner = halo_tile(line, c)
            halo = p1[c, layer + 1, ny : ny + 8, :] + own_x * corner
            fixed[c, end, 2] = halo
            fixed[c, end, 0] = p1[c, outside, 0:8, :] + jnp.where(sub == 0, low_y * line[c, 0:1, :], 0.0)
            fixed[c, end, 1] = p1[c, outside, ny - 8 : ny, :] + jnp.where(sub == 7, high_y * line[c, 1:2, :], 0.0)

        def tile(k, c, t):
            if k == (-1 if end == 0 else 1):
                return fixed[c, end, 0 if t == 0 else 1]
            if t == inner:
                return fixed[c, end, 2]
            return p1[c, layer + 1 + k, 8 * t : 8 * t + 8, :]

        def store(c, t, value):
            ends_ref[c, end, 8 * t : 8 * t + 8, :] = value
            for k in range(tiles):
                at = (k * nx + layer) * ny + 8 * t
                flat[c, at : at + 8, :] = value[:, k * LANES : (k + 1) * LANES]

        stencil(tile, (0, inner - 1), inner, store)
    out_copies = [
        pltpu.make_async_copy(ends_ref.at[:, 0], advanced_ref.at[:, 0], sems.at[0]),
        pltpu.make_async_copy(ends_ref.at[:, 1], advanced_ref.at[:, nx - 1], sems.at[1]),
    ]
    for copy in out_copies:
        copy.start()

    count = ids_ref.shape[0]
    lane = lax.broadcasted_iota(jnp.int32, (1, LANES), 1)

    @pl.loop(0, count // 8)
    def _(i):
        for k in range(8):
            cell = ids_ref[i * 8 + k]
            line = lax.shift_right_logical(cell, int(math.log2(LANES)))
            at = (line & (tiles - 1)) * (nx * ny) + lax.shift_right_logical(line, int(math.log2(tiles)))
            hit = lane == (cell & (LANES - 1))
            for c in range(comps):
                row = flat[c, pl.ds(at, 1), :]
                picked[c, pl.ds(i * 8 + k, 1), :] = jnp.where(hit, row, 0.0)

    ones = jnp.ones((8, LANES), jnp.float32)
    parts = [dot(ones, picked[c], 1, 1)[0:1] for c in range(comps)]
    sample = jnp.concatenate(parts, axis=1)

    snaps_count = steps_ref.shape[0]
    place = jnp.int32(0)
    for j in range(snaps_count):
        place = jnp.where(steps_ref[j] == snaps_count - 1, j, place)
    snaps_out_ref[...] = snaps_ref[...]
    snaps_out_ref[pl.ds(place, 1), :] = sample

    k = modes_ref.shape[0]
    half = snaps_count
    tall = jnp.transpose(jnp.broadcast_to(w_ref[...], (k, k)))
    with_modes = jnp.sum(modes_ref[...] * sample, axis=1, keepdims=True) * tall
    with_snaps = jnp.sum(snaps_out_ref[...] * sample, axis=1, keepdims=True)
    col = lax.broadcasted_iota(jnp.int32, (half, half), 1)
    row = lax.broadcasted_iota(jnp.int32, (half, half), 0)
    col_k = lax.broadcasted_iota(jnp.int32, (k, half), 1)
    cross = jnp.where(col_k == place, with_modes[:, 0:half], gram_ref[0:k, k:])
    splat = jnp.broadcast_to(with_snaps, (half, LANES))[:, 0:half]
    low = jnp.where(col == place, splat, gram_ref[k:, k:])
    low = jnp.where(row == place, jnp.transpose(splat), low)
    packed[0:half, 0:half] = gram_ref[0:half, half:k]
    packed[0:half, half:k] = cross[0:half]
    packed[half:k, 0:half] = gram_ref[half:k, half:k]
    packed[half:k, half:k] = cross[half:k]
    packed[k:, 0:half] = gram_ref[0:half, 0:half]
    packed[k:, half:k] = low
    part = mine_ref.shape[0]
    core = lax.axis_index("grp") & 1
    mine_ref[...] = packed[pl.ds(pl.multiple_of(core * part, 8), part), :]
    other_ref[...] = packed[pl.ds(pl.multiple_of((1 - core) * part, 8), part), :]
    for copy in out_copies:
        copy.wait()


def sample_call(
    ids, steps, weights, xlo, xhi, clo, chi, own_lo, own_hi, p1, modes, snaps, gram, advanced, ends, flat
):
    comps, _, _, nz = xlo.shape
    total = gram.shape[0]
    part = total // 2
    smem = pl.BlockSpec(memory_space=pltpu.SMEM)
    vmem = pl.BlockSpec(memory_space=pltpu.VMEM)
    hbm = pl.BlockSpec(memory_space=pl.ANY)
    tail = (weights, xlo, xhi, clo, chi, own_lo, own_hi, p1, modes, snaps, gram)
    return pl.pallas_call(
        sample_kernel,
        in_specs=[smem] * 2 + [vmem] * 11 + [hbm, vmem, vmem],
        out_specs=[hbm, vmem, vmem, vmem, vmem, vmem],
        out_shape=[
            pltpu.HBM(advanced.shape, jnp.float32),
            pltpu.VMEM(ends.shape, jnp.float32),
            pltpu.VMEM(flat.shape, jnp.float32),
            pltpu.VMEM(snaps.shape, jnp.float32),
            pltpu.VMEM((part, LANES), jnp.float32),
            pltpu.VMEM((part, LANES), jnp.float32),
        ],
        input_output_aliases={13: 0, 14: 1, 15: 2},
        scratch_shapes=[
            pltpu.VMEM((comps, 2, 3, 8, nz), jnp.float32),
            pltpu.VMEM((comps, ids.shape[0], LANES), jnp.float32),
            pltpu.VMEM((total, LANES), jnp.float32),
            pltpu.SemaphoreType.DMA((2,)),
        ],
        compiler_params=pltpu.CompilerParams(vmem_limit_bytes=6 * 2**20),
        cost_estimate=pl.CostEstimate(
            flops=20 * flat.size, bytes_accessed=2 * flat.size, transcendentals=0
        ),
        name="sample_and_gram",
    )(
        in_vmem(ids), in_vmem(steps), *(in_vmem(a) for a in tail),
        in_hbm(advanced), in_vmem(ends), in_vmem(flat),
    )


def eliminate(block):
    n = block.shape[0]
    eye = (
        lax.broadcasted_iota(jnp.int32, (n, n), 0) == lax.broadcasted_iota(jnp.int32, (n, n), 1)
    ).astype(jnp.float32)
    table = jnp.concatenate([block, eye], axis=1)
    width = table.shape[1]
    done = []
    base = 0
    for j in range(0, n, GROUP):
        first = (j // 8) * 8
        if first > base:
            done.append(table[: first - base])
            table = table[first - base :]
            base = first
        h = n - base
        rows = lax.broadcasted_iota(jnp.int32, (h, width), 0) + base
        spread = [jnp.broadcast_to(table[:, j + k : j + k + 1], (h, width)) for k in range(GROUP)]
        for k in range(GROUP):
            i = j + k - base
            ratio = jnp.where(rows > j + k, spread[k] * (1.0 / spread[k][i : i + 1, :]), 0.0)
            for l in range(k + 1, GROUP):
                spread[l] = spread[l] - ratio * spread[l][i : i + 1, :]
            table = table - ratio * table[i : i + 1, :]
    done.append(table)
    table = jnp.concatenate(done, axis=0)
    pivots = jnp.sum(table[:, :n] * eye, axis=1, keepdims=True)
    table = table * lax.rsqrt(pivots)
    upper = lax.broadcasted_iota(jnp.int32, (n, n), 1) >= lax.broadcasted_iota(jnp.int32, (n, n), 0)
    return jnp.where(upper, table[:, :n], 0.0), table[:, n:]


def basis_kernel(root, w_ref, mine_ref, other_ref, modes_ref, snaps_ref, factor_ref, basis_ref, packed, inverse):
    total = factor_ref.shape[0]
    half = total // 3
    two = 2 * half

    @pl.when(pl.program_id(0) == 0)
    def _():
        part = mine_ref.shape[0]
        core = lax.axis_index("grp") & 1
        packed[pl.ds(pl.multiple_of(core * part, 8), part), :] = mine_ref[...]
        packed[pl.ds(pl.multiple_of((1 - core) * part, 8), part), :] = other_ref[...]
        a00 = packed[two:, 0:half]
        a22 = packed[two:, half:two]
        u00, m00 = eliminate(a00)
        w0 = dot(m00, packed[0:half, :])
        w01, w02 = w0[:, 0:half], w0[:, half:two]
        a1 = packed[half:two, :] - dot(w01, w0, 0, 0)
        u11, m11 = eliminate(a1[:, 0:half])
        w12 = dot(m11, a1[:, half:two])
        a22 = a22 - dot(w02, w02, 0, 0) - dot(w12, w12, 0, 0)
        m10 = -dot(m11, dot(w01, m00, 0, 0))
        u22, m22 = eliminate(a22)
        m20 = -dot(m22, dot(w02, m00, 0, 0) + dot(w12, m10, 0, 0))
        m21 = -dot(m22, dot(w12, m11, 0, 0))
        zero = jnp.zeros((half, half), jnp.float32)
        scale = 1.0 / root
        factor_ref[0:half, 0:half] = u00 * scale
        factor_ref[0:half, half:two] = w01 * scale
        factor_ref[0:half, two:] = w02 * scale
        factor_ref[half:two, 0:half] = zero
        factor_ref[half:two, half:two] = u11 * scale
        factor_ref[half:two, two:] = w12 * scale
        factor_ref[two:, 0:half] = zero
        factor_ref[two:, half:two] = zero
        factor_ref[two:, two:] = u22 * scale
        wide = w_ref[...] * root
        inverse[0:half, 0:two] = jnp.concatenate([m00, zero], axis=1) * wide
        inverse[half:two, 0:two] = jnp.concatenate([m10, m11], axis=1) * wide
        inverse[two:, 0:two] = jnp.concatenate([m20, m21], axis=1) * wide
        inverse[0:half, two:total] = zero
        inverse[half:two, two:total] = zero
        inverse[two:, two:total] = m22 * root

    rows = jnp.concatenate([modes_ref[...], snaps_ref[...]], axis=0)
    basis_ref[...] = dot(inverse[:, 0:total], rows)


def basis_call(root, weights, mine, other, modes, snaps):
    k, width = modes.shape
    count = snaps.shape[0]
    total = k + count
    chunk = 512
    whole = lambda shape: pl.BlockSpec(shape, lambda i: (0, 0))
    return pl.pallas_call(
        functools.partial(basis_kernel, root),
        grid=(width // chunk,),
        in_specs=[
            whole(weights.shape),
            whole(mine.shape),
            whole(other.shape),
            pl.BlockSpec((k, chunk), lambda i: (0, i)),
            pl.BlockSpec((count, chunk), lambda i: (0, i)),
        ],
        out_specs=[whole((total, total)), pl.BlockSpec((total, chunk), lambda i: (0, i))],
        out_shape=[
            jax.ShapeDtypeStruct((total, total), jnp.float32),
            jax.ShapeDtypeStruct((total, width), jnp.float32),
        ],
        scratch_shapes=[
            pltpu.VMEM((total, LANES), jnp.float32),
            pltpu.VMEM((total, 2 * LANES), jnp.float32),
        ],
        compiler_params=pltpu.CompilerParams(vmem_limit_bytes=10 * 2**20),
        cost_estimate=pl.CostEstimate(
            flops=12 * total * total * width, bytes_accessed=8 * total * width, transcendentals=0
        ),
        name="factor_and_basis",
    )(in_vmem(weights), in_vmem(mine), in_vmem(other), in_vmem(modes), in_vmem(snaps))


def ring(axis):
    count = lax.axis_size(axis)
    forward = [(i, (i + 1) % count) for i in range(count)]
    backward = [(i, (i - 1) % count) for i in range(count)]
    return forward, backward


def swap(axis, bit):
    return [(i, i ^ bit) for i in range(lax.axis_size(axis))]


def per_device(velocity, modes, mode_weights, history, slab_ids, snap_steps):
    ylow, yhigh, xlow, xhigh = faces(velocity)
    up_y, down_y = ring("tile")
    up, down = ring("grp")
    ylo = lax.ppermute(yhigh, "tile", up_y)
    yhi = lax.ppermute(ylow, "tile", down_y)
    xlo = lax.ppermute(xhigh, "grp", up)
    xhi = lax.ppermute(xlow, "grp", down)

    weights = mode_weights.reshape(1, -1)
    gram, snaps = early_gram(snap_steps, weights, modes, history)

    clow, chigh = corners(ylo, yhi, gram)
    clo = lax.ppermute(chigh, "grp", up)
    chi = lax.ppermute(clow, "grp", down)

    advanced, p1, ends, flat = field_call(velocity, xlo, xhi, ylo, yhi)
    advanced, _, _, snaps, mine, other = sample_call(
        slab_ids, snap_steps, weights, xlo, xhi, clo, chi, clow, chigh, p1, modes, snaps, gram, advanced, ends, flat
    )

    mine = mine + lax.ppermute(other, "grp", swap("grp", 1))
    for axis, first in (("grp", 2), ("tile", 1)):
        bit = first
        while bit < lax.axis_size(axis):
            mine = mine + lax.ppermute(mine, axis, swap(axis, bit))
            bit *= 2
    other = lax.ppermute(mine, "grp", swap("grp", 1))

    total_rows = modes.shape[1] * lax.axis_size("tile") * lax.axis_size("grp")
    root = math.sqrt(total_rows)
    factor, basis = basis_call(root, weights, mine, other, modes, snaps)
    return (advanced, basis, factor)


def solution(mesh):
    return jax.shard_map(
        per_device,
        mesh=mesh,
        in_specs=(
            P(None, "grp", "tile", None),
            P(None, ("tile", "grp")),
            P(),
            P(None, ("tile", "grp")),
            P(("tile", "grp")),
            P(),
        ),
        out_specs=(P(None, "grp", "tile", None), P(None, ("tile", "grp")), P()),
        check_vma=False,
    )
```

```python
import functools
import math

import jax
import jax.numpy as jnp
from jax import lax
from jax.experimental import pallas as pl
from jax.experimental.pallas import tpu as pltpu
from jax.sharding import PartitionSpec as P

time_step = 0.1
viscosity = 0.5
HIGHEST = lax.Precision.HIGHEST
LANES = 128
GROUP = 16
PARTS = 3


def in_hbm(array):
    return pltpu.with_memory_space_constraint(array, pltpu.HBM)


def in_vmem(array):
    return pltpu.with_memory_space_constraint(array, pltpu.VMEM)


def dot(a, b, ca=1, cb=0):
    return lax.dot_general(
        a, b, (((ca,), (cb,)), ((), ())), precision=HIGHEST, preferred_element_type=jnp.float32
    )


def faces_kernel(velocity_ref, ylow_ref, yhigh_ref, xlow_ref, xhigh_ref, sems):
    nx, ny = velocity_ref.shape[1:3]
    copies = [
        pltpu.make_async_copy(velocity_ref.at[:, :, 0:2, :], ylow_ref, sems.at[0]),
        pltpu.make_async_copy(velocity_ref.at[:, :, ny - 2 : ny, :], yhigh_ref, sems.at[1]),
        pltpu.make_async_copy(velocity_ref.at[:, 0:2], xlow_ref, sems.at[2]),
        pltpu.make_async_copy(velocity_ref.at[:, nx - 2 : nx], xhigh_ref, sems.at[3]),
    ]
    for copy in copies:
        copy.start()
    for copy in copies:
        copy.wait()


def faces(velocity):
    comps, nx, ny, nz = velocity.shape
    vmem = pl.BlockSpec(memory_space=pltpu.VMEM)
    across_x = pltpu.VMEM((comps, 2, ny, nz), jnp.float32)
    across_y = pltpu.VMEM((comps, nx, 2, nz), jnp.float32)
    return pl.pallas_call(
        faces_kernel,
        in_specs=[pl.BlockSpec(memory_space=pl.ANY)],
        out_specs=[vmem] * 4,
        out_shape=[across_y, across_y, across_x, across_x],
        scratch_shapes=[pltpu.SemaphoreType.DMA((4,))],
        compiler_params=pltpu.CompilerParams(vmem_limit_bytes=2 * 2**20),
        name="faces",
    )(in_hbm(velocity))


def corners_kernel(ylo_ref, yhi_ref, gram_ref, low_ref, high_ref):
    nx = ylo_ref.shape[1]
    for c in range(ylo_ref.shape[0]):
        low_ref[c, 0:1, :] = ylo_ref[c, 0, 1:2, :]
        low_ref[c, 1:2, :] = yhi_ref[c, 0, 0:1, :]
        high_ref[c, 0:1, :] = ylo_ref[c, nx - 1, 1:2, :]
        high_ref[c, 1:2, :] = yhi_ref[c, nx - 1, 0:1, :]


def corners(ylo, yhi, gram):
    comps, _, _, nz = ylo.shape
    vmem = pl.BlockSpec(memory_space=pltpu.VMEM)
    return pl.pallas_call(
        corners_kernel,
        in_specs=[vmem, vmem, pl.BlockSpec(memory_space=pl.ANY)],
        out_specs=[vmem, vmem],
        out_shape=[pltpu.VMEM((comps, 2, nz), jnp.float32)] * 2,
        compiler_params=pltpu.CompilerParams(vmem_limit_bytes=4 * 2**20),
        name="corners",
    )(in_vmem(ylo), in_vmem(yhi), in_vmem(gram))


def gram_kernel(steps_ref, w_ref, modes_ref, history_ref, gram_ref, snaps_ref):
    k = modes_ref.shape[0]
    count = snaps_ref.shape[0]
    last = count - 1
    for j in range(count):
        step = steps_ref[j]
        source = jnp.minimum(step, last - 1)
        row = history_ref[pl.ds(source, 1), :]
        snaps_ref[j : j + 1, :] = jnp.where(step == last, 0.0, row)
    modes = modes_ref[...]
    snaps = snaps_ref[...]
    wide = jnp.broadcast_to(w_ref[...], (k, k))
    tall = jnp.transpose(wide)
    gram_ref[0:k, 0:k] = dot(modes, modes, 1, 1) * wide * tall
    gram_ref[0:k, k:] = dot(modes, snaps, 1, 1) * tall[:, 0:count]
    gram_ref[k:, 0:k] = jnp.zeros((count, k), jnp.float32)
    gram_ref[k:, k:] = dot(snaps, snaps, 1, 1)


def early_gram(steps, weights, modes, history):
    k, width = modes.shape
    count = steps.shape[0]
    total = k + count
    return pl.pallas_call(
        gram_kernel,
        in_specs=[pl.BlockSpec(memory_space=pltpu.SMEM)] + [pl.BlockSpec(memory_space=pltpu.VMEM)] * 3,
        out_specs=[pl.BlockSpec(memory_space=pltpu.VMEM)] * 2,
        out_shape=[
            pltpu.VMEM((total, total), jnp.float32),
            pltpu.VMEM((count, width), jnp.float32),
        ],
        compiler_params=pltpu.CompilerParams(vmem_limit_bytes=10 * 2**20),
        cost_estimate=pl.CostEstimate(
            flops=12 * total * total * width, bytes_accessed=12 * total * width, transcendentals=0
        ),
        name="early_gram",
    )(in_vmem(steps), in_vmem(weights), in_vmem(modes), in_vmem(history))


def stencil(tile, which, inner, store):
    adv = 0.5 * time_step
    diff = time_step * viscosity
    sub = lax.broadcasted_iota(jnp.int32, tile(0, 0, 0).shape, 0)
    first, last = sub == 0, sub == 7
    for t in which:
        before, after = (t - 1) % (inner + 1), (t + 1) % (inner + 1)
        mid = [tile(0, c, t) for c in range(3)]
        scaled = [adv * v for v in mid]
        plus = [diff - v for v in scaled]
        minus = [diff + v for v in scaled]
        for c in range(3):
            v = mid[c]
            y_plus = jnp.where(last, pltpu.roll(tile(0, c, after), 7, 0), pltpu.roll(v, 7, 0))
            y_minus = jnp.where(first, pltpu.roll(tile(0, c, before), 1, 0), pltpu.roll(v, 1, 0))
            out = (1.0 - 6.0 * diff) * v
            out = out + plus[0] * tile(1, c, t) + minus[0] * tile(-1, c, t)
            out = out + plus[1] * y_plus + minus[1] * y_minus
            out = out + plus[2] * pltpu.roll(v, v.shape[1] - 1, 1) + minus[2] * pltpu.roll(v, 1, 1)
            store(c, t, out)


def field_kernel(
    velocity_ref, xlo_ref, xhi_ref, ylo_ref, yhi_ref,
    advanced_ref, p1, ends_ref, flat, ring_tile, u2, out_sems,
):
    comps, nx, ny, nz = velocity_ref.shape
    inner = ny // 8
    tiles = nz // LANES
    for c in range(comps):
        for x in range(nx):
            ring_tile[c, x, 0:2, :] = yhi_ref[c, x]
            ring_tile[c, x, 6:8, :] = ylo_ref[c, x]

    def first_layer(x, refs, layers, count):
        def tile(k, c, t):
            if t == inner:
                if isinstance(x, int) and not 0 <= x + k < nx:
                    return jnp.zeros((8, nz), jnp.float32)
                return ring_tile[c, x + k]
            return refs[k + 1][c, layers[k + 1], 8 * t : 8 * t + 8, :]

        def store(c, t, value):
            p1[c, x + 1, 8 * t : 8 * t + 8, :] = value

        stencil(tile, range(count), inner, store)

    vel = velocity_ref
    first_layer(-1, (xlo_ref, xlo_ref, vel), (0, 1, 0), inner)
    first_layer(0, (xlo_ref, vel, vel), (1, 0, 1), inner + 1)

    @pl.loop(1, nx - 1)
    def _(x):
        first_layer(x, (vel, vel, vel), (x - 1, x, x + 1), inner + 1)

    first_layer(nx - 1, (vel, vel, xhi_ref), (nx - 2, nx - 1, 0), inner + 1)
    first_layer(nx, (vel, xhi_ref, xhi_ref), (nx - 1, 0, 1), inner)

    def second_layer(x, out, layer):
        def tile(k, c, t):
            return p1[c, x + 1 + k, 8 * t : 8 * t + 8, :]

        def store(c, t, value):
            out[c, layer, 8 * t : 8 * t + 8, :] = value
            for k in range(tiles):
                at = pl.multiple_of((k * nx + x) * ny + 8 * t, 8)
                flat[c, pl.ds(at, 8), :] = value[:, k * LANES : (k + 1) * LANES]

        stencil(tile, range(inner), inner, store)

    def out_copy(x):
        return pltpu.make_async_copy(u2.at[:, x], advanced_ref.at[:, x], out_sems.at[x])

    @pl.loop(1, nx - 1)
    def _(x):
        second_layer(x, u2, x)
        out_copy(x).start()

    second_layer(0, ends_ref, 0)
    second_layer(nx - 1, ends_ref, 1)

    @pl.loop(1, nx - 1)
    def _(x):
        out_copy(x).wait()


def field_call(velocity, xlo, xhi, ylo, yhi):
    comps, nx, ny, nz = velocity.shape
    vmem = pl.BlockSpec(memory_space=pltpu.VMEM)
    return pl.pallas_call(
        field_kernel,
        in_specs=[vmem] * 5,
        out_specs=[pl.BlockSpec(memory_space=pl.ANY), vmem, vmem, vmem],
        out_shape=[
            pltpu.HBM(velocity.shape, jnp.float32),
            pltpu.VMEM((comps, nx + 2, ny + 8, nz), jnp.float32),
            pltpu.VMEM((comps, 2, ny, nz), jnp.float32),
            pltpu.VMEM((comps, nx * ny * nz // LANES, LANES), jnp.float32),
        ],
        scratch_shapes=[
            pltpu.VMEM((comps, nx, 8, nz), jnp.float32),
            pltpu.VMEM((comps, nx, ny, nz), jnp.float32),
            pltpu.SemaphoreType.DMA((nx,)),
        ],
        compiler_params=pltpu.CompilerParams(vmem_limit_bytes=8 * 2**20),
        cost_estimate=pl.CostEstimate(
            flops=60 * velocity.size, bytes_accessed=8 * velocity.size, transcendentals=0
        ),
        name="substeps",
    )(*(in_vmem(a) for a in (velocity, xlo, xhi, ylo, yhi)))


def sample_kernel(
    ids_ref, steps_ref, w_ref, xlo_ref, xhi_ref, clo_ref, chi_ref, own_lo_ref, own_hi_ref,
    p1, modes_ref, snaps_ref, gram_ref, advanced_in, ends_in, flat_in,
    advanced_ref, ends_ref, flat, snaps_out_ref, mine_ref, other_ref,
    fixed, picked, packed, sems,
):
    comps, _, ny, nz = xlo_ref.shape
    nx = flat.shape[1] * LANES // (ny * nz)
    inner = ny // 8
    tiles = nz // LANES
    sub = lax.broadcasted_iota(jnp.int32, (8, nz), 0)
    adv = 0.5 * time_step
    diff = time_step * viscosity

    def halo_tile(line, c):
        return jnp.where(sub == 0, line[c, 1:2, :], line[c, 0:1, :])

    for end, layer, mid, line, own in (
        (0, 0, xlo_ref.at[:, 1], clo_ref, own_lo_ref),
        (1, nx - 1, xhi_ref.at[:, 0], chi_ref, own_hi_ref),
    ):
        sign = 1.0 if end == 0 else -1.0
        outside = layer if end == 0 else layer + 2
        own_x = diff + sign * adv * halo_tile(own, 0)
        low_y = diff + adv * mid[1, 0:8, :]
        high_y = diff - adv * mid[1, ny - 8 : ny, :]
        for c in range(comps):
            corner = halo_tile(line, c)
            halo = p1[c, layer + 1, ny : ny + 8, :] + own_x * corner
            fixed[c, end, 2] = halo
            fixed[c, end, 0] = p1[c, outside, 0:8, :] + jnp.where(sub == 0, low_y * line[c, 0:1, :], 0.0)
            fixed[c, end, 1] = p1[c, outside, ny - 8 : ny, :] + jnp.where(sub == 7, high_y * line[c, 1:2, :], 0.0)

        def tile(k, c, t):
            if k == (-1 if end == 0 else 1):
                return fixed[c, end, 0 if t == 0 else 1]
            if t == inner:
                return fixed[c, end, 2]
            return p1[c, layer + 1 + k, 8 * t : 8 * t + 8, :]

        def store(c, t, value):
            ends_ref[c, end, 8 * t : 8 * t + 8, :] = value
            for k in range(tiles):
                at = (k * nx + layer) * ny + 8 * t
                flat[c, at : at + 8, :] = value[:, k * LANES : (k + 1) * LANES]

        stencil(tile, (0, inner - 1), inner, store)
    out_copies = [
        pltpu.make_async_copy(ends_ref.at[:, 0], advanced_ref.at[:, 0], sems.at[0]),
        pltpu.make_async_copy(ends_ref.at[:, 1], advanced_ref.at[:, nx - 1], sems.at[1]),
    ]
    for copy in out_copies:
        copy.start()

    count = ids_ref.shape[0]
    lane = lax.broadcasted_iota(jnp.int32, (1, LANES), 1)

    @pl.loop(0, count // 8)
    def _(i):
        for k in range(8):
            cell = ids_ref[i * 8 + k]
            line = lax.shift_right_logical(cell, int(math.log2(LANES)))
            at = (line & (tiles - 1)) * (nx * ny) + lax.shift_right_logical(line, int(math.log2(tiles)))
            hit = lane == (cell & (LANES - 1))
            for c in range(comps):
                row = flat[c, pl.ds(at, 1), :]
                picked[c, pl.ds(i * 8 + k, 1), :] = jnp.where(hit, row, 0.0)

    ones = jnp.ones((8, LANES), jnp.float32)
    parts = [dot(ones, picked[c], 1, 1)[0:1] for c in range(comps)]
    sample = jnp.concatenate(parts, axis=1)

    snaps_count = steps_ref.shape[0]
    place = jnp.int32(0)
    for j in range(snaps_count):
        place = jnp.where(steps_ref[j] == snaps_count - 1, j, place)
    snaps_out_ref[...] = snaps_ref[...]
    snaps_out_ref[pl.ds(place, 1), :] = sample

    k = modes_ref.shape[0]
    half = snaps_count
    tall = jnp.transpose(jnp.broadcast_to(w_ref[...], (k, k)))
    with_modes = jnp.sum(modes_ref[...] * sample, axis=1, keepdims=True) * tall
    with_snaps = jnp.sum(snaps_out_ref[...] * sample, axis=1, keepdims=True)
    col = lax.broadcasted_iota(jnp.int32, (half, half), 1)
    row = lax.broadcasted_iota(jnp.int32, (half, half), 0)
    col_k = lax.broadcasted_iota(jnp.int32, (k, half), 1)
    cross = jnp.where(col_k == place, with_modes[:, 0:half], gram_ref[0:k, k:])
    splat = jnp.broadcast_to(with_snaps, (half, LANES))[:, 0:half]
    low = jnp.where(col == place, splat, gram_ref[k:, k:])
    low = jnp.where(row == place, jnp.transpose(splat), low)
    packed[0:half, 0:half] = gram_ref[0:half, half:k]
    packed[0:half, half:k] = cross[0:half]
    packed[half:k, 0:half] = gram_ref[half:k, half:k]
    packed[half:k, half:k] = cross[half:k]
    packed[k:, 0:half] = gram_ref[0:half, 0:half]
    packed[k:, half:k] = low
    part = mine_ref.shape[0]
    core = lax.axis_index("grp") & 1
    mine_ref[...] = packed[pl.ds(pl.multiple_of(core * part, 8), part), :]
    other_ref[...] = packed[pl.ds(pl.multiple_of((1 - core) * part, 8), part), :]
    for copy in out_copies:
        copy.wait()


def sample_call(
    ids, steps, weights, xlo, xhi, clo, chi, own_lo, own_hi, p1, modes, snaps, gram, advanced, ends, flat
):
    comps, _, _, nz = xlo.shape
    total = gram.shape[0]
    part = total // 2
    smem = pl.BlockSpec(memory_space=pltpu.SMEM)
    vmem = pl.BlockSpec(memory_space=pltpu.VMEM)
    hbm = pl.BlockSpec(memory_space=pl.ANY)
    tail = (weights, xlo, xhi, clo, chi, own_lo, own_hi, p1, modes, snaps, gram)
    return pl.pallas_call(
        sample_kernel,
        in_specs=[smem] * 2 + [vmem] * 11 + [hbm, vmem, vmem],
        out_specs=[hbm, vmem, vmem, vmem, vmem, vmem],
        out_shape=[
            pltpu.HBM(advanced.shape, jnp.float32),
            pltpu.VMEM(ends.shape, jnp.float32),
            pltpu.VMEM(flat.shape, jnp.float32),
            pltpu.VMEM(snaps.shape, jnp.float32),
            pltpu.VMEM((part, LANES), jnp.float32),
            pltpu.VMEM((part, LANES), jnp.float32),
        ],
        input_output_aliases={13: 0, 14: 1, 15: 2},
        scratch_shapes=[
            pltpu.VMEM((comps, 2, 3, 8, nz), jnp.float32),
            pltpu.VMEM((comps, ids.shape[0], LANES), jnp.float32),
            pltpu.VMEM((total, LANES), jnp.float32),
            pltpu.SemaphoreType.DMA((2,)),
        ],
        compiler_params=pltpu.CompilerParams(vmem_limit_bytes=6 * 2**20),
        cost_estimate=pl.CostEstimate(
            flops=20 * flat.size, bytes_accessed=2 * flat.size, transcendentals=0
        ),
        name="sample_and_gram",
    )(
        in_vmem(ids), in_vmem(steps), *(in_vmem(a) for a in tail),
        in_hbm(advanced), in_vmem(ends), in_vmem(flat),
    )


def eliminate(pieces, start):
    n = pieces[0].shape[0]
    done = []
    base = 0
    for j in range(0, n, GROUP):
        if j > base:
            done.append([piece[: j - base] for piece in pieces])
            pieces = [piece[j - base :] for piece in pieces]
            base = j
        h = n - base
        rows = lax.broadcasted_iota(jnp.int32, (h, LANES), 0) + base
        spread = []
        for k in range(GROUP):
            column = start + j + k
            spread.append(jnp.broadcast_to(pieces[0][:, column : column + 1], (h, LANES)))
        for k in range(GROUP):
            pivot = spread[k][k : k + 1, :]
            ratio = jnp.where(rows > j + k, spread[k], 0.0) * (1.0 / pivot)
            for l in range(k + 1, GROUP):
                spread[l] = spread[l] - ratio * spread[l][k : k + 1, :]
            pieces = [piece - ratio * piece[k : k + 1, :] for piece in pieces]
    done.append(pieces)
    pieces = [jnp.concatenate([d[q] for d in done], axis=0) for q in range(len(pieces))]
    row = lax.broadcasted_iota(jnp.int32, (n, LANES), 0)
    lane = lax.broadcasted_iota(jnp.int32, (n, LANES), 1)
    pivots = jnp.sum(jnp.where(lane == row + start, pieces[0], 0.0), axis=1, keepdims=True)
    scale = lax.rsqrt(pivots)
    return [piece * scale for piece in pieces]


def basis_kernel(
    root, w_ref, mine_ref, other_ref, modes_ref, snaps_ref, factor_ref, basis_ref, packed, inverse, factor, basis, sems
):
    total = factor.shape[0]
    half = total // 3
    two = 2 * half
    part = mine_ref.shape[0]
    core = lax.axis_index("grp") & 1
    packed[pl.ds(pl.multiple_of(core * part, 8), part), :] = mine_ref[...]
    packed[pl.ds(pl.multiple_of((1 - core) * part, 8), part), :] = other_ref[...]
    row = lax.broadcasted_iota(jnp.int32, (half, LANES), 0)
    lane = lax.broadcasted_iota(jnp.int32, (half, LANES), 1)
    left = lane < half
    eye = (row == lane).astype(jnp.float32)
    eye_right = (row + half == lane).astype(jnp.float32)
    ends = packed[two:, :]
    r0, w0 = eliminate([jnp.where(left, ends, eye_right), packed[0:half, :]], 0)
    d = dot(w0, jnp.concatenate([r0, w0], axis=1), 0, 0)
    r1, m1 = eliminate([packed[half:two, :] - d[0:half, LANES:], jnp.where(left, eye, -d[0:half, 0:LANES])], 0)
    e = dot(r1, jnp.concatenate([r1, m1], axis=1), 0, 0)[half:two]
    r2, m2 = eliminate(
        [
            jnp.where(left, eye, ends - d[half:two, LANES:] - e[:, 0:LANES]),
            jnp.where(left, 0.0, -d[half:two, 0:LANES]) - e[:, LANES:],
        ],
        half,
    )
    wide = pltpu.roll(w_ref[...], half, 1) * root
    inverse[0:half, 0:two] = jnp.where(left, 0.0, r0) * wide
    inverse[half:two, 0:two] = m1 * wide
    inverse[two:, 0:two] = m2 * wide
    zero = jnp.zeros((half, half), jnp.float32)
    inverse[0:half, two:total] = zero
    inverse[half:two, two:total] = zero
    inverse[two:, two:total] = r2[:, 0:half] * root
    scale = 1.0 / root
    factor[0:half, 0:half] = jnp.where(row <= lane, r0, 0.0)[:, 0:half] * scale
    factor[0:half, half:] = w0 * scale
    factor[half:two, 0:half] = zero
    factor[half:two, half:] = jnp.where(row <= lane, r1, 0.0) * scale
    factor[two:, 0:half] = zero
    factor[two:, half:two] = zero
    factor[two:, two:] = jnp.where(row + half <= lane, r2, 0.0)[:, half:] * scale
    copies = [pltpu.make_async_copy(factor, factor_ref, sems.at[0])]
    copies[0].start()
    width = basis.shape[1]
    parts = sems.shape[0] - 1
    chunk = width // parts
    for i in range(parts):
        at = slice(i * chunk, (i + 1) * chunk)
        rows = jnp.concatenate([modes_ref[half:two, at], modes_ref[0:half, at], snaps_ref[:, at]], axis=0)
        basis[:, at] = dot(inverse[:, 0:total], rows)
        copies.append(pltpu.make_async_copy(basis.at[:, at], basis_ref.at[:, at], sems.at[i + 1]))
        copies[-1].start()
    for copy in copies:
        copy.wait()


def basis_call(root, weights, mine, other, modes, snaps):
    k, width = modes.shape
    total = k + snaps.shape[0]
    vmem = pl.BlockSpec(memory_space=pltpu.VMEM)
    hbm = pl.BlockSpec(memory_space=pl.ANY)
    return pl.pallas_call(
        functools.partial(basis_kernel, root),
        in_specs=[vmem] * 5,
        out_specs=[hbm, hbm],
        out_shape=[pltpu.HBM((total, total), jnp.float32), pltpu.HBM((total, width), jnp.float32)],
        scratch_shapes=[
            pltpu.VMEM((total, LANES), jnp.float32),
            pltpu.VMEM((total, 2 * LANES), jnp.float32),
            pltpu.VMEM((total, total), jnp.float32),
            pltpu.VMEM((total, width), jnp.float32),
            pltpu.SemaphoreType.DMA((PARTS + 1,)),
        ],
        compiler_params=pltpu.CompilerParams(vmem_limit_bytes=16 * 2**20),
        cost_estimate=pl.CostEstimate(
            flops=12 * total * total * width, bytes_accessed=8 * total * width, transcendentals=0
        ),
        name="factor_and_basis",
    )(in_vmem(weights), in_vmem(mine), in_vmem(other), in_vmem(modes), in_vmem(snaps))


def ring(axis):
    count = lax.axis_size(axis)
    forward = [(i, (i + 1) % count) for i in range(count)]
    backward = [(i, (i - 1) % count) for i in range(count)]
    return forward, backward


def swap(array, bits):
    devices = lax.axis_size("tile") * lax.axis_size("grp")
    return lax.ppermute(array, ("tile", "grp"), [(i, i ^ bits) for i in range(devices)])


def per_device(velocity, modes, mode_weights, history, slab_ids, snap_steps):
    ylow, yhigh, xlow, xhigh = faces(velocity)
    up_y, down_y = ring("tile")
    up, down = ring("grp")
    ylo = lax.ppermute(yhigh, "tile", up_y)
    yhi = lax.ppermute(ylow, "tile", down_y)
    xlo = lax.ppermute(xhigh, "grp", up)
    xhi = lax.ppermute(xlow, "grp", down)

    weights = mode_weights.reshape(1, -1)
    gram, snaps = early_gram(snap_steps, weights, modes, history)

    clow, chigh = corners(ylo, yhi, gram)
    clo = lax.ppermute(chigh, "grp", up)
    chi = lax.ppermute(clow, "grp", down)

    advanced, p1, ends, flat = field_call(velocity, xlo, xhi, ylo, yhi)
    advanced, _, _, snaps, mine, other = sample_call(
        slab_ids, snap_steps, weights, xlo, xhi, clo, chi, clow, chigh, p1, modes, snaps, gram, advanced, ends, flat
    )

    devices = lax.axis_size("tile") * lax.axis_size("grp")
    mine = mine + swap(other, 1)
    bit = 2
    while bit < devices:
        total = mine + swap(mine, bit)
        if 2 * bit < devices:
            total = total + (swap(mine, 2 * bit) + swap(mine, 3 * bit))
        mine = total
        bit *= 4
    other = swap(mine, 1)

    root = math.sqrt(modes.shape[1] * devices)
    factor, basis = basis_call(root, weights, mine, other, modes, snaps)
    return (advanced, basis, factor)


def solution(mesh):
    return jax.shard_map(
        per_device,
        mesh=mesh,
        in_specs=(
            P(None, "grp", "tile", None),
            P(None, ("tile", "grp")),
            P(),
            P(None, ("tile", "grp")),
            P(("tile", "grp")),
            P(),
        ),
        out_specs=(P(None, "grp", "tile", None), P(None, ("tile", "grp")), P()),
        check_vma=False,
    )
```

```python
import functools
import math

import jax
import jax.numpy as jnp
from jax import lax
from jax.experimental import pallas as pl
from jax.experimental.pallas import tpu as pltpu
from jax.sharding import PartitionSpec as P

time_step = 0.1
viscosity = 0.5
HIGHEST = lax.Precision.HIGHEST
LANES = 128
GROUP = 16
PARTS = 3


def in_hbm(array):
    return pltpu.with_memory_space_constraint(array, pltpu.HBM)


def in_vmem(array):
    return pltpu.with_memory_space_constraint(array, pltpu.VMEM)


def dot(a, b, ca=1, cb=0):
    return lax.dot_general(
        a, b, (((ca,), (cb,)), ((), ())), precision=HIGHEST, preferred_element_type=jnp.float32
    )


def faces_kernel(velocity_ref, ylow_ref, yhigh_ref, xlow_ref, xhigh_ref, sems):
    nx, ny = velocity_ref.shape[1:3]
    copies = [
        pltpu.make_async_copy(velocity_ref.at[:, :, 0:2, :], ylow_ref, sems.at[0]),
        pltpu.make_async_copy(velocity_ref.at[:, :, ny - 2 : ny, :], yhigh_ref, sems.at[1]),
        pltpu.make_async_copy(velocity_ref.at[:, 0:2], xlow_ref, sems.at[2]),
        pltpu.make_async_copy(velocity_ref.at[:, nx - 2 : nx], xhigh_ref, sems.at[3]),
    ]
    for copy in copies:
        copy.start()
    for copy in copies:
        copy.wait()


def faces(velocity):
    comps, nx, ny, nz = velocity.shape
    vmem = pl.BlockSpec(memory_space=pltpu.VMEM)
    across_x = pltpu.VMEM((comps, 2, ny, nz), jnp.float32)
    across_y = pltpu.VMEM((comps, nx, 2, nz), jnp.float32)
    return pl.pallas_call(
        faces_kernel,
        in_specs=[pl.BlockSpec(memory_space=pl.ANY)],
        out_specs=[vmem] * 4,
        out_shape=[across_y, across_y, across_x, across_x],
        scratch_shapes=[pltpu.SemaphoreType.DMA((4,))],
        compiler_params=pltpu.CompilerParams(vmem_limit_bytes=2 * 2**20),
        name="faces",
    )(in_hbm(velocity))


def split(array):
    high = array.astype(jnp.bfloat16)
    rest = array - high.astype(jnp.float32)
    mid = rest.astype(jnp.bfloat16)
    return high, mid, (rest - mid.astype(jnp.float32)).astype(jnp.bfloat16)


def gram_kernel(
    lines, steps_ref, w_ref, modes_ref, history_ref, ids_ref, gram_ref, snaps_ref, tall_ref, at_ref, mask_ref
):
    k = modes_ref.shape[0]
    count = snaps_ref.shape[0]
    last = count - 1
    place = jnp.int32(0)
    for j in range(count):
        step = steps_ref[j]
        place = jnp.where(step == last, j, place)
        row = history_ref[pl.ds(jnp.minimum(step, last - 1), 1), :]
        snaps_ref[j : j + 1, :] = jnp.where(step == last, 0.0, row)
    total = k + count
    nt = (((1,), (1,)), ((), ()))
    high, mid, low = split(jnp.concatenate([modes_ref[...], snaps_ref[...]], axis=0))
    first = lax.dot_general(
        jnp.concatenate([high, mid, low], axis=0), high, nt, preferred_element_type=jnp.float32
    )
    second = lax.dot_general(mid, mid, nt, preferred_element_type=jnp.float32)
    side = first[total : 2 * total] + first[2 * total :]
    gram = first[0:total] + (second + (side + jnp.transpose(side)))
    wide = jnp.broadcast_to(w_ref[...], (k, k))
    tall = jnp.transpose(wide)
    tall_ref[...] = tall
    gram_ref[0:k, 0:k] = gram[0:k, 0:k] * wide * tall
    gram_ref[0:k, k:] = gram[0:k, k:] * tall[:, 0:count]
    gram_ref[k:, 0:k] = jnp.zeros((count, k), jnp.float32)
    gram_ref[k:, k:] = gram[k:, k:]
    ids = ids_ref[...]
    groups = ids.shape[0]
    tiles = lines[1]
    line = lax.shift_right_logical(ids, int(math.log2(LANES)))
    at_ref[0:groups, :] = (line & (tiles - 1)) * lines[0] + lax.shift_right_logical(line, int(math.log2(tiles)))
    at_ref[groups:, :] = jnp.broadcast_to(place, (at_ref.shape[0] - groups, LANES))
    lane = (ids & (LANES - 1)).astype(jnp.float32)
    here = lax.broadcasted_iota(jnp.int32, (LANES, LANES), 1).astype(jnp.float32)
    for i in range(groups):
        there = jnp.transpose(jnp.broadcast_to(lane[i : i + 1, :], (LANES, LANES)))
        mask_ref[i * LANES : (i + 1) * LANES, :] = (here == there).astype(jnp.float32)


def early_gram(lines, steps, weights, modes, history, ids):
    k, width = modes.shape
    count = steps.shape[0]
    total = k + count
    vmem = pl.BlockSpec(memory_space=pltpu.VMEM)
    return pl.pallas_call(
        functools.partial(gram_kernel, lines),
        in_specs=[pl.BlockSpec(memory_space=pltpu.SMEM)] + [vmem] * 4,
        out_specs=[vmem] * 5,
        out_shape=[
            pltpu.VMEM((total, total), jnp.float32),
            pltpu.VMEM((count, width), jnp.float32),
            pltpu.VMEM((k, k), jnp.float32),
            pltpu.VMEM((ids.shape[0] + 8, LANES), jnp.int32),
            pltpu.VMEM((ids.size, LANES), jnp.float32),
        ],
        compiler_params=pltpu.CompilerParams(vmem_limit_bytes=16 * 2**20),
        cost_estimate=pl.CostEstimate(
            flops=8 * total * total * width, bytes_accessed=12 * total * width, transcendentals=0
        ),
        name="early_gram",
    )(*(in_vmem(a) for a in (steps, weights, modes, history, ids)))


def stencil(tile, which, inner, store):
    adv = 0.5 * time_step
    diff = time_step * viscosity
    sub = lax.broadcasted_iota(jnp.int32, tile(0, 0, 0).shape, 0)
    first, last = sub == 0, sub == 7
    for t in which:
        before, after = (t - 1) % (inner + 1), (t + 1) % (inner + 1)
        mid = [tile(0, c, t) for c in range(3)]
        scaled = [adv * v for v in mid]
        plus = [diff - v for v in scaled]
        minus = [diff + v for v in scaled]
        for c in range(3):
            v = mid[c]
            y_plus = jnp.where(last, pltpu.roll(tile(0, c, after), 7, 0), pltpu.roll(v, 7, 0))
            y_minus = jnp.where(first, pltpu.roll(tile(0, c, before), 1, 0), pltpu.roll(v, 1, 0))
            out = (1.0 - 6.0 * diff) * v
            out = out + plus[0] * tile(1, c, t) + minus[0] * tile(-1, c, t)
            out = out + plus[1] * y_plus + minus[1] * y_minus
            out = out + plus[2] * pltpu.roll(v, v.shape[1] - 1, 1) + minus[2] * pltpu.roll(v, 1, 1)
            store(c, t, out)


def inner_kernel(velocity_ref, p1, flat, u2):
    comps, nx, ny, nz = velocity_ref.shape
    inner = ny // 8
    zero = jnp.zeros((8, nz), jnp.float32)

    def first_layer(x):
        def tile(k, c, t):
            if t == inner or (isinstance(x, int) and not 0 <= x + k < nx):
                return zero
            return velocity_ref[c, x + k, 8 * t : 8 * t + 8, :]

        def store(c, t, value):
            p1[c, x + 1, 8 * t : 8 * t + 8, :] = value

        stencil(tile, range(inner), inner, store)

    first_layer(0)

    @pl.loop(1, nx - 1)
    def _(x):
        first_layer(x)

    first_layer(nx - 1)

    @pl.loop(2, nx - 2)
    def _(x):
        second_layer(p1, u2, flat, x, range(1, inner - 1))


def second_layer(p1, u2, flat, x, which):
    comps, nx, ny, nz = u2.shape

    def tile(k, c, t):
        return p1[c, x + 1 + k, 8 * t : 8 * t + 8, :]

    def store(c, t, value):
        u2[c, x, 8 * t : 8 * t + 8, :] = value
        for k in range(nz // LANES):
            at = (k * nx + x) * ny + 8 * t
            flat[c, pl.ds(at if isinstance(at, int) else pl.multiple_of(at, 8), 8), :] = value[
                :, k * LANES : (k + 1) * LANES
            ]

    stencil(tile, which, ny // 8, store)


def halo_kernel(
    velocity_ref, xlo_ref, xhi_ref, ylo_ref, yhi_ref, gram_ref, p1_in, p1, clow_ref, chigh_ref, ring_tile
):
    comps, nx, ny, nz = velocity_ref.shape
    inner = ny // 8
    adv = 0.5 * time_step
    diff = time_step * viscosity
    vel = velocity_ref
    for c in range(comps):
        clow_ref[c, 0:1, :] = ylo_ref[c, 0, 1:2, :]
        clow_ref[c, 1:2, :] = yhi_ref[c, 0, 0:1, :]
        chigh_ref[c, 0:1, :] = ylo_ref[c, nx - 1, 1:2, :]
        chigh_ref[c, 1:2, :] = yhi_ref[c, nx - 1, 0:1, :]
        for x in range(nx):
            ring_tile[c, x, 0:2, :] = yhi_ref[c, x]
            ring_tile[c, x, 6:8, :] = ylo_ref[c, x]
    for x in range(nx):
        low = diff + adv * vel[1, x, 0:1, :]
        high = diff - adv * vel[1, x, ny - 1 : ny, :]
        for c in range(comps):
            p1[c, x + 1, 0:1, :] = p1[c, x + 1, 0:1, :] + low * ylo_ref[c, x, 1:2, :]
            p1[c, x + 1, ny - 1 : ny, :] = p1[c, x + 1, ny - 1 : ny, :] + high * yhi_ref[c, x, 0:1, :]
    low = diff + adv * vel[0, 0]
    high = diff - adv * vel[0, nx - 1]
    for c in range(comps):
        p1[c, 1, 0:ny, :] = p1[c, 1, 0:ny, :] + low * xlo_ref[c, 1]
        p1[c, nx, 0:ny, :] = p1[c, nx, 0:ny, :] + high * xhi_ref[c, 0]

    def layer(x, refs, layers, which):
        def tile(k, c, t):
            if t == inner:
                if isinstance(x, int) and not 0 <= x + k < nx:
                    return jnp.zeros((8, nz), jnp.float32)
                return ring_tile[c, x + k]
            return refs[k + 1][c, layers[k + 1], 8 * t : 8 * t + 8, :]

        def store(c, t, value):
            p1[c, x + 1, 8 * t : 8 * t + 8, :] = value

        stencil(tile, which, inner, store)

    layer(-1, (xlo_ref, xlo_ref, vel), (0, 1, 0), range(inner))
    layer(nx, (vel, xhi_ref, xhi_ref), (nx - 1, 0, 1), range(inner))
    layer(0, (vel, vel, vel), (0, 0, 1), (inner,))

    @pl.loop(1, nx - 1)
    def _(x):
        layer(x, (vel, vel, vel), (x - 1, x, x + 1), (inner,))

    layer(nx - 1, (vel, vel, vel), (nx - 2, nx - 1, nx - 1), (inner,))


def outer_kernel(p1, flat_in, u2_in, flat, u2, advanced_ref, out_sems):
    comps, nx, ny, nz = u2.shape
    inner = ny // 8

    def out_copy(x):
        return pltpu.make_async_copy(u2.at[:, x], advanced_ref.at[:, x], out_sems.at[x])

    @pl.loop(2, nx - 2)
    def _(x):
        second_layer(p1, u2, flat, x, (0, inner - 1))
        out_copy(x).start()

    for x in (1, nx - 2):
        second_layer(p1, u2, flat, x, range(inner))
        out_copy(x).start()
    for x in (0, nx - 1):
        second_layer(p1, u2, flat, x, range(inner))

    @pl.loop(1, nx - 1)
    def _(x):
        out_copy(x).wait()


def spaces(velocity):
    comps, nx, ny, nz = velocity.shape
    return (
        pltpu.VMEM((comps, nx + 2, ny + 8, nz), jnp.float32),
        pltpu.VMEM((comps, nx * ny * nz // LANES, LANES), jnp.float32),
        pltpu.VMEM((comps, nx, ny, nz), jnp.float32),
    )


def inner_call(velocity):
    vmem = pl.BlockSpec(memory_space=pltpu.VMEM)
    return pl.pallas_call(
        inner_kernel,
        in_specs=[vmem],
        out_specs=[vmem] * 3,
        out_shape=list(spaces(velocity)),
        compiler_params=pltpu.CompilerParams(vmem_limit_bytes=2 * 2**20),
        cost_estimate=pl.CostEstimate(
            flops=60 * velocity.size, bytes_accessed=4 * velocity.size, transcendentals=0
        ),
        name="inner_cells",
    )(in_vmem(velocity))


def halo_call(velocity, xlo, xhi, ylo, yhi, gram, p1):
    comps, nx, ny, nz = velocity.shape
    vmem = pl.BlockSpec(memory_space=pltpu.VMEM)
    line = pltpu.VMEM((comps, 2, nz), jnp.float32)
    return pl.pallas_call(
        halo_kernel,
        in_specs=[vmem] * 7,
        out_specs=[vmem] * 3,
        out_shape=[spaces(velocity)[0], line, line],
        input_output_aliases={6: 0},
        scratch_shapes=[pltpu.VMEM((comps, nx, 8, nz), jnp.float32)],
        compiler_params=pltpu.CompilerParams(vmem_limit_bytes=4 * 2**20),
        cost_estimate=pl.CostEstimate(
            flops=15 * velocity.size, bytes_accessed=velocity.size, transcendentals=0
        ),
        name="halo_part",
    )(*(in_vmem(a) for a in (velocity, xlo, xhi, ylo, yhi, gram, p1)))


def outer_call(velocity, p1, flat, u2):
    nx = velocity.shape[1]
    vmem = pl.BlockSpec(memory_space=pltpu.VMEM)
    return pl.pallas_call(
        outer_kernel,
        in_specs=[vmem] * 3,
        out_specs=[vmem, vmem, pl.BlockSpec(memory_space=pl.ANY)],
        out_shape=[*spaces(velocity)[1:], pltpu.HBM(velocity.shape, jnp.float32)],
        input_output_aliases={1: 0, 2: 1},
        scratch_shapes=[pltpu.SemaphoreType.DMA((nx,))],
        compiler_params=pltpu.CompilerParams(vmem_limit_bytes=2 * 2**20),
        cost_estimate=pl.CostEstimate(
            flops=20 * velocity.size, bytes_accessed=4 * velocity.size, transcendentals=0
        ),
        name="outer_cells",
    )(in_vmem(p1), in_vmem(flat), in_vmem(u2))


def sample_kernel(
    at_ref, mask_ref, tall_ref, xlo_ref, xhi_ref, clo_ref, chi_ref, own_lo_ref, own_hi_ref,
    p1, modes_ref, gram_ref, advanced_in, u2_in, flat_in, snaps_in,
    advanced_ref, u2, flat, snaps_ref, mine_ref, other_ref,
    fixed, picked, packed, sems,
):
    comps, _, ny, nz = xlo_ref.shape
    nx = flat.shape[1] * LANES // (ny * nz)
    inner = ny // 8
    tiles = nz // LANES
    sub = lax.broadcasted_iota(jnp.int32, (8, nz), 0)
    adv = 0.5 * time_step
    diff = time_step * viscosity

    def halo_tile(line, c):
        return jnp.where(sub == 0, line[c, 1:2, :], line[c, 0:1, :])

    for end, layer, mid, line, own in (
        (0, 0, xlo_ref.at[:, 1], clo_ref, own_lo_ref),
        (1, nx - 1, xhi_ref.at[:, 0], chi_ref, own_hi_ref),
    ):
        sign = 1.0 if end == 0 else -1.0
        outside = layer if end == 0 else layer + 2
        own_x = diff + sign * adv * halo_tile(own, 0)
        low_y = diff + adv * mid[1, 0:8, :]
        high_y = diff - adv * mid[1, ny - 8 : ny, :]
        for c in range(comps):
            corner = halo_tile(line, c)
            halo = p1[c, layer + 1, ny : ny + 8, :] + own_x * corner
            fixed[c, end, 2] = halo
            fixed[c, end, 0] = p1[c, outside, 0:8, :] + jnp.where(sub == 0, low_y * line[c, 0:1, :], 0.0)
            fixed[c, end, 1] = p1[c, outside, ny - 8 : ny, :] + jnp.where(sub == 7, high_y * line[c, 1:2, :], 0.0)

        def tile(k, c, t):
            if k == (-1 if end == 0 else 1):
                return fixed[c, end, 0 if t == 0 else 1]
            if t == inner:
                return fixed[c, end, 2]
            return p1[c, layer + 1 + k, 8 * t : 8 * t + 8, :]

        def store(c, t, value):
            u2[c, layer, 8 * t : 8 * t + 8, :] = value
            for k in range(tiles):
                at = (k * nx + layer) * ny + 8 * t
                flat[c, at : at + 8, :] = value[:, k * LANES : (k + 1) * LANES]

        stencil(tile, (0, inner - 1), inner, store)
    out_copies = [
        pltpu.make_async_copy(u2.at[:, 0], advanced_ref.at[:, 0], sems.at[0]),
        pltpu.make_async_copy(u2.at[:, nx - 1], advanced_ref.at[:, nx - 1], sems.at[1]),
    ]
    for copy in out_copies:
        copy.start()

    count = mask_ref.shape[0]
    groups = count // LANES

    @pl.loop(0, groups)
    def _(g):
        for first in range(0, LANES, 8):
            ats = [at_ref[g, first + k] for k in range(8)]
            to = pl.multiple_of(g * LANES + first, 8)
            for c in range(comps):
                picked[c, pl.ds(to, 8), :] = jnp.concatenate([flat[c, pl.ds(at, 1), :] for at in ats], axis=0)

    ones = jnp.ones((16, 3 * LANES), jnp.bfloat16)
    parts = []
    for c in range(comps):
        pieces = jnp.concatenate(split(picked[c] * mask_ref[...]), axis=1)
        parts.append(
            lax.dot_general(ones, pieces, (((1,), (1,)), ((), ())), preferred_element_type=jnp.float32)[0:1]
        )
    sample = jnp.concatenate(parts, axis=1)
    place = at_ref[groups, 0]
    snaps_ref[pl.ds(place, 1), :] = sample

    k = modes_ref.shape[0]
    half = snaps_ref.shape[0]
    with_modes = jnp.sum(modes_ref[...] * sample, axis=1, keepdims=True) * tall_ref[...]
    with_snaps = jnp.sum(snaps_ref[...] * sample, axis=1, keepdims=True)
    col = lax.broadcasted_iota(jnp.int32, (half, half), 1)
    row = lax.broadcasted_iota(jnp.int32, (half, half), 0)
    col_k = lax.broadcasted_iota(jnp.int32, (k, half), 1)
    cross = jnp.where(col_k == place, with_modes[:, 0:half], gram_ref[0:k, k:])
    splat = jnp.broadcast_to(with_snaps, (half, LANES))[:, 0:half]
    low = jnp.where(col == place, splat, gram_ref[k:, k:])
    low = jnp.where(row == place, jnp.transpose(splat), low)
    packed[0:half, 0:half] = gram_ref[0:half, half:k]
    packed[0:half, half:k] = cross[0:half]
    packed[half:k, 0:half] = gram_ref[half:k, half:k]
    packed[half:k, half:k] = cross[half:k]
    packed[k:, 0:half] = gram_ref[0:half, 0:half]
    packed[k:, half:k] = low
    part = mine_ref.shape[0]
    core = lax.axis_index("grp") & 1
    mine_ref[...] = packed[pl.ds(pl.multiple_of(core * part, 8), part), :]
    other_ref[...] = packed[pl.ds(pl.multiple_of((1 - core) * part, 8), part), :]
    for copy in out_copies:
        copy.wait()


def sample_call(
    at, mask, tall, xlo, xhi, clo, chi, own_lo, own_hi, p1, modes, gram, advanced, u2, flat, snaps
):
    comps, _, _, nz = xlo.shape
    part = gram.shape[0] // 2
    vmem = pl.BlockSpec(memory_space=pltpu.VMEM)
    hbm = pl.BlockSpec(memory_space=pl.ANY)
    ins = (at, mask, tall, xlo, xhi, clo, chi, own_lo, own_hi, p1, modes, gram)
    return pl.pallas_call(
        sample_kernel,
        in_specs=[pl.BlockSpec(memory_space=pltpu.SMEM)] + [vmem] * 11 + [hbm, vmem, vmem, vmem],
        out_specs=[hbm] + [vmem] * 5,
        out_shape=[
            pltpu.HBM(advanced.shape, jnp.float32),
            pltpu.VMEM(u2.shape, jnp.float32),
            pltpu.VMEM(flat.shape, jnp.float32),
            pltpu.VMEM(snaps.shape, jnp.float32),
            pltpu.VMEM((part, LANES), jnp.float32),
            pltpu.VMEM((part, LANES), jnp.float32),
        ],
        input_output_aliases={12: 0, 13: 1, 14: 2, 15: 3},
        scratch_shapes=[
            pltpu.VMEM((comps, 2, 3, 8, nz), jnp.float32),
            pltpu.VMEM((comps, mask.shape[0], LANES), jnp.float32),
            pltpu.VMEM((2 * part, LANES), jnp.float32),
            pltpu.SemaphoreType.DMA((2,)),
        ],
        compiler_params=pltpu.CompilerParams(vmem_limit_bytes=8 * 2**20),
        cost_estimate=pl.CostEstimate(
            flops=20 * flat.size, bytes_accessed=2 * flat.size, transcendentals=0
        ),
        name="sample_and_gram",
    )(*(in_vmem(a) for a in ins), in_hbm(advanced), in_vmem(u2), in_vmem(flat), in_vmem(snaps))


def eliminate(pieces, start):
    n = pieces[0].shape[0]
    done = []
    base = 0
    for j in range(0, n, GROUP):
        if j > base:
            done.append([piece[: j - base] for piece in pieces])
            pieces = [piece[j - base :] for piece in pieces]
            base = j
        h = n - base
        rows = lax.broadcasted_iota(jnp.int32, (h, LANES), 0) + base
        spread = []
        for k in range(GROUP):
            column = start + j + k
            spread.append(jnp.broadcast_to(pieces[0][:, column : column + 1], (h, LANES)))
        for k in range(GROUP):
            pivot = spread[k][k : k + 1, :]
            ratio = jnp.where(rows > j + k, spread[k], 0.0) * (1.0 / pivot)
            for l in range(k + 1, GROUP):
                spread[l] = spread[l] - ratio * spread[l][k : k + 1, :]
            pieces = [piece - ratio * piece[k : k + 1, :] for piece in pieces]
    done.append(pieces)
    pieces = [jnp.concatenate([d[q] for d in done], axis=0) for q in range(len(pieces))]
    row = lax.broadcasted_iota(jnp.int32, (n, LANES), 0)
    lane = lax.broadcasted_iota(jnp.int32, (n, LANES), 1)
    pivots = jnp.sum(jnp.where(lane == row + start, pieces[0], 0.0), axis=1, keepdims=True)
    scale = lax.rsqrt(pivots)
    return [piece * scale for piece in pieces]


def basis_kernel(
    root, w_ref, mine_ref, other_ref, modes_ref, snaps_ref, factor_ref, basis_ref, packed, inverse, factor, basis, sems
):
    total = factor.shape[0]
    half = total // 3
    two = 2 * half
    part = mine_ref.shape[0]
    core = lax.axis_index("grp") & 1
    packed[pl.ds(pl.multiple_of(core * part, 8), part), :] = mine_ref[...]
    packed[pl.ds(pl.multiple_of((1 - core) * part, 8), part), :] = other_ref[...]
    row = lax.broadcasted_iota(jnp.int32, (half, LANES), 0)
    lane = lax.broadcasted_iota(jnp.int32, (half, LANES), 1)
    left = lane < half
    eye = (row == lane).astype(jnp.float32)
    eye_right = (row + half == lane).astype(jnp.float32)
    ends = packed[two:, :]
    r0, w0 = eliminate([jnp.where(left, ends, eye_right), packed[0:half, :]], 0)
    d = dot(w0, jnp.concatenate([r0, w0], axis=1), 0, 0)
    r1, m1 = eliminate([packed[half:two, :] - d[0:half, LANES:], jnp.where(left, eye, -d[0:half, 0:LANES])], 0)
    e = dot(r1, jnp.concatenate([r1, m1], axis=1), 0, 0)[half:two]
    r2, m2 = eliminate(
        [
            jnp.where(left, eye, ends - d[half:two, LANES:] - e[:, 0:LANES]),
            jnp.where(left, 0.0, -d[half:two, 0:LANES]) - e[:, LANES:],
        ],
        half,
    )
    wide = pltpu.roll(w_ref[...], half, 1) * root
    inverse[0:half, 0:two] = jnp.where(left, 0.0, r0) * wide
    inverse[half:two, 0:two] = m1 * wide
    inverse[two:, 0:two] = m2 * wide
    zero = jnp.zeros((half, half), jnp.float32)
    inverse[0:half, two:total] = zero
    inverse[half:two, two:total] = zero
    inverse[two:, two:total] = r2[:, 0:half] * root
    scale = 1.0 / root
    factor[0:half, 0:half] = jnp.where(row <= lane, r0, 0.0)[:, 0:half] * scale
    factor[0:half, half:] = w0 * scale
    factor[half:two, 0:half] = zero
    factor[half:two, half:] = jnp.where(row <= lane, r1, 0.0) * scale
    factor[two:, 0:half] = zero
    factor[two:, half:two] = zero
    factor[two:, two:] = jnp.where(row + half <= lane, r2, 0.0)[:, half:] * scale
    copies = [pltpu.make_async_copy(factor, factor_ref, sems.at[0])]
    copies[0].start()
    width = basis.shape[1]
    parts = sems.shape[0] - 1
    chunk = width // parts
    for i in range(parts):
        at = slice(i * chunk, (i + 1) * chunk)
        rows = jnp.concatenate([modes_ref[half:two, at], modes_ref[0:half, at], snaps_ref[:, at]], axis=0)
        basis[:, at] = dot(inverse[:, 0:total], rows)
        copies.append(pltpu.make_async_copy(basis.at[:, at], basis_ref.at[:, at], sems.at[i + 1]))
        copies[-1].start()
    for copy in copies:
        copy.wait()


def basis_call(root, weights, mine, other, modes, snaps):
    k, width = modes.shape
    total = k + snaps.shape[0]
    vmem = pl.BlockSpec(memory_space=pltpu.VMEM)
    hbm = pl.BlockSpec(memory_space=pl.ANY)
    return pl.pallas_call(
        functools.partial(basis_kernel, root),
        in_specs=[vmem] * 5,
        out_specs=[hbm, hbm],
        out_shape=[pltpu.HBM((total, total), jnp.float32), pltpu.HBM((total, width), jnp.float32)],
        scratch_shapes=[
            pltpu.VMEM((total, LANES), jnp.float32),
            pltpu.VMEM((total, 2 * LANES), jnp.float32),
            pltpu.VMEM((total, total), jnp.float32),
            pltpu.VMEM((total, width), jnp.float32),
            pltpu.SemaphoreType.DMA((PARTS + 1,)),
        ],
        compiler_params=pltpu.CompilerParams(vmem_limit_bytes=16 * 2**20),
        cost_estimate=pl.CostEstimate(
            flops=12 * total * total * width, bytes_accessed=8 * total * width, transcendentals=0
        ),
        name="factor_and_basis",
    )(in_vmem(weights), in_vmem(mine), in_vmem(other), in_vmem(modes), in_vmem(snaps))


def ring(axis):
    count = lax.axis_size(axis)
    forward = [(i, (i + 1) % count) for i in range(count)]
    backward = [(i, (i - 1) % count) for i in range(count)]
    return forward, backward


def swap(array, bits):
    devices = lax.axis_size("tile") * lax.axis_size("grp")
    return lax.ppermute(array, ("tile", "grp"), [(i, i ^ bits) for i in range(devices)])


def per_device(velocity, modes, mode_weights, history, slab_ids, snap_steps):
    ylow, yhigh, xlow, xhigh = faces(velocity)
    up_y, down_y = ring("tile")
    up, down = ring("grp")
    ylo = lax.ppermute(yhigh, "tile", up_y)
    yhi = lax.ppermute(ylow, "tile", down_y)
    xlo = lax.ppermute(xhigh, "grp", up)
    xhi = lax.ppermute(xlow, "grp", down)

    weights = mode_weights.reshape(1, -1)
    comps, nx, ny, nz = velocity.shape
    gram, snaps, tall, at, mask = early_gram(
        (nx * ny, nz // LANES), snap_steps, weights, modes, history, slab_ids.reshape(-1, LANES)
    )

    p1, flat, u2 = inner_call(velocity)
    p1, clow, chigh = halo_call(velocity, xlo, xhi, ylo, yhi, gram, p1)
    clo = lax.ppermute(chigh, "grp", up)
    chi = lax.ppermute(clow, "grp", down)
    flat, u2, advanced = outer_call(velocity, p1, flat, u2)
    advanced, _, _, snaps, mine, other = sample_call(
        at, mask, tall, xlo, xhi, clo, chi, clow, chigh, p1, modes, gram, advanced, u2, flat, snaps
    )

    devices = lax.axis_size("tile") * lax.axis_size("grp")
    mine = mine + swap(other, 1)
    bit = 2
    while bit < devices:
        total = mine + swap(mine, bit)
        if 2 * bit < devices:
            total = total + (swap(mine, 2 * bit) + swap(mine, 3 * bit))
        mine = total
        bit *= 4
    other = swap(mine, 1)

    root = math.sqrt(modes.shape[1] * devices)
    factor, basis = basis_call(root, weights, mine, other, modes, snaps)
    return (advanced, basis, factor)


def solution(mesh):
    return jax.shard_map(
        per_device,
        mesh=mesh,
        in_specs=(
            P(None, "grp", "tile", None),
            P(None, ("tile", "grp")),
            P(),
            P(None, ("tile", "grp")),
            P(("tile", "grp")),
            P(),
        ),
        out_specs=(P(None, "grp", "tile", None), P(None, ("tile", "grp")), P()),
        check_vma=False,
    )
```

```python
import functools
import math

import jax
import jax.numpy as jnp
from jax import lax
from jax.experimental import pallas as pl
from jax.experimental.pallas import tpu as pltpu
from jax.sharding import PartitionSpec as P

time_step = 0.1
viscosity = 0.5
HIGHEST = lax.Precision.HIGHEST
LANES = 128
GROUP = 16
PARTS = 3


def in_hbm(array):
    return pltpu.with_memory_space_constraint(array, pltpu.HBM)


def in_vmem(array):
    return pltpu.with_memory_space_constraint(array, pltpu.VMEM)


def dot(a, b, ca=1, cb=0):
    return lax.dot_general(
        a, b, (((ca,), (cb,)), ((), ())), precision=HIGHEST, preferred_element_type=jnp.float32
    )


def faces_kernel(velocity_ref, ylow_ref, yhigh_ref, xlow_ref, xhigh_ref, sems):
    nx, ny = velocity_ref.shape[1:3]
    copies = [
        pltpu.make_async_copy(velocity_ref.at[:, :, 0:2, :], ylow_ref, sems.at[0]),
        pltpu.make_async_copy(velocity_ref.at[:, :, ny - 2 : ny, :], yhigh_ref, sems.at[1]),
        pltpu.make_async_copy(velocity_ref.at[:, 0:2], xlow_ref, sems.at[2]),
        pltpu.make_async_copy(velocity_ref.at[:, nx - 2 : nx], xhigh_ref, sems.at[3]),
    ]
    for copy in copies:
        copy.start()
    for copy in copies:
        copy.wait()


def faces(velocity):
    comps, nx, ny, nz = velocity.shape
    vmem = pl.BlockSpec(memory_space=pltpu.VMEM)
    across_x = pltpu.VMEM((comps, 2, ny, nz), jnp.float32)
    across_y = pltpu.VMEM((comps, nx, 2, nz), jnp.float32)
    return pl.pallas_call(
        faces_kernel,
        in_specs=[pl.BlockSpec(memory_space=pl.ANY)],
        out_specs=[vmem] * 4,
        out_shape=[across_y, across_y, across_x, across_x],
        scratch_shapes=[pltpu.SemaphoreType.DMA((4,))],
        compiler_params=pltpu.CompilerParams(vmem_limit_bytes=2 * 2**20),
        name="faces",
    )(in_hbm(velocity))


def split(array):
    high = array.astype(jnp.bfloat16)
    rest = array - high.astype(jnp.float32)
    mid = rest.astype(jnp.bfloat16)
    return high, mid, (rest - mid.astype(jnp.float32)).astype(jnp.bfloat16)


def gram_kernel(
    lines, steps_ref, w_ref, modes_ref, history_ref, ids_ref, p1_ref,
    mine_ref, other_ref, snaps_ref, tall_ref, at_ref, mask_ref, gram_ref,
):
    k = modes_ref.shape[0]
    count = snaps_ref.shape[0]
    last = count - 1
    place = jnp.int32(0)
    for j in range(count):
        step = steps_ref[j]
        place = jnp.where(step == last, j, place)
        row = history_ref[pl.ds(jnp.minimum(step, last - 1), 1), :]
        snaps_ref[j : j + 1, :] = jnp.where(step == last, 0.0, row)
    total = k + count
    nt = (((1,), (1,)), ((), ()))
    high, mid, low = split(jnp.concatenate([modes_ref[...], snaps_ref[...]], axis=0))
    first = lax.dot_general(
        jnp.concatenate([high, mid, low], axis=0), high, nt, preferred_element_type=jnp.float32
    )
    second = lax.dot_general(mid, mid, nt, preferred_element_type=jnp.float32)
    side = first[total : 2 * total] + first[2 * total :]
    gram = first[0:total] + (second + (side + jnp.transpose(side)))
    wide = jnp.broadcast_to(w_ref[...], (k, k))
    tall = jnp.transpose(wide)
    tall_ref[...] = tall
    first_rows = gram[0:k, 0:k] * wide * tall
    cross = gram[0:k, k:] * tall[:, 0:count]
    gram_ref[0:count, 0:count] = first_rows[0:count, count:]
    gram_ref[0:count, count:] = cross[0:count]
    gram_ref[count:k, 0:count] = first_rows[count:, count:]
    gram_ref[count:k, count:] = cross[count:]
    gram_ref[k:, 0:count] = first_rows[0:count, 0:count]
    gram_ref[k:, count:] = gram[k:, k:]
    part = mine_ref.shape[0]
    core = lax.axis_index("grp") & 1
    mine_ref[...] = gram_ref[pl.ds(pl.multiple_of(core * part, 8), part), :]
    other_ref[...] = gram_ref[pl.ds(pl.multiple_of((1 - core) * part, 8), part), :]
    ids = ids_ref[...]
    groups = ids.shape[0]
    tiles = lines[1]
    line = lax.shift_right_logical(ids, int(math.log2(LANES)))
    at_ref[0:groups, :] = (line & (tiles - 1)) * lines[0] + lax.shift_right_logical(line, int(math.log2(tiles)))
    at_ref[groups:, :] = jnp.broadcast_to(place, (at_ref.shape[0] - groups, LANES))
    lane = (ids & (LANES - 1)).astype(jnp.float32)
    here = lax.broadcasted_iota(jnp.int32, (LANES, LANES), 1).astype(jnp.float32)
    for i in range(groups):
        there = jnp.transpose(jnp.broadcast_to(lane[i : i + 1, :], (LANES, LANES)))
        mask_ref[i * LANES : (i + 1) * LANES, :] = (here == there).astype(jnp.float32)


def early_gram(lines, steps, weights, modes, history, ids, p1):
    k, width = modes.shape
    count = steps.shape[0]
    total = k + count
    vmem = pl.BlockSpec(memory_space=pltpu.VMEM)
    return pl.pallas_call(
        functools.partial(gram_kernel, lines),
        in_specs=[pl.BlockSpec(memory_space=pltpu.SMEM)] + [vmem] * 5,
        out_specs=[vmem] * 6,
        out_shape=[
            pltpu.VMEM((total // 2, LANES), jnp.float32),
            pltpu.VMEM((total // 2, LANES), jnp.float32),
            pltpu.VMEM((count, width), jnp.float32),
            pltpu.VMEM((k, k), jnp.float32),
            pltpu.VMEM((ids.shape[0] + 8, LANES), jnp.int32),
            pltpu.VMEM((ids.size, LANES), jnp.float32),
        ],
        scratch_shapes=[pltpu.VMEM((total, LANES), jnp.float32)],
        compiler_params=pltpu.CompilerParams(vmem_limit_bytes=16 * 2**20),
        cost_estimate=pl.CostEstimate(
            flops=8 * total * total * width, bytes_accessed=12 * total * width, transcendentals=0
        ),
        name="early_gram",
    )(*(in_vmem(a) for a in (steps, weights, modes, history, ids, p1)))


def stencil(tile, which, inner, store):
    adv = 0.5 * time_step
    diff = time_step * viscosity
    sub = lax.broadcasted_iota(jnp.int32, tile(0, 0, 0).shape, 0)
    first, last = sub == 0, sub == 7
    for t in which:
        before, after = (t - 1) % (inner + 1), (t + 1) % (inner + 1)
        mid = [tile(0, c, t) for c in range(3)]
        scaled = [adv * v for v in mid]
        plus = [diff - v for v in scaled]
        minus = [diff + v for v in scaled]
        for c in range(3):
            v = mid[c]
            y_plus = jnp.where(last, pltpu.roll(tile(0, c, after), 7, 0), pltpu.roll(v, 7, 0))
            y_minus = jnp.where(first, pltpu.roll(tile(0, c, before), 1, 0), pltpu.roll(v, 1, 0))
            out = (1.0 - 6.0 * diff) * v
            out = out + plus[0] * tile(1, c, t) + minus[0] * tile(-1, c, t)
            out = out + plus[1] * y_plus + minus[1] * y_minus
            out = out + plus[2] * pltpu.roll(v, v.shape[1] - 1, 1) + minus[2] * pltpu.roll(v, 1, 1)
            store(c, t, out)


def inner_kernel(velocity_ref, p1, flat, u2):
    comps, nx, ny, nz = velocity_ref.shape
    inner = ny // 8
    zero = jnp.zeros((8, nz), jnp.float32)

    def first_layer(x):
        def tile(k, c, t):
            if t == inner or (isinstance(x, int) and not 0 <= x + k < nx):
                return zero
            return velocity_ref[c, x + k, 8 * t : 8 * t + 8, :]

        def store(c, t, value):
            p1[c, x + 1, 8 * t : 8 * t + 8, :] = value

        stencil(tile, range(inner), inner, store)

    first_layer(0)

    @pl.loop(1, nx - 1)
    def _(x):
        first_layer(x)

    first_layer(nx - 1)

    @pl.loop(2, nx - 2)
    def _(x):
        second_layer(p1, u2, flat, x, range(1, inner - 1))


def second_layer(p1, u2, flat, x, which):
    comps, nx, ny, nz = u2.shape

    def tile(k, c, t):
        return p1[c, x + 1 + k, 8 * t : 8 * t + 8, :]

    def store(c, t, value):
        u2[c, x, 8 * t : 8 * t + 8, :] = value
        for k in range(nz // LANES):
            at = (k * nx + x) * ny + 8 * t
            flat[c, pl.ds(at if isinstance(at, int) else pl.multiple_of(at, 8), 8), :] = value[
                :, k * LANES : (k + 1) * LANES
            ]

    stencil(tile, which, ny // 8, store)


def corners_kernel(ylo_ref, yhi_ref, gram_ref, p1_ref, low_ref, high_ref):
    nx = ylo_ref.shape[1]
    for c in range(ylo_ref.shape[0]):
        low_ref[c, 0:1, :] = ylo_ref[c, 0, 1:2, :]
        low_ref[c, 1:2, :] = yhi_ref[c, 0, 0:1, :]
        high_ref[c, 0:1, :] = ylo_ref[c, nx - 1, 1:2, :]
        high_ref[c, 1:2, :] = yhi_ref[c, nx - 1, 0:1, :]


def corners(ylo, yhi, gram, p1):
    comps, _, _, nz = ylo.shape
    vmem = pl.BlockSpec(memory_space=pltpu.VMEM)
    return pl.pallas_call(
        corners_kernel,
        in_specs=[vmem] * 4,
        out_specs=[vmem, vmem],
        out_shape=[pltpu.VMEM((comps, 2, nz), jnp.float32)] * 2,
        compiler_params=pltpu.CompilerParams(vmem_limit_bytes=1 * 2**20),
        name="corners",
    )(*(in_vmem(a) for a in (ylo, yhi, gram, p1)))


def outer_kernel(
    velocity_ref, xlo_ref, xhi_ref, ylo_ref, yhi_ref, p1_in, flat_in, u2_in,
    p1, flat, u2, advanced_ref, ring_tile, out_sems,
):
    comps, nx, ny, nz = velocity_ref.shape
    inner = ny // 8
    adv = 0.5 * time_step
    diff = time_step * viscosity
    vel = velocity_ref
    for c in range(comps):
        for x in range(nx):
            ring_tile[c, x, 0:2, :] = yhi_ref[c, x]
            ring_tile[c, x, 6:8, :] = ylo_ref[c, x]
    for x in range(nx):
        low = diff + adv * vel[1, x, 0:1, :]
        high = diff - adv * vel[1, x, ny - 1 : ny, :]
        for c in range(comps):
            p1[c, x + 1, 0:1, :] = p1[c, x + 1, 0:1, :] + low * ylo_ref[c, x, 1:2, :]
            p1[c, x + 1, ny - 1 : ny, :] = p1[c, x + 1, ny - 1 : ny, :] + high * yhi_ref[c, x, 0:1, :]
    low = diff + adv * vel[0, 0]
    high = diff - adv * vel[0, nx - 1]
    for c in range(comps):
        p1[c, 1, 0:ny, :] = p1[c, 1, 0:ny, :] + low * xlo_ref[c, 1]
        p1[c, nx, 0:ny, :] = p1[c, nx, 0:ny, :] + high * xhi_ref[c, 0]

    def layer(x, refs, layers, which):
        def tile(k, c, t):
            if t == inner:
                if isinstance(x, int) and not 0 <= x + k < nx:
                    return jnp.zeros((8, nz), jnp.float32)
                return ring_tile[c, x + k]
            return refs[k + 1][c, layers[k + 1], 8 * t : 8 * t + 8, :]

        def store(c, t, value):
            p1[c, x + 1, 8 * t : 8 * t + 8, :] = value

        stencil(tile, which, inner, store)

    layer(-1, (xlo_ref, xlo_ref, vel), (0, 1, 0), range(inner))
    layer(nx, (vel, xhi_ref, xhi_ref), (nx - 1, 0, 1), range(inner))
    layer(0, (vel, vel, vel), (0, 0, 1), (inner,))

    @pl.loop(1, nx - 1)
    def _(x):
        layer(x, (vel, vel, vel), (x - 1, x, x + 1), (inner,))

    layer(nx - 1, (vel, vel, vel), (nx - 2, nx - 1, nx - 1), (inner,))

    def out_copy(x):
        return pltpu.make_async_copy(u2.at[:, x], advanced_ref.at[:, x], out_sems.at[x])

    @pl.loop(2, nx - 2)
    def _(x):
        second_layer(p1, u2, flat, x, (0, inner - 1))
        out_copy(x).start()

    for x in (1, nx - 2):
        second_layer(p1, u2, flat, x, range(inner))
        out_copy(x).start()
    for x in (0, nx - 1):
        second_layer(p1, u2, flat, x, range(inner))

    @pl.loop(1, nx - 1)
    def _(x):
        out_copy(x).wait()


def spaces(velocity):
    comps, nx, ny, nz = velocity.shape
    return (
        pltpu.VMEM((comps, nx + 2, ny + 8, nz), jnp.float32),
        pltpu.VMEM((comps, nx * ny * nz // LANES, LANES), jnp.float32),
        pltpu.VMEM((comps, nx, ny, nz), jnp.float32),
    )


def inner_call(velocity):
    vmem = pl.BlockSpec(memory_space=pltpu.VMEM)
    return pl.pallas_call(
        inner_kernel,
        in_specs=[vmem],
        out_specs=[vmem] * 3,
        out_shape=list(spaces(velocity)),
        compiler_params=pltpu.CompilerParams(vmem_limit_bytes=2 * 2**20),
        cost_estimate=pl.CostEstimate(
            flops=60 * velocity.size, bytes_accessed=4 * velocity.size, transcendentals=0
        ),
        name="inner_cells",
    )(in_vmem(velocity))


def outer_call(velocity, xlo, xhi, ylo, yhi, p1, flat, u2):
    comps, nx, _, nz = velocity.shape
    vmem = pl.BlockSpec(memory_space=pltpu.VMEM)
    return pl.pallas_call(
        outer_kernel,
        in_specs=[vmem] * 8,
        out_specs=[vmem, vmem, vmem, pl.BlockSpec(memory_space=pl.ANY)],
        out_shape=[*spaces(velocity), pltpu.HBM(velocity.shape, jnp.float32)],
        input_output_aliases={5: 0, 6: 1, 7: 2},
        scratch_shapes=[pltpu.VMEM((comps, nx, 8, nz), jnp.float32), pltpu.SemaphoreType.DMA((nx,))],
        compiler_params=pltpu.CompilerParams(vmem_limit_bytes=4 * 2**20),
        cost_estimate=pl.CostEstimate(
            flops=40 * velocity.size, bytes_accessed=4 * velocity.size, transcendentals=0
        ),
        name="outer_cells",
    )(*(in_vmem(a) for a in (velocity, xlo, xhi, ylo, yhi, p1, flat, u2)))


def sample_kernel(
    at_ref, mask_ref, tall_ref, xlo_ref, xhi_ref, clo_ref, chi_ref, own_lo_ref, own_hi_ref,
    p1, modes_ref, early_ref, beside_ref, advanced_in, u2_in, flat_in, snaps_in,
    advanced_ref, u2, flat, snaps_ref, sum_ref,
    fixed, picked, sems,
):
    comps, _, ny, nz = xlo_ref.shape
    nx = flat.shape[1] * LANES // (ny * nz)
    inner = ny // 8
    tiles = nz // LANES
    sub = lax.broadcasted_iota(jnp.int32, (8, nz), 0)
    adv = 0.5 * time_step
    diff = time_step * viscosity

    def halo_tile(line, c):
        return jnp.where(sub == 0, line[c, 1:2, :], line[c, 0:1, :])

    for end, layer, mid, line, own in (
        (0, 0, xlo_ref.at[:, 1], clo_ref, own_lo_ref),
        (1, nx - 1, xhi_ref.at[:, 0], chi_ref, own_hi_ref),
    ):
        sign = 1.0 if end == 0 else -1.0
        outside = layer if end == 0 else layer + 2
        own_x = diff + sign * adv * halo_tile(own, 0)
        low_y = diff + adv * mid[1, 0:8, :]
        high_y = diff - adv * mid[1, ny - 8 : ny, :]
        for c in range(comps):
            corner = halo_tile(line, c)
            halo = p1[c, layer + 1, ny : ny + 8, :] + own_x * corner
            fixed[c, end, 2] = halo
            fixed[c, end, 0] = p1[c, outside, 0:8, :] + jnp.where(sub == 0, low_y * line[c, 0:1, :], 0.0)
            fixed[c, end, 1] = p1[c, outside, ny - 8 : ny, :] + jnp.where(sub == 7, high_y * line[c, 1:2, :], 0.0)

        def tile(k, c, t):
            if k == (-1 if end == 0 else 1):
                return fixed[c, end, 0 if t == 0 else 1]
            if t == inner:
                return fixed[c, end, 2]
            return p1[c, layer + 1 + k, 8 * t : 8 * t + 8, :]

        def store(c, t, value):
            u2[c, layer, 8 * t : 8 * t + 8, :] = value
            for k in range(tiles):
                at = (k * nx + layer) * ny + 8 * t
                flat[c, at : at + 8, :] = value[:, k * LANES : (k + 1) * LANES]

        stencil(tile, (0, inner - 1), inner, store)
    out_copies = [
        pltpu.make_async_copy(u2.at[:, 0], advanced_ref.at[:, 0], sems.at[0]),
        pltpu.make_async_copy(u2.at[:, nx - 1], advanced_ref.at[:, nx - 1], sems.at[1]),
    ]
    for copy in out_copies:
        copy.start()

    count = mask_ref.shape[0]
    groups = count // LANES

    @pl.loop(0, groups)
    def _(g):
        for first in range(0, LANES, 8):
            ats = [at_ref[g, first + k] for k in range(8)]
            to = pl.multiple_of(g * LANES + first, 8)
            for c in range(comps):
                picked[c, pl.ds(to, 8), :] = jnp.concatenate([flat[c, pl.ds(at, 1), :] for at in ats], axis=0)

    ones = jnp.ones((16, 3 * LANES), jnp.bfloat16)
    parts = []
    for c in range(comps):
        pieces = jnp.concatenate(split(picked[c] * mask_ref[...]), axis=1)
        parts.append(
            lax.dot_general(ones, pieces, (((1,), (1,)), ((), ())), preferred_element_type=jnp.float32)[0:1]
        )
    sample = jnp.concatenate(parts, axis=1)
    place = at_ref[groups, 0]
    snaps_ref[pl.ds(place, 1), :] = sample

    k = modes_ref.shape[0]
    half = snaps_ref.shape[0]
    with_modes = jnp.sum(modes_ref[...] * sample, axis=1, keepdims=True) * tall_ref[...]
    with_snaps = jnp.sum(snaps_ref[...] * sample, axis=1, keepdims=True)
    part = early_ref.shape[0]
    sum_ref[0:part, :] = early_ref[...] + beside_ref[...]
    sum_ref[part:, :] = jnp.zeros((sum_ref.shape[0] - part, LANES), jnp.float32)
    sum_ref[part : part + 1, :] = jnp.transpose(with_modes)[0:1, :]
    sum_ref[part + 1 : part + 2, 0:half] = jnp.transpose(jnp.broadcast_to(with_snaps, (half, LANES)))[0:1, :]
    for copy in out_copies:
        copy.wait()


def sample_call(
    at, mask, tall, xlo, xhi, clo, chi, own_lo, own_hi, p1, modes, early, beside, advanced, u2, flat, snaps
):
    comps, _, _, nz = xlo.shape
    vmem = pl.BlockSpec(memory_space=pltpu.VMEM)
    hbm = pl.BlockSpec(memory_space=pl.ANY)
    ins = (at, mask, tall, xlo, xhi, clo, chi, own_lo, own_hi, p1, modes, early, beside)
    return pl.pallas_call(
        sample_kernel,
        in_specs=[pl.BlockSpec(memory_space=pltpu.SMEM)] + [vmem] * 12 + [hbm, vmem, vmem, vmem],
        out_specs=[hbm] + [vmem] * 4,
        out_shape=[
            pltpu.HBM(advanced.shape, jnp.float32),
            pltpu.VMEM(u2.shape, jnp.float32),
            pltpu.VMEM(flat.shape, jnp.float32),
            pltpu.VMEM(snaps.shape, jnp.float32),
            pltpu.VMEM((early.shape[0] + 8, LANES), jnp.float32),
        ],
        input_output_aliases={13: 0, 14: 1, 15: 2, 16: 3},
        scratch_shapes=[
            pltpu.VMEM((comps, 2, 3, 8, nz), jnp.float32),
            pltpu.VMEM((comps, mask.shape[0], LANES), jnp.float32),
            pltpu.SemaphoreType.DMA((2,)),
        ],
        compiler_params=pltpu.CompilerParams(vmem_limit_bytes=8 * 2**20),
        cost_estimate=pl.CostEstimate(
            flops=20 * flat.size, bytes_accessed=2 * flat.size, transcendentals=0
        ),
        name="sample_and_gram",
    )(*(in_vmem(a) for a in ins), in_hbm(advanced), in_vmem(u2), in_vmem(flat), in_vmem(snaps))


def eliminate(pieces, start):
    n = pieces[0].shape[0]
    done = []
    base = 0
    for j in range(0, n, GROUP):
        if j > base:
            done.append([piece[: j - base] for piece in pieces])
            pieces = [piece[j - base :] for piece in pieces]
            base = j
        h = n - base
        rows = lax.broadcasted_iota(jnp.int32, (h, LANES), 0) + base
        spread = []
        for k in range(GROUP):
            column = start + j + k
            spread.append(jnp.broadcast_to(pieces[0][:, column : column + 1], (h, LANES)))
        for k in range(GROUP):
            if k and k % 8 == 0:
                done.append([piece[:8] for piece in pieces])
                pieces = [piece[8:] for piece in pieces]
                spread = [column[8:] for column in spread]
                rows = rows[8:]
                base += 8
            i = k % 8
            pivot = spread[k][i : i + 1, :]
            ratio = jnp.where(rows > j + k, spread[k], 0.0) * (1.0 / pivot)
            for l in range(k + 1, GROUP):
                spread[l] = spread[l] - ratio * spread[l][i : i + 1, :]
            pieces = [piece - ratio * piece[i : i + 1, :] for piece in pieces]
    done.append(pieces)
    pieces = [jnp.concatenate([d[q] for d in done], axis=0) for q in range(len(pieces))]
    row = lax.broadcasted_iota(jnp.int32, (n, LANES), 0)
    lane = lax.broadcasted_iota(jnp.int32, (n, LANES), 1)
    pivots = jnp.sum(jnp.where(lane == row + start, pieces[0], 0.0), axis=1, keepdims=True)
    scale = lax.rsqrt(pivots)
    return [piece * scale for piece in pieces]


def basis_kernel(
    root, w_ref, mine_ref, other_ref, at_ref, modes_ref, snaps_ref, factor_ref, basis_ref, packed, inverse, factor, basis, sems
):
    total = factor.shape[0]
    half = total // 3
    two = 2 * half
    part = total // 2
    core = lax.axis_index("grp") & 1
    packed[pl.ds(pl.multiple_of(core * part, 8), part), :] = mine_ref[0:part, :]
    packed[pl.ds(pl.multiple_of((1 - core) * part, 8), part), :] = other_ref[0:part, :]
    row = lax.broadcasted_iota(jnp.int32, (half, LANES), 0)
    lane = lax.broadcasted_iota(jnp.int32, (half, LANES), 1)
    place = at_ref[at_ref.shape[0] - 8 : at_ref.shape[0] - 7, :]
    late = mine_ref[part:, :] + other_ref[part:, :]
    with_modes = jnp.transpose(jnp.broadcast_to(late[0:1], (LANES, LANES)))
    with_snaps = jnp.transpose(jnp.broadcast_to(late[1:2], (LANES, LANES)))[0:half]
    here = lane == half + place
    first_rows = jnp.where(here, with_modes[0:half], packed[0:half, :])
    second_rows = jnp.where(here, with_modes[half:two], packed[half:two, :])
    ends = jnp.where(here, with_snaps, packed[two:, :])
    ends = jnp.where((row == place) & (lane >= half), pltpu.roll(late[1:2], half, 1), ends)
    left = lane < half
    eye = (row == lane).astype(jnp.float32)
    eye_right = (row + half == lane).astype(jnp.float32)
    r0, w0 = eliminate([jnp.where(left, ends, eye_right), first_rows], 0)
    d = dot(w0, jnp.concatenate([r0, w0], axis=1), 0, 0)
    r1, m1 = eliminate([second_rows - d[0:half, LANES:], jnp.where(left, eye, -d[0:half, 0:LANES])], 0)
    e = dot(r1, jnp.concatenate([r1, m1], axis=1), 0, 0)[half:two]
    r2, m2 = eliminate(
        [
            jnp.where(left, eye, ends - d[half:two, LANES:] - e[:, 0:LANES]),
            jnp.where(left, 0.0, -d[half:two, 0:LANES]) - e[:, LANES:],
        ],
        half,
    )
    wide = pltpu.roll(w_ref[...], half, 1) * root
    inverse[0:half, 0:two] = jnp.where(left, 0.0, r0) * wide
    inverse[half:two, 0:two] = m1 * wide
    inverse[two:, 0:two] = m2 * wide
    zero = jnp.zeros((half, half), jnp.float32)
    inverse[0:half, two:total] = zero
    inverse[half:two, two:total] = zero
    inverse[two:, two:total] = r2[:, 0:half] * root
    scale = 1.0 / root
    factor[0:half, 0:half] = jnp.where(row <= lane, r0, 0.0)[:, 0:half] * scale
    factor[0:half, half:] = w0 * scale
    factor[half:two, 0:half] = zero
    factor[half:two, half:] = jnp.where(row <= lane, r1, 0.0) * scale
    factor[two:, 0:half] = zero
    factor[two:, half:two] = zero
    factor[two:, two:] = jnp.where(row + half <= lane, r2, 0.0)[:, half:] * scale
    copies = [pltpu.make_async_copy(factor, factor_ref, sems.at[0])]
    copies[0].start()
    width = basis.shape[1]
    parts = sems.shape[0] - 1
    chunk = width // parts
    for i in range(parts):
        at = slice(i * chunk, (i + 1) * chunk)
        rows = jnp.concatenate([modes_ref[half:two, at], modes_ref[0:half, at], snaps_ref[:, at]], axis=0)
        basis[:, at] = dot(inverse[:, 0:total], rows)
        copies.append(pltpu.make_async_copy(basis.at[:, at], basis_ref.at[:, at], sems.at[i + 1]))
        copies[-1].start()
    for copy in copies:
        copy.wait()


def basis_call(root, weights, mine, other, at, modes, snaps):
    k, width = modes.shape
    total = k + snaps.shape[0]
    vmem = pl.BlockSpec(memory_space=pltpu.VMEM)
    hbm = pl.BlockSpec(memory_space=pl.ANY)
    return pl.pallas_call(
        functools.partial(basis_kernel, root),
        in_specs=[vmem] * 6,
        out_specs=[hbm, hbm],
        out_shape=[pltpu.HBM((total, total), jnp.float32), pltpu.HBM((total, width), jnp.float32)],
        scratch_shapes=[
            pltpu.VMEM((total, LANES), jnp.float32),
            pltpu.VMEM((total, 2 * LANES), jnp.float32),
            pltpu.VMEM((total, total), jnp.float32),
            pltpu.VMEM((total, width), jnp.float32),
            pltpu.SemaphoreType.DMA((PARTS + 1,)),
        ],
        compiler_params=pltpu.CompilerParams(vmem_limit_bytes=16 * 2**20),
        cost_estimate=pl.CostEstimate(
            flops=12 * total * total * width, bytes_accessed=8 * total * width, transcendentals=0
        ),
        name="factor_and_basis",
    )(*(in_vmem(a) for a in (weights, mine, other, at, modes, snaps)))


def ring(axis):
    count = lax.axis_size(axis)
    forward = [(i, (i + 1) % count) for i in range(count)]
    backward = [(i, (i - 1) % count) for i in range(count)]
    return forward, backward


def swap(array, bits):
    devices = lax.axis_size("tile") * lax.axis_size("grp")
    return lax.ppermute(array, ("tile", "grp"), [(i, i ^ bits) for i in range(devices)])


def per_device(velocity, modes, mode_weights, history, slab_ids, snap_steps):
    ylow, yhigh, xlow, xhigh = faces(velocity)
    up_y, down_y = ring("tile")
    up, down = ring("grp")
    xlo = lax.ppermute(xhigh, "grp", up)
    xhi = lax.ppermute(xlow, "grp", down)
    ylo = lax.ppermute(yhigh, "tile", up_y)
    yhi = lax.ppermute(ylow, "tile", down_y)

    weights = mode_weights.reshape(1, -1)
    comps, nx, ny, nz = velocity.shape
    p1, flat, u2 = inner_call(velocity)
    early, beside, snaps, tall, at, mask = early_gram(
        (nx * ny, nz // LANES), snap_steps, weights, modes, history, slab_ids.reshape(-1, LANES), p1
    )

    clow, chigh = corners(ylo, yhi, early, p1)
    beside = swap(beside, 1)
    clo = lax.ppermute(chigh, "grp", up)
    chi = lax.ppermute(clow, "grp", down)
    p1, flat, u2, advanced = outer_call(velocity, xlo, xhi, ylo, yhi, p1, flat, u2)
    advanced, _, _, snaps, mine = sample_call(
        at, mask, tall, xlo, xhi, clo, chi, clow, chigh, p1, modes, early, beside, advanced, u2, flat, snaps
    )

    devices = lax.axis_size("tile") * lax.axis_size("grp")
    bit = 2
    while bit < devices:
        if 2 * bit < devices:
            far = swap(mine, 3 * bit)
            total = mine + ((far + swap(mine, 2 * bit)) + swap(mine, bit))
        else:
            total = mine + swap(mine, bit)
        mine = total
        bit *= 4
    other = swap(mine, 1)

    root = math.sqrt(modes.shape[1] * devices)
    factor, basis = basis_call(root, weights, mine, other, at, modes, snaps)
    return (advanced, basis, factor)


def solution(mesh):
    return jax.shard_map(
        per_device,
        mesh=mesh,
        in_specs=(
            P(None, "grp", "tile", None),
            P(None, ("tile", "grp")),
            P(),
            P(None, ("tile", "grp")),
            P(("tile", "grp")),
            P(),
        ),
        out_specs=(P(None, "grp", "tile", None), P(None, ("tile", "grp")), P()),
        check_vma=False,
    )
```

```python
import functools
import math

import jax
import jax.numpy as jnp
from jax import lax
from jax.experimental import pallas as pl
from jax.experimental.pallas import tpu as pltpu
from jax.sharding import PartitionSpec as P

time_step = 0.1
viscosity = 0.5
HIGHEST = lax.Precision.HIGHEST
LANES = 128
GROUP = 16
PARTS = 3


def in_hbm(array):
    return pltpu.with_memory_space_constraint(array, pltpu.HBM)


def in_vmem(array):
    return pltpu.with_memory_space_constraint(array, pltpu.VMEM)


def dot(a, b, ca=1, cb=0):
    return lax.dot_general(
        a, b, (((ca,), (cb,)), ((), ())), precision=HIGHEST, preferred_element_type=jnp.float32
    )


def faces_kernel(velocity_ref, ylow_ref, yhigh_ref, xlow_ref, xhigh_ref, sems):
    nx, ny = velocity_ref.shape[1:3]
    copies = [
        pltpu.make_async_copy(velocity_ref.at[:, :, 0:2, :], ylow_ref, sems.at[0]),
        pltpu.make_async_copy(velocity_ref.at[:, :, ny - 2 : ny, :], yhigh_ref, sems.at[1]),
        pltpu.make_async_copy(velocity_ref.at[:, 0:2], xlow_ref, sems.at[2]),
        pltpu.make_async_copy(velocity_ref.at[:, nx - 2 : nx], xhigh_ref, sems.at[3]),
    ]
    for copy in copies:
        copy.start()
    for copy in copies:
        copy.wait()


def faces(velocity):
    comps, nx, ny, nz = velocity.shape
    vmem = pl.BlockSpec(memory_space=pltpu.VMEM)
    across_x = pltpu.VMEM((comps, 2, ny, nz), jnp.float32)
    across_y = pltpu.VMEM((comps, nx, 2, nz), jnp.float32)
    return pl.pallas_call(
        faces_kernel,
        in_specs=[pl.BlockSpec(memory_space=pl.ANY)],
        out_specs=[vmem] * 4,
        out_shape=[across_y, across_y, across_x, across_x],
        scratch_shapes=[pltpu.SemaphoreType.DMA((4,))],
        compiler_params=pltpu.CompilerParams(vmem_limit_bytes=2 * 2**20),
        name="faces",
    )(in_hbm(velocity))


def split(array):
    high = array.astype(jnp.bfloat16)
    rest = array - high.astype(jnp.float32)
    mid = rest.astype(jnp.bfloat16)
    return high, mid, (rest - mid.astype(jnp.float32)).astype(jnp.bfloat16)


def gram_kernel(
    lines, steps_ref, w_ref, modes_ref, history_ref, ids_ref, p1_ref,
    mine_ref, other_ref, snaps_ref, tall_ref, at_ref, mask_ref, gram_ref,
):
    k = modes_ref.shape[0]
    count = snaps_ref.shape[0]
    last = count - 1
    place = jnp.int32(0)
    for j in range(count):
        step = steps_ref[j]
        place = jnp.where(step == last, j, place)
        row = history_ref[pl.ds(jnp.minimum(step, last - 1), 1), :]
        snaps_ref[j : j + 1, :] = jnp.where(step == last, 0.0, row)
    total = k + count
    nt = (((1,), (1,)), ((), ()))
    high, mid, low = split(jnp.concatenate([modes_ref[...], snaps_ref[...]], axis=0))
    first = lax.dot_general(
        jnp.concatenate([high, mid, low], axis=0), high, nt, preferred_element_type=jnp.float32
    )
    second = lax.dot_general(mid, mid, nt, preferred_element_type=jnp.float32)
    side = first[total : 2 * total] + first[2 * total :]
    gram = first[0:total] + (second + (side + jnp.transpose(side)))
    wide = jnp.broadcast_to(w_ref[...], (k, k))
    tall = jnp.transpose(wide)
    tall_ref[...] = tall
    first_rows = gram[0:k, 0:k] * wide * tall
    cross = gram[0:k, k:] * tall[:, 0:count]
    gram_ref[0:count, 0:count] = first_rows[0:count, count:]
    gram_ref[0:count, count:] = cross[0:count]
    gram_ref[count:k, 0:count] = first_rows[count:, count:]
    gram_ref[count:k, count:] = cross[count:]
    gram_ref[k:, 0:count] = first_rows[0:count, 0:count]
    gram_ref[k:, count:] = gram[k:, k:]
    part = mine_ref.shape[0]
    core = lax.axis_index("grp") & 1
    mine_ref[...] = gram_ref[pl.ds(pl.multiple_of(core * part, 8), part), :]
    other_ref[...] = gram_ref[pl.ds(pl.multiple_of((1 - core) * part, 8), part), :]
    ids = ids_ref[...]
    groups = ids.shape[0]
    tiles = lines[1]
    line = lax.shift_right_logical(ids, int(math.log2(LANES)))
    at_ref[0:groups, :] = (line & (tiles - 1)) * lines[0] + lax.shift_right_logical(line, int(math.log2(tiles)))
    at_ref[groups:, :] = jnp.broadcast_to(place, (at_ref.shape[0] - groups, LANES))
    lane = (ids & (LANES - 1)).astype(jnp.float32)
    here = lax.broadcasted_iota(jnp.int32, (LANES, LANES), 1).astype(jnp.float32)
    for i in range(groups):
        there = jnp.transpose(jnp.broadcast_to(lane[i : i + 1, :], (LANES, LANES)))
        mask_ref[i * LANES : (i + 1) * LANES, :] = (here == there).astype(jnp.float32)


def early_gram(lines, steps, weights, modes, history, ids, p1):
    k, width = modes.shape
    count = steps.shape[0]
    total = k + count
    vmem = pl.BlockSpec(memory_space=pltpu.VMEM)
    return pl.pallas_call(
        functools.partial(gram_kernel, lines),
        in_specs=[pl.BlockSpec(memory_space=pltpu.SMEM)] + [vmem] * 5,
        out_specs=[vmem] * 6,
        out_shape=[
            pltpu.VMEM((total // 2, LANES), jnp.float32),
            pltpu.VMEM((total // 2, LANES), jnp.float32),
            pltpu.VMEM((count, width), jnp.float32),
            pltpu.VMEM((k, k), jnp.float32),
            pltpu.VMEM((ids.shape[0] + 8, LANES), jnp.int32),
            pltpu.VMEM((ids.size, LANES), jnp.float32),
        ],
        scratch_shapes=[pltpu.VMEM((total, LANES), jnp.float32)],
        compiler_params=pltpu.CompilerParams(vmem_limit_bytes=16 * 2**20),
        cost_estimate=pl.CostEstimate(
            flops=8 * total * total * width, bytes_accessed=12 * total * width, transcendentals=0
        ),
        name="early_gram",
    )(*(in_vmem(a) for a in (steps, weights, modes, history, ids, p1)))


def stencil(tile, which, inner, store):
    adv = 0.5 * time_step
    diff = time_step * viscosity
    sub = lax.broadcasted_iota(jnp.int32, tile(0, 0, 0).shape, 0)
    first, last = sub == 0, sub == 7
    for t in which:
        before, after = (t - 1) % (inner + 1), (t + 1) % (inner + 1)
        mid = [tile(0, c, t) for c in range(3)]
        scaled = [adv * v for v in mid]
        plus = [diff - v for v in scaled]
        minus = [diff + v for v in scaled]
        for c in range(3):
            v = mid[c]
            y_plus = jnp.where(last, pltpu.roll(tile(0, c, after), 7, 0), pltpu.roll(v, 7, 0))
            y_minus = jnp.where(first, pltpu.roll(tile(0, c, before), 1, 0), pltpu.roll(v, 1, 0))
            out = (1.0 - 6.0 * diff) * v
            out = out + plus[0] * tile(1, c, t) + minus[0] * tile(-1, c, t)
            out = out + plus[1] * y_plus + minus[1] * y_minus
            out = out + plus[2] * pltpu.roll(v, v.shape[1] - 1, 1) + minus[2] * pltpu.roll(v, 1, 1)
            store(c, t, out)


def inner_kernel(velocity_ref, p1, flat, u2):
    comps, nx, ny, nz = velocity_ref.shape
    inner = ny // 8
    zero = jnp.zeros((8, nz), jnp.float32)

    def first_layer(x):
        def tile(k, c, t):
            if t == inner or (isinstance(x, int) and not 0 <= x + k < nx):
                return zero
            return velocity_ref[c, x + k, 8 * t : 8 * t + 8, :]

        def store(c, t, value):
            p1[c, x + 1, 8 * t : 8 * t + 8, :] = value

        stencil(tile, range(inner), inner, store)

    first_layer(0)

    @pl.loop(1, nx - 1, unroll=2)
    def _(x):
        first_layer(x)

    first_layer(nx - 1)

    @pl.loop(2, nx - 2, unroll=2)
    def _(x):
        second_layer(p1, u2, flat, x, range(1, inner - 1))


def second_layer(p1, u2, flat, x, which):
    comps, nx, ny, nz = u2.shape

    def tile(k, c, t):
        return p1[c, x + 1 + k, 8 * t : 8 * t + 8, :]

    def store(c, t, value):
        u2[c, x, 8 * t : 8 * t + 8, :] = value
        for k in range(nz // LANES):
            at = (k * nx + x) * ny + 8 * t
            flat[c, pl.ds(at if isinstance(at, int) else pl.multiple_of(at, 8), 8), :] = value[
                :, k * LANES : (k + 1) * LANES
            ]

    stencil(tile, which, ny // 8, store)


def corners_kernel(ylo_ref, yhi_ref, gram_ref, p1_ref, low_ref, high_ref):
    nx = ylo_ref.shape[1]
    for c in range(ylo_ref.shape[0]):
        low_ref[c, 0:1, :] = ylo_ref[c, 0, 1:2, :]
        low_ref[c, 1:2, :] = yhi_ref[c, 0, 0:1, :]
        high_ref[c, 0:1, :] = ylo_ref[c, nx - 1, 1:2, :]
        high_ref[c, 1:2, :] = yhi_ref[c, nx - 1, 0:1, :]


def corners(ylo, yhi, gram, p1):
    comps, _, _, nz = ylo.shape
    vmem = pl.BlockSpec(memory_space=pltpu.VMEM)
    return pl.pallas_call(
        corners_kernel,
        in_specs=[vmem] * 4,
        out_specs=[vmem, vmem],
        out_shape=[pltpu.VMEM((comps, 2, nz), jnp.float32)] * 2,
        compiler_params=pltpu.CompilerParams(vmem_limit_bytes=1 * 2**20),
        name="corners",
    )(*(in_vmem(a) for a in (ylo, yhi, gram, p1)))


def outer_kernel(
    velocity_ref, xlo_ref, xhi_ref, ylo_ref, yhi_ref, p1_in, flat_in, u2_in,
    p1, flat, u2, advanced_ref, ring_tile, out_sems,
):
    comps, nx, ny, nz = velocity_ref.shape
    inner = ny // 8
    adv = 0.5 * time_step
    diff = time_step * viscosity
    vel = velocity_ref
    for c in range(comps):
        for x in range(nx):
            ring_tile[c, x, 0:2, :] = yhi_ref[c, x]
            ring_tile[c, x, 6:8, :] = ylo_ref[c, x]
    for x in range(nx):
        low = diff + adv * vel[1, x, 0:1, :]
        high = diff - adv * vel[1, x, ny - 1 : ny, :]
        for c in range(comps):
            p1[c, x + 1, 0:1, :] = p1[c, x + 1, 0:1, :] + low * ylo_ref[c, x, 1:2, :]
            p1[c, x + 1, ny - 1 : ny, :] = p1[c, x + 1, ny - 1 : ny, :] + high * yhi_ref[c, x, 0:1, :]
    low = diff + adv * vel[0, 0]
    high = diff - adv * vel[0, nx - 1]
    for c in range(comps):
        p1[c, 1, 0:ny, :] = p1[c, 1, 0:ny, :] + low * xlo_ref[c, 1]
        p1[c, nx, 0:ny, :] = p1[c, nx, 0:ny, :] + high * xhi_ref[c, 0]

    def layer(x, refs, layers, which):
        def tile(k, c, t):
            if t == inner:
                if isinstance(x, int) and not 0 <= x + k < nx:
                    return jnp.zeros((8, nz), jnp.float32)
                return ring_tile[c, x + k]
            return refs[k + 1][c, layers[k + 1], 8 * t : 8 * t + 8, :]

        def store(c, t, value):
            p1[c, x + 1, 8 * t : 8 * t + 8, :] = value

        stencil(tile, which, inner, store)

    layer(-1, (xlo_ref, xlo_ref, vel), (0, 1, 0), range(inner))
    layer(nx, (vel, xhi_ref, xhi_ref), (nx - 1, 0, 1), range(inner))
    layer(0, (vel, vel, vel), (0, 0, 1), (inner,))

    @pl.loop(1, nx - 1, unroll=True)
    def _(x):
        layer(x, (vel, vel, vel), (x - 1, x, x + 1), (inner,))

    layer(nx - 1, (vel, vel, vel), (nx - 2, nx - 1, nx - 1), (inner,))

    def out_copy(x):
        return pltpu.make_async_copy(u2.at[:, x], advanced_ref.at[:, x], out_sems.at[x])

    @pl.loop(2, nx - 2, unroll=True)
    def _(x):
        second_layer(p1, u2, flat, x, (0, inner - 1))
        out_copy(x).start()

    for x in (1, nx - 2):
        second_layer(p1, u2, flat, x, range(inner))
        out_copy(x).start()
    for x in (0, nx - 1):
        second_layer(p1, u2, flat, x, range(inner))

    @pl.loop(1, nx - 1)
    def _(x):
        out_copy(x).wait()


def spaces(velocity):
    comps, nx, ny, nz = velocity.shape
    return (
        pltpu.VMEM((comps, nx + 2, ny + 8, nz), jnp.float32),
        pltpu.VMEM((comps, nx * ny * nz // LANES, LANES), jnp.float32),
        pltpu.VMEM((comps, nx, ny, nz), jnp.float32),
    )


def inner_call(velocity):
    vmem = pl.BlockSpec(memory_space=pltpu.VMEM)
    return pl.pallas_call(
        inner_kernel,
        in_specs=[vmem],
        out_specs=[vmem] * 3,
        out_shape=list(spaces(velocity)),
        compiler_params=pltpu.CompilerParams(vmem_limit_bytes=2 * 2**20),
        cost_estimate=pl.CostEstimate(
            flops=60 * velocity.size, bytes_accessed=4 * velocity.size, transcendentals=0
        ),
        name="inner_cells",
    )(in_vmem(velocity))


def outer_call(velocity, xlo, xhi, ylo, yhi, p1, flat, u2):
    comps, nx, _, nz = velocity.shape
    vmem = pl.BlockSpec(memory_space=pltpu.VMEM)
    return pl.pallas_call(
        outer_kernel,
        in_specs=[vmem] * 8,
        out_specs=[vmem, vmem, vmem, pl.BlockSpec(memory_space=pl.ANY)],
        out_shape=[*spaces(velocity), pltpu.HBM(velocity.shape, jnp.float32)],
        input_output_aliases={5: 0, 6: 1, 7: 2},
        scratch_shapes=[pltpu.VMEM((comps, nx, 8, nz), jnp.float32), pltpu.SemaphoreType.DMA((nx,))],
        compiler_params=pltpu.CompilerParams(vmem_limit_bytes=4 * 2**20),
        cost_estimate=pl.CostEstimate(
            flops=40 * velocity.size, bytes_accessed=4 * velocity.size, transcendentals=0
        ),
        name="outer_cells",
    )(*(in_vmem(a) for a in (velocity, xlo, xhi, ylo, yhi, p1, flat, u2)))


def sample_kernel(
    at_in, mask_ref, tall_ref, xlo_ref, xhi_ref, clo_ref, chi_ref, own_lo_ref, own_hi_ref,
    p1, modes_ref, early_ref, beside_ref, advanced_in, u2_in, flat_in, snaps_in,
    advanced_ref, u2, flat, snaps_ref, sum_ref,
    fixed, picked, at_ref, sems,
):
    at_copy = pltpu.make_async_copy(at_in, at_ref, sems.at[2])
    at_copy.start()
    comps, _, ny, nz = xlo_ref.shape
    nx = flat.shape[1] * LANES // (ny * nz)
    inner = ny // 8
    tiles = nz // LANES
    sub = lax.broadcasted_iota(jnp.int32, (8, nz), 0)
    adv = 0.5 * time_step
    diff = time_step * viscosity

    def halo_tile(line, c):
        return jnp.where(sub == 0, line[c, 1:2, :], line[c, 0:1, :])

    for end, layer, mid, line, own in (
        (0, 0, xlo_ref.at[:, 1], clo_ref, own_lo_ref),
        (1, nx - 1, xhi_ref.at[:, 0], chi_ref, own_hi_ref),
    ):
        sign = 1.0 if end == 0 else -1.0
        outside = layer if end == 0 else layer + 2
        own_x = diff + sign * adv * halo_tile(own, 0)
        low_y = diff + adv * mid[1, 0:8, :]
        high_y = diff - adv * mid[1, ny - 8 : ny, :]
        for c in range(comps):
            corner = halo_tile(line, c)
            halo = p1[c, layer + 1, ny : ny + 8, :] + own_x * corner
            fixed[c, end, 2] = halo
            fixed[c, end, 0] = p1[c, outside, 0:8, :] + jnp.where(sub == 0, low_y * line[c, 0:1, :], 0.0)
            fixed[c, end, 1] = p1[c, outside, ny - 8 : ny, :] + jnp.where(sub == 7, high_y * line[c, 1:2, :], 0.0)

        def tile(k, c, t):
            if k == (-1 if end == 0 else 1):
                return fixed[c, end, 0 if t == 0 else 1]
            if t == inner:
                return fixed[c, end, 2]
            return p1[c, layer + 1 + k, 8 * t : 8 * t + 8, :]

        def store(c, t, value):
            u2[c, layer, 8 * t : 8 * t + 8, :] = value
            for k in range(tiles):
                at = (k * nx + layer) * ny + 8 * t
                flat[c, at : at + 8, :] = value[:, k * LANES : (k + 1) * LANES]

        stencil(tile, (0, inner - 1), inner, store)
    out_copies = [
        pltpu.make_async_copy(u2.at[:, 0], advanced_ref.at[:, 0], sems.at[0]),
        pltpu.make_async_copy(u2.at[:, nx - 1], advanced_ref.at[:, nx - 1], sems.at[1]),
    ]
    for copy in out_copies:
        copy.start()

    count = mask_ref.shape[0]
    groups = count // LANES
    at_copy.wait()

    @pl.loop(0, groups)
    def _(g):
        for first in range(0, LANES, 8):
            ats = [at_ref[g, first + k] for k in range(8)]
            to = pl.multiple_of(g * LANES + first, 8)
            for c in range(comps):
                picked[c, pl.ds(to, 8), :] = jnp.concatenate([flat[c, pl.ds(at, 1), :] for at in ats], axis=0)

    ones = jnp.ones((16, 3 * LANES), jnp.bfloat16)
    parts = []
    for c in range(comps):
        pieces = jnp.concatenate(split(picked[c] * mask_ref[...]), axis=1)
        parts.append(
            lax.dot_general(ones, pieces, (((1,), (1,)), ((), ())), preferred_element_type=jnp.float32)[0:1]
        )
    sample = jnp.concatenate(parts, axis=1)
    place = at_ref[groups, 0]
    snaps_ref[pl.ds(place, 1), :] = sample

    k = modes_ref.shape[0]
    half = snaps_ref.shape[0]
    with_modes = jnp.sum(modes_ref[...] * sample, axis=1, keepdims=True) * tall_ref[...]
    with_snaps = jnp.sum(snaps_ref[...] * sample, axis=1, keepdims=True)
    part = early_ref.shape[0]
    sum_ref[0:part, :] = early_ref[...] + beside_ref[...]
    sum_ref[part:, :] = jnp.zeros((sum_ref.shape[0] - part, LANES), jnp.float32)
    sum_ref[part : part + 1, :] = jnp.transpose(with_modes)[0:1, :]
    sum_ref[part + 1 : part + 2, 0:half] = jnp.transpose(jnp.broadcast_to(with_snaps, (half, LANES)))[0:1, :]
    for copy in out_copies:
        copy.wait()


def sample_call(
    at, mask, tall, xlo, xhi, clo, chi, own_lo, own_hi, p1, modes, early, beside, advanced, u2, flat, snaps
):
    comps, _, _, nz = xlo.shape
    vmem = pl.BlockSpec(memory_space=pltpu.VMEM)
    hbm = pl.BlockSpec(memory_space=pl.ANY)
    ins = (at, mask, tall, xlo, xhi, clo, chi, own_lo, own_hi, p1, modes, early, beside)
    return pl.pallas_call(
        sample_kernel,
        in_specs=[vmem] * 13 + [hbm, vmem, vmem, vmem],
        out_specs=[hbm] + [vmem] * 4,
        out_shape=[
            pltpu.HBM(advanced.shape, jnp.float32),
            pltpu.VMEM(u2.shape, jnp.float32),
            pltpu.VMEM(flat.shape, jnp.float32),
            pltpu.VMEM(snaps.shape, jnp.float32),
            pltpu.VMEM((early.shape[0] + 8, LANES), jnp.float32),
        ],
        input_output_aliases={13: 0, 14: 1, 15: 2, 16: 3},
        scratch_shapes=[
            pltpu.VMEM((comps, 2, 3, 8, nz), jnp.float32),
            pltpu.VMEM((comps, mask.shape[0], LANES), jnp.float32),
            pltpu.SMEM(at.shape, jnp.int32),
            pltpu.SemaphoreType.DMA((3,)),
        ],
        compiler_params=pltpu.CompilerParams(vmem_limit_bytes=8 * 2**20),
        cost_estimate=pl.CostEstimate(
            flops=20 * flat.size, bytes_accessed=2 * flat.size, transcendentals=0
        ),
        name="sample_and_gram",
    )(*(in_vmem(a) for a in ins), in_hbm(advanced), in_vmem(u2), in_vmem(flat), in_vmem(snaps))


def eliminate(pieces, start):
    n = pieces[0].shape[0]
    done = []
    base = 0
    for j in range(0, n, GROUP):
        if j > base:
            done.append([piece[: j - base] for piece in pieces])
            pieces = [piece[j - base :] for piece in pieces]
            base = j
        h = n - base
        rows = lax.broadcasted_iota(jnp.int32, (h, LANES), 0) + base
        spread = []
        for k in range(GROUP):
            column = start + j + k
            spread.append(jnp.broadcast_to(pieces[0][:, column : column + 1], (h, LANES)))
        for k in range(GROUP):
            if k and k % 8 == 0:
                done.append([piece[:8] for piece in pieces])
                pieces = [piece[8:] for piece in pieces]
                spread = [column[8:] for column in spread]
                rows = rows[8:]
                base += 8
            i = k % 8
            pivot = spread[k][i : i + 1, :]
            ratio = jnp.where(rows > j + k, spread[k], 0.0) * (1.0 / pivot)
            for l in range(k + 1, GROUP):
                spread[l] = spread[l] - ratio * spread[l][i : i + 1, :]
            pieces = [piece - ratio * piece[i : i + 1, :] for piece in pieces]
    done.append(pieces)
    pieces = [jnp.concatenate([d[q] for d in done], axis=0) for q in range(len(pieces))]
    row = lax.broadcasted_iota(jnp.int32, (n, LANES), 0)
    lane = lax.broadcasted_iota(jnp.int32, (n, LANES), 1)
    pivots = jnp.sum(jnp.where(lane == row + start, pieces[0], 0.0), axis=1, keepdims=True)
    scale = lax.rsqrt(pivots)
    return [piece * scale for piece in pieces]


def basis_kernel(
    root, w_ref, mine_ref, other_ref, at_ref, modes_ref, snaps_ref, factor_ref, basis_ref, packed, inverse, factor, basis, sems
):
    total = factor.shape[0]
    half = total // 3
    two = 2 * half
    part = total // 2
    core = lax.axis_index("grp") & 1
    packed[pl.ds(pl.multiple_of(core * part, 8), part), :] = mine_ref[0:part, :]
    packed[pl.ds(pl.multiple_of((1 - core) * part, 8), part), :] = other_ref[0:part, :]
    row = lax.broadcasted_iota(jnp.int32, (half, LANES), 0)
    lane = lax.broadcasted_iota(jnp.int32, (half, LANES), 1)
    place = at_ref[at_ref.shape[0] - 8 : at_ref.shape[0] - 7, :]
    late = mine_ref[part:, :] + other_ref[part:, :]
    with_modes = jnp.transpose(jnp.broadcast_to(late[0:1], (LANES, LANES)))
    with_snaps = jnp.transpose(jnp.broadcast_to(late[1:2], (LANES, LANES)))[0:half]
    here = lane == half + place
    first_rows = jnp.where(here, with_modes[0:half], packed[0:half, :])
    second_rows = jnp.where(here, with_modes[half:two], packed[half:two, :])
    ends = jnp.where(here, with_snaps, packed[two:, :])
    ends = jnp.where((row == place) & (lane >= half), pltpu.roll(late[1:2], half, 1), ends)
    left = lane < half
    eye = (row == lane).astype(jnp.float32)
    eye_right = (row + half == lane).astype(jnp.float32)
    r0, w0 = eliminate([jnp.where(left, ends, eye_right), first_rows], 0)
    d = dot(w0, jnp.concatenate([r0, w0], axis=1), 0, 0)
    r1, m1 = eliminate([second_rows - d[0:half, LANES:], jnp.where(left, eye, -d[0:half, 0:LANES])], 0)
    e = dot(r1, jnp.concatenate([r1, m1], axis=1), 0, 0)[half:two]
    r2, m2 = eliminate(
        [
            jnp.where(left, eye, ends - d[half:two, LANES:] - e[:, 0:LANES]),
            jnp.where(left, 0.0, -d[half:two, 0:LANES]) - e[:, LANES:],
        ],
        half,
    )
    wide = pltpu.roll(w_ref[...], half, 1) * root
    inverse[0:half, 0:two] = jnp.where(left, 0.0, r0) * wide
    inverse[half:two, 0:two] = m1 * wide
    inverse[two:, 0:two] = m2 * wide
    zero = jnp.zeros((half, half), jnp.float32)
    inverse[0:half, two:total] = zero
    inverse[half:two, two:total] = zero
    inverse[two:, two:total] = r2[:, 0:half] * root
    scale = 1.0 / root
    factor[0:half, 0:half] = jnp.where(row <= lane, r0, 0.0)[:, 0:half] * scale
    factor[0:half, half:] = w0 * scale
    factor[half:two, 0:half] = zero
    factor[half:two, half:] = jnp.where(row <= lane, r1, 0.0) * scale
    factor[two:, 0:half] = zero
    factor[two:, half:two] = zero
    factor[two:, two:] = jnp.where(row + half <= lane, r2, 0.0)[:, half:] * scale
    copies = [pltpu.make_async_copy(factor, factor_ref, sems.at[0])]
    copies[0].start()
    width = basis.shape[1]
    parts = sems.shape[0] - 1
    chunk = width // parts
    for i in range(parts):
        at = slice(i * chunk, (i + 1) * chunk)
        rows = jnp.concatenate([modes_ref[half:two, at], modes_ref[0:half, at], snaps_ref[:, at]], axis=0)
        basis[:, at] = dot(inverse[:, 0:total], rows)
        copies.append(pltpu.make_async_copy(basis.at[:, at], basis_ref.at[:, at], sems.at[i + 1]))
        copies[-1].start()
    for copy in copies:
        copy.wait()


def basis_call(root, weights, mine, other, at, modes, snaps):
    k, width = modes.shape
    total = k + snaps.shape[0]
    vmem = pl.BlockSpec(memory_space=pltpu.VMEM)
    hbm = pl.BlockSpec(memory_space=pl.ANY)
    return pl.pallas_call(
        functools.partial(basis_kernel, root),
        in_specs=[vmem] * 6,
        out_specs=[hbm, hbm],
        out_shape=[pltpu.HBM((total, total), jnp.float32), pltpu.HBM((total, width), jnp.float32)],
        scratch_shapes=[
            pltpu.VMEM((total, LANES), jnp.float32),
            pltpu.VMEM((total, 2 * LANES), jnp.float32),
            pltpu.VMEM((total, total), jnp.float32),
            pltpu.VMEM((total, width), jnp.float32),
            pltpu.SemaphoreType.DMA((PARTS + 1,)),
        ],
        compiler_params=pltpu.CompilerParams(vmem_limit_bytes=16 * 2**20),
        cost_estimate=pl.CostEstimate(
            flops=12 * total * total * width, bytes_accessed=8 * total * width, transcendentals=0
        ),
        name="factor_and_basis",
    )(*(in_vmem(a) for a in (weights, mine, other, at, modes, snaps)))


def ring(axis):
    count = lax.axis_size(axis)
    forward = [(i, (i + 1) % count) for i in range(count)]
    backward = [(i, (i - 1) % count) for i in range(count)]
    return forward, backward


def swap(array, bits):
    devices = lax.axis_size("tile") * lax.axis_size("grp")
    return lax.ppermute(array, ("tile", "grp"), [(i, i ^ bits) for i in range(devices)])


def per_device(velocity, modes, mode_weights, history, slab_ids, snap_steps):
    ylow, yhigh, xlow, xhigh = faces(velocity)
    up_y, down_y = ring("tile")
    up, down = ring("grp")
    xlo = lax.ppermute(xhigh, "grp", up)
    xhi = lax.ppermute(xlow, "grp", down)
    ylo = lax.ppermute(yhigh, "tile", up_y)
    yhi = lax.ppermute(ylow, "tile", down_y)

    weights = mode_weights.reshape(1, -1)
    comps, nx, ny, nz = velocity.shape
    p1, flat, u2 = inner_call(velocity)
    early, beside, snaps, tall, at, mask = early_gram(
        (nx * ny, nz // LANES), snap_steps, weights, modes, history, slab_ids.reshape(-1, LANES), p1
    )

    clow, chigh = corners(ylo, yhi, early, p1)
    beside = swap(beside, 1)
    clo = lax.ppermute(chigh, "grp", up)
    chi = lax.ppermute(clow, "grp", down)
    p1, flat, u2, advanced = outer_call(velocity, xlo, xhi, ylo, yhi, p1, flat, u2)
    advanced, _, _, snaps, mine = sample_call(
        at, mask, tall, xlo, xhi, clo, chi, clow, chigh, p1, modes, early, beside, advanced, u2, flat, snaps
    )

    devices = lax.axis_size("tile") * lax.axis_size("grp")
    bit = 2
    while bit < devices:
        if 2 * bit < devices:
            far = swap(mine, 3 * bit)
            total = mine + ((far + swap(mine, 2 * bit)) + swap(mine, bit))
        else:
            total = mine + swap(mine, bit)
        mine = total
        bit *= 4
    other = swap(mine, 1)

    root = math.sqrt(modes.shape[1] * devices)
    factor, basis = basis_call(root, weights, mine, other, at, modes, snaps)
    return (advanced, basis, factor)


def solution(mesh):
    return jax.shard_map(
        per_device,
        mesh=mesh,
        in_specs=(
            P(None, "grp", "tile", None),
            P(None, ("tile", "grp")),
            P(),
            P(None, ("tile", "grp")),
            P(("tile", "grp")),
            P(),
        ),
        out_specs=(P(None, "grp", "tile", None), P(None, ("tile", "grp")), P()),
        check_vma=False,
    )
```

```python
import functools
import math

import jax
import jax.numpy as jnp
from jax import lax
from jax.experimental import pallas as pl
from jax.experimental.pallas import tpu as pltpu
from jax.sharding import PartitionSpec as P

time_step = 0.1
viscosity = 0.5
HIGHEST = lax.Precision.HIGHEST
LANES = 128
GROUP = 16
PARTS = 3


def in_hbm(array):
    return pltpu.with_memory_space_constraint(array, pltpu.HBM)


def in_vmem(array):
    return pltpu.with_memory_space_constraint(array, pltpu.VMEM)


def dot(a, b, ca=1, cb=0):
    return lax.dot_general(
        a, b, (((ca,), (cb,)), ((), ())), precision=HIGHEST, preferred_element_type=jnp.float32
    )


def faces_kernel(velocity_ref, ylow_ref, yhigh_ref, xlow_ref, xhigh_ref, sems):
    nx, ny = velocity_ref.shape[1:3]
    copies = [
        pltpu.make_async_copy(velocity_ref.at[:, :, 0:2, :], ylow_ref, sems.at[0]),
        pltpu.make_async_copy(velocity_ref.at[:, :, ny - 2 : ny, :], yhigh_ref, sems.at[1]),
        pltpu.make_async_copy(velocity_ref.at[:, 0:2], xlow_ref, sems.at[2]),
        pltpu.make_async_copy(velocity_ref.at[:, nx - 2 : nx], xhigh_ref, sems.at[3]),
    ]
    for copy in copies:
        copy.start()
    for copy in copies:
        copy.wait()


def faces(velocity):
    comps, nx, ny, nz = velocity.shape
    vmem = pl.BlockSpec(memory_space=pltpu.VMEM)
    across_x = pltpu.VMEM((comps, 2, ny, nz), jnp.float32)
    across_y = pltpu.VMEM((comps, nx, 2, nz), jnp.float32)
    return pl.pallas_call(
        faces_kernel,
        in_specs=[pl.BlockSpec(memory_space=pl.ANY)],
        out_specs=[vmem] * 4,
        out_shape=[across_y, across_y, across_x, across_x],
        scratch_shapes=[pltpu.SemaphoreType.DMA((4,))],
        compiler_params=pltpu.CompilerParams(vmem_limit_bytes=2 * 2**20),
        name="faces",
    )(in_hbm(velocity))


def product(a, pieces):
    n = a.shape[0]
    high, mid, low = split(a)
    first = bf16_dot(jnp.concatenate([high, mid, low], axis=0), pieces[0])
    second = bf16_dot(jnp.concatenate([high, mid], axis=0), pieces[1])
    small = first[2 * n :] + second[n:] + bf16_dot(high, pieces[2])
    return first[0:n] + (first[n : 2 * n] + second[0:n] + small)


def bf16_dot(a, b):
    return lax.dot_general(a, b, (((1,), (0,)), ((), ())), preferred_element_type=jnp.float32)


def split(array):
    high = array.astype(jnp.bfloat16)
    rest = array - high.astype(jnp.float32)
    mid = rest.astype(jnp.bfloat16)
    return high, mid, (rest - mid.astype(jnp.float32)).astype(jnp.bfloat16)


def gram_kernel(
    lines, steps_ref, w_ref, modes_ref, history_ref, ids_ref, p1_ref,
    mine_ref, other_ref, snaps_ref, tall_ref, at_ref, mask_ref, gram_ref,
):
    k = modes_ref.shape[0]
    count = snaps_ref.shape[0]
    last = count - 1
    place = jnp.int32(0)
    for j in range(count):
        step = steps_ref[j]
        place = jnp.where(step == last, j, place)
        row = history_ref[pl.ds(jnp.minimum(step, last - 1), 1), :]
        snaps_ref[j : j + 1, :] = jnp.where(step == last, 0.0, row)
    total = k + count
    nt = (((1,), (1,)), ((), ()))
    high, mid, low = split(jnp.concatenate([modes_ref[...], snaps_ref[...]], axis=0))
    first = lax.dot_general(
        jnp.concatenate([high, mid, low], axis=0), high, nt, preferred_element_type=jnp.float32
    )
    second = lax.dot_general(mid, mid, nt, preferred_element_type=jnp.float32)
    side = first[total : 2 * total] + first[2 * total :]
    gram = first[0:total] + (second + (side + jnp.transpose(side)))
    wide = jnp.broadcast_to(w_ref[...], (k, k))
    tall = jnp.transpose(wide)
    tall_ref[...] = tall
    first_rows = gram[0:k, 0:k] * wide * tall
    cross = gram[0:k, k:] * tall[:, 0:count]
    gram_ref[0:count, 0:count] = first_rows[0:count, count:]
    gram_ref[0:count, count:] = cross[0:count]
    gram_ref[count:k, 0:count] = first_rows[count:, count:]
    gram_ref[count:k, count:] = cross[count:]
    gram_ref[k:, 0:count] = first_rows[0:count, 0:count]
    gram_ref[k:, count:] = gram[k:, k:]
    part = mine_ref.shape[0]
    core = lax.axis_index("grp") & 1
    mine_ref[...] = gram_ref[pl.ds(pl.multiple_of(core * part, 8), part), :]
    other_ref[...] = gram_ref[pl.ds(pl.multiple_of((1 - core) * part, 8), part), :]
    ids = ids_ref[...]
    groups = ids.shape[0]
    tiles = lines[1]
    line = lax.shift_right_logical(ids, int(math.log2(LANES)))
    at_ref[0:groups, :] = (line & (tiles - 1)) * lines[0] + lax.shift_right_logical(line, int(math.log2(tiles)))
    at_ref[groups:, :] = jnp.broadcast_to(place, (at_ref.shape[0] - groups, LANES))
    lane = (ids & (LANES - 1)).astype(jnp.float32)
    here = lax.broadcasted_iota(jnp.int32, (LANES, LANES), 1).astype(jnp.float32)
    for i in range(groups):
        there = jnp.transpose(jnp.broadcast_to(lane[i : i + 1, :], (LANES, LANES)))
        mask_ref[i * LANES : (i + 1) * LANES, :] = (here == there).astype(jnp.float32)


def early_gram(lines, steps, weights, modes, history, ids, p1):
    k, width = modes.shape
    count = steps.shape[0]
    total = k + count
    vmem = pl.BlockSpec(memory_space=pltpu.VMEM)
    return pl.pallas_call(
        functools.partial(gram_kernel, lines),
        in_specs=[pl.BlockSpec(memory_space=pltpu.SMEM)] + [vmem] * 5,
        out_specs=[vmem] * 6,
        out_shape=[
            pltpu.VMEM((total // 2, LANES), jnp.float32),
            pltpu.VMEM((total // 2, LANES), jnp.float32),
            pltpu.VMEM((count, width), jnp.float32),
            pltpu.VMEM((k, k), jnp.float32),
            pltpu.VMEM((ids.shape[0] + 8, LANES), jnp.int32),
            pltpu.VMEM((ids.size, LANES), jnp.float32),
        ],
        scratch_shapes=[pltpu.VMEM((total, LANES), jnp.float32)],
        compiler_params=pltpu.CompilerParams(vmem_limit_bytes=16 * 2**20),
        cost_estimate=pl.CostEstimate(
            flops=8 * total * total * width, bytes_accessed=12 * total * width, transcendentals=0
        ),
        name="early_gram",
    )(*(in_vmem(a) for a in (steps, weights, modes, history, ids, p1)))


def stencil(tile, which, inner, store):
    adv = 0.5 * time_step
    diff = time_step * viscosity
    sub = lax.broadcasted_iota(jnp.int32, tile(0, 0, 0).shape, 0)
    first, last = sub == 0, sub == 7
    for t in which:
        before, after = (t - 1) % (inner + 1), (t + 1) % (inner + 1)
        mid = [tile(0, c, t) for c in range(3)]
        scaled = [adv * v for v in mid]
        plus = [diff - v for v in scaled]
        minus = [diff + v for v in scaled]
        for c in range(3):
            v = mid[c]
            y_plus = jnp.where(last, pltpu.roll(tile(0, c, after), 7, 0), pltpu.roll(v, 7, 0))
            y_minus = jnp.where(first, pltpu.roll(tile(0, c, before), 1, 0), pltpu.roll(v, 1, 0))
            out = (1.0 - 6.0 * diff) * v
            out = out + plus[0] * tile(1, c, t) + minus[0] * tile(-1, c, t)
            out = out + plus[1] * y_plus + minus[1] * y_minus
            out = out + plus[2] * pltpu.roll(v, v.shape[1] - 1, 1) + minus[2] * pltpu.roll(v, 1, 1)
            store(c, t, out)


def inner_kernel(velocity_ref, p1, flat, u2):
    comps, nx, ny, nz = velocity_ref.shape
    inner = ny // 8
    zero = jnp.zeros((8, nz), jnp.float32)

    def first_layer(x):
        def tile(k, c, t):
            if t == inner or (isinstance(x, int) and not 0 <= x + k < nx):
                return zero
            return velocity_ref[c, x + k, 8 * t : 8 * t + 8, :]

        def store(c, t, value):
            p1[c, x + 1, 8 * t : 8 * t + 8, :] = value

        stencil(tile, range(inner), inner, store)

    first_layer(0)

    @pl.loop(1, nx - 1, unroll=2)
    def _(x):
        first_layer(x)

    first_layer(nx - 1)

    @pl.loop(2, nx - 2, unroll=2)
    def _(x):
        second_layer(p1, u2, flat, x, range(1, inner - 1))


def second_layer(p1, u2, flat, x, which):
    comps, nx, ny, nz = u2.shape

    def tile(k, c, t):
        return p1[c, x + 1 + k, 8 * t : 8 * t + 8, :]

    def store(c, t, value):
        u2[c, x, 8 * t : 8 * t + 8, :] = value
        for k in range(nz // LANES):
            at = (k * nx + x) * ny + 8 * t
            flat[c, pl.ds(at if isinstance(at, int) else pl.multiple_of(at, 8), 8), :] = value[
                :, k * LANES : (k + 1) * LANES
            ]

    stencil(tile, which, ny // 8, store)


def corners_kernel(ylo_ref, yhi_ref, gram_ref, p1_ref, low_ref, high_ref):
    nx = ylo_ref.shape[1]
    for c in range(ylo_ref.shape[0]):
        low_ref[c, 0:1, :] = ylo_ref[c, 0, 1:2, :]
        low_ref[c, 1:2, :] = yhi_ref[c, 0, 0:1, :]
        high_ref[c, 0:1, :] = ylo_ref[c, nx - 1, 1:2, :]
        high_ref[c, 1:2, :] = yhi_ref[c, nx - 1, 0:1, :]


def corners(ylo, yhi, gram, p1):
    comps, _, _, nz = ylo.shape
    vmem = pl.BlockSpec(memory_space=pltpu.VMEM)
    return pl.pallas_call(
        corners_kernel,
        in_specs=[vmem] * 4,
        out_specs=[vmem, vmem],
        out_shape=[pltpu.VMEM((comps, 2, nz), jnp.float32)] * 2,
        compiler_params=pltpu.CompilerParams(vmem_limit_bytes=1 * 2**20),
        name="corners",
    )(*(in_vmem(a) for a in (ylo, yhi, gram, p1)))


def outer_kernel(
    velocity_ref, xlo_ref, xhi_ref, ylo_ref, yhi_ref, p1_in, flat_in, u2_in,
    p1, flat, u2, advanced_ref, ring_tile, out_sems,
):
    comps, nx, ny, nz = velocity_ref.shape
    inner = ny // 8
    adv = 0.5 * time_step
    diff = time_step * viscosity
    vel = velocity_ref
    for c in range(comps):
        for x in range(nx):
            ring_tile[c, x, 0:2, :] = yhi_ref[c, x]
            ring_tile[c, x, 6:8, :] = ylo_ref[c, x]
    for x in range(nx):
        low = diff + adv * vel[1, x, 0:1, :]
        high = diff - adv * vel[1, x, ny - 1 : ny, :]
        for c in range(comps):
            p1[c, x + 1, 0:1, :] = p1[c, x + 1, 0:1, :] + low * ylo_ref[c, x, 1:2, :]
            p1[c, x + 1, ny - 1 : ny, :] = p1[c, x + 1, ny - 1 : ny, :] + high * yhi_ref[c, x, 0:1, :]
    low = diff + adv * vel[0, 0]
    high = diff - adv * vel[0, nx - 1]
    for c in range(comps):
        p1[c, 1, 0:ny, :] = p1[c, 1, 0:ny, :] + low * xlo_ref[c, 1]
        p1[c, nx, 0:ny, :] = p1[c, nx, 0:ny, :] + high * xhi_ref[c, 0]

    def layer(x, refs, layers, which):
        def tile(k, c, t):
            if t == inner:
                if isinstance(x, int) and not 0 <= x + k < nx:
                    return jnp.zeros((8, nz), jnp.float32)
                return ring_tile[c, x + k]
            return refs[k + 1][c, layers[k + 1], 8 * t : 8 * t + 8, :]

        def store(c, t, value):
            p1[c, x + 1, 8 * t : 8 * t + 8, :] = value

        stencil(tile, which, inner, store)

    layer(-1, (xlo_ref, xlo_ref, vel), (0, 1, 0), range(inner))
    layer(nx, (vel, xhi_ref, xhi_ref), (nx - 1, 0, 1), range(inner))
    layer(0, (vel, vel, vel), (0, 0, 1), (inner,))

    @pl.loop(1, nx - 1, unroll=True)
    def _(x):
        layer(x, (vel, vel, vel), (x - 1, x, x + 1), (inner,))

    layer(nx - 1, (vel, vel, vel), (nx - 2, nx - 1, nx - 1), (inner,))

    def out_copy(x):
        return pltpu.make_async_copy(u2.at[:, x], advanced_ref.at[:, x], out_sems.at[x])

    @pl.loop(2, nx - 2, unroll=True)
    def _(x):
        second_layer(p1, u2, flat, x, (0, inner - 1))
        out_copy(x).start()

    for x in (1, nx - 2):
        second_layer(p1, u2, flat, x, range(inner))
        out_copy(x).start()
    for x in (0, nx - 1):
        second_layer(p1, u2, flat, x, range(inner))

    @pl.loop(1, nx - 1)
    def _(x):
        out_copy(x).wait()


def spaces(velocity):
    comps, nx, ny, nz = velocity.shape
    return (
        pltpu.VMEM((comps, nx + 2, ny + 8, nz), jnp.float32),
        pltpu.VMEM((comps, nx * ny * nz // LANES, LANES), jnp.float32),
        pltpu.VMEM((comps, nx, ny, nz), jnp.float32),
    )


def inner_call(velocity):
    vmem = pl.BlockSpec(memory_space=pltpu.VMEM)
    return pl.pallas_call(
        inner_kernel,
        in_specs=[vmem],
        out_specs=[vmem] * 3,
        out_shape=list(spaces(velocity)),
        compiler_params=pltpu.CompilerParams(vmem_limit_bytes=2 * 2**20),
        cost_estimate=pl.CostEstimate(
            flops=60 * velocity.size, bytes_accessed=4 * velocity.size, transcendentals=0
        ),
        name="inner_cells",
    )(in_vmem(velocity))


def outer_call(velocity, xlo, xhi, ylo, yhi, p1, flat, u2):
    comps, nx, _, nz = velocity.shape
    vmem = pl.BlockSpec(memory_space=pltpu.VMEM)
    return pl.pallas_call(
        outer_kernel,
        in_specs=[vmem] * 8,
        out_specs=[vmem, vmem, vmem, pl.BlockSpec(memory_space=pl.ANY)],
        out_shape=[*spaces(velocity), pltpu.HBM(velocity.shape, jnp.float32)],
        input_output_aliases={5: 0, 6: 1, 7: 2},
        scratch_shapes=[pltpu.VMEM((comps, nx, 8, nz), jnp.float32), pltpu.SemaphoreType.DMA((nx,))],
        compiler_params=pltpu.CompilerParams(vmem_limit_bytes=4 * 2**20),
        cost_estimate=pl.CostEstimate(
            flops=40 * velocity.size, bytes_accessed=4 * velocity.size, transcendentals=0
        ),
        name="outer_cells",
    )(*(in_vmem(a) for a in (velocity, xlo, xhi, ylo, yhi, p1, flat, u2)))


def sample_kernel(
    at_in, mask_ref, tall_ref, xlo_ref, xhi_ref, clo_ref, chi_ref, own_lo_ref, own_hi_ref,
    p1, modes_ref, early_ref, beside_ref, advanced_in, u2_in, flat_in, snaps_in,
    advanced_ref, u2, flat, snaps_ref, sum_ref,
    fixed, picked, at_ref, sems,
):
    at_copy = pltpu.make_async_copy(at_in, at_ref, sems.at[2])
    at_copy.start()
    comps, _, ny, nz = xlo_ref.shape
    nx = flat.shape[1] * LANES // (ny * nz)
    inner = ny // 8
    tiles = nz // LANES
    sub = lax.broadcasted_iota(jnp.int32, (8, nz), 0)
    adv = 0.5 * time_step
    diff = time_step * viscosity

    def halo_tile(line, c):
        return jnp.where(sub == 0, line[c, 1:2, :], line[c, 0:1, :])

    for end, layer, mid, line, own in (
        (0, 0, xlo_ref.at[:, 1], clo_ref, own_lo_ref),
        (1, nx - 1, xhi_ref.at[:, 0], chi_ref, own_hi_ref),
    ):
        sign = 1.0 if end == 0 else -1.0
        outside = layer if end == 0 else layer + 2
        own_x = diff + sign * adv * halo_tile(own, 0)
        low_y = diff + adv * mid[1, 0:8, :]
        high_y = diff - adv * mid[1, ny - 8 : ny, :]
        for c in range(comps):
            corner = halo_tile(line, c)
            halo = p1[c, layer + 1, ny : ny + 8, :] + own_x * corner
            fixed[c, end, 2] = halo
            fixed[c, end, 0] = p1[c, outside, 0:8, :] + jnp.where(sub == 0, low_y * line[c, 0:1, :], 0.0)
            fixed[c, end, 1] = p1[c, outside, ny - 8 : ny, :] + jnp.where(sub == 7, high_y * line[c, 1:2, :], 0.0)

        def tile(k, c, t):
            if k == (-1 if end == 0 else 1):
                return fixed[c, end, 0 if t == 0 else 1]
            if t == inner:
                return fixed[c, end, 2]
            return p1[c, layer + 1 + k, 8 * t : 8 * t + 8, :]

        def store(c, t, value):
            u2[c, layer, 8 * t : 8 * t + 8, :] = value
            for k in range(tiles):
                at = (k * nx + layer) * ny + 8 * t
                flat[c, at : at + 8, :] = value[:, k * LANES : (k + 1) * LANES]

        stencil(tile, (0, inner - 1), inner, store)
    out_copies = [
        pltpu.make_async_copy(u2.at[:, 0], advanced_ref.at[:, 0], sems.at[0]),
        pltpu.make_async_copy(u2.at[:, nx - 1], advanced_ref.at[:, nx - 1], sems.at[1]),
    ]
    for copy in out_copies:
        copy.start()

    count = mask_ref.shape[0]
    groups = count // LANES
    at_copy.wait()

    @pl.loop(0, groups)
    def _(g):
        for first in range(0, LANES, 8):
            ats = [at_ref[g, first + k] for k in range(8)]
            to = pl.multiple_of(g * LANES + first, 8)
            for c in range(comps):
                picked[c, pl.ds(to, 8), :] = jnp.concatenate([flat[c, pl.ds(at, 1), :] for at in ats], axis=0)

    ones = jnp.ones((16, 3 * LANES), jnp.bfloat16)
    parts = []
    for c in range(comps):
        pieces = jnp.concatenate(split(picked[c] * mask_ref[...]), axis=1)
        parts.append(
            lax.dot_general(ones, pieces, (((1,), (1,)), ((), ())), preferred_element_type=jnp.float32)[0:1]
        )
    sample = jnp.concatenate(parts, axis=1)
    place = at_ref[groups, 0]
    snaps_ref[pl.ds(place, 1), :] = sample

    k = modes_ref.shape[0]
    half = snaps_ref.shape[0]
    with_modes = jnp.sum(modes_ref[...] * sample, axis=1, keepdims=True) * tall_ref[...]
    with_snaps = jnp.sum(snaps_ref[...] * sample, axis=1, keepdims=True)
    part = early_ref.shape[0]
    sum_ref[0:part, :] = early_ref[...] + beside_ref[...]
    sum_ref[part:, :] = jnp.zeros((sum_ref.shape[0] - part, LANES), jnp.float32)
    sum_ref[part : part + 1, :] = jnp.transpose(with_modes)[0:1, :]
    sum_ref[part + 1 : part + 2, 0:half] = jnp.transpose(jnp.broadcast_to(with_snaps, (half, LANES)))[0:1, :]
    for copy in out_copies:
        copy.wait()


def sample_call(
    at, mask, tall, xlo, xhi, clo, chi, own_lo, own_hi, p1, modes, early, beside, advanced, u2, flat, snaps
):
    comps, _, _, nz = xlo.shape
    vmem = pl.BlockSpec(memory_space=pltpu.VMEM)
    hbm = pl.BlockSpec(memory_space=pl.ANY)
    ins = (at, mask, tall, xlo, xhi, clo, chi, own_lo, own_hi, p1, modes, early, beside)
    return pl.pallas_call(
        sample_kernel,
        in_specs=[vmem] * 13 + [hbm, vmem, vmem, vmem],
        out_specs=[hbm] + [vmem] * 4,
        out_shape=[
            pltpu.HBM(advanced.shape, jnp.float32),
            pltpu.VMEM(u2.shape, jnp.float32),
            pltpu.VMEM(flat.shape, jnp.float32),
            pltpu.VMEM(snaps.shape, jnp.float32),
            pltpu.VMEM((early.shape[0] + 8, LANES), jnp.float32),
        ],
        input_output_aliases={13: 0, 14: 1, 15: 2, 16: 3},
        scratch_shapes=[
            pltpu.VMEM((comps, 2, 3, 8, nz), jnp.float32),
            pltpu.VMEM((comps, mask.shape[0], LANES), jnp.float32),
            pltpu.SMEM(at.shape, jnp.int32),
            pltpu.SemaphoreType.DMA((3,)),
        ],
        compiler_params=pltpu.CompilerParams(vmem_limit_bytes=8 * 2**20),
        cost_estimate=pl.CostEstimate(
            flops=20 * flat.size, bytes_accessed=2 * flat.size, transcendentals=0
        ),
        name="sample_and_gram",
    )(*(in_vmem(a) for a in ins), in_hbm(advanced), in_vmem(u2), in_vmem(flat), in_vmem(snaps))


def eliminate(pieces, start):
    n = pieces[0].shape[0]
    done = []
    base = 0
    for j in range(0, n, GROUP):
        if j > base:
            done.append([piece[: j - base] for piece in pieces])
            pieces = [piece[j - base :] for piece in pieces]
            base = j
        h = n - base
        rows = lax.broadcasted_iota(jnp.int32, (h, LANES), 0) + base
        spread = []
        for k in range(GROUP):
            column = start + j + k
            spread.append(jnp.broadcast_to(pieces[0][:, column : column + 1], (h, LANES)))
        for k in range(GROUP):
            if k and k % 8 == 0:
                done.append([piece[:8] for piece in pieces])
                pieces = [piece[8:] for piece in pieces]
                spread = [column[8:] for column in spread]
                rows = rows[8:]
                base += 8
            i = k % 8
            pivot = spread[k][i : i + 1, :]
            ratio = jnp.where(rows > j + k, spread[k], 0.0) * (1.0 / pivot)
            for l in range(k + 1, GROUP):
                spread[l] = spread[l] - ratio * spread[l][i : i + 1, :]
            pieces = [piece - ratio * piece[i : i + 1, :] for piece in pieces]
    done.append(pieces)
    pieces = [jnp.concatenate([d[q] for d in done], axis=0) for q in range(len(pieces))]
    row = lax.broadcasted_iota(jnp.int32, (n, LANES), 0)
    lane = lax.broadcasted_iota(jnp.int32, (n, LANES), 1)
    pivots = jnp.sum(jnp.where(lane == row + start, pieces[0], 0.0), axis=1, keepdims=True)
    scale = lax.rsqrt(pivots)
    return [piece * scale for piece in pieces]


def basis_kernel(
    root, w_ref, mine_ref, other_ref, at_ref, modes_ref, snaps_ref, factor_ref, basis_ref, packed, factor, basis, pieces, sems
):
    total = factor.shape[0]
    half = total // 3
    two = 2 * half
    part = total // 2
    core = lax.axis_index("grp") & 1
    packed[pl.ds(pl.multiple_of(core * part, 8), part), :] = mine_ref[0:part, :]
    packed[pl.ds(pl.multiple_of((1 - core) * part, 8), part), :] = other_ref[0:part, :]
    row = lax.broadcasted_iota(jnp.int32, (half, LANES), 0)
    lane = lax.broadcasted_iota(jnp.int32, (half, LANES), 1)
    place = at_ref[at_ref.shape[0] - 8 : at_ref.shape[0] - 7, :]
    late = mine_ref[part:, :] + other_ref[part:, :]
    with_modes = jnp.transpose(jnp.broadcast_to(late[0:1], (LANES, LANES)))
    with_snaps = jnp.transpose(jnp.broadcast_to(late[1:2], (LANES, LANES)))[0:half]
    here = lane == half + place
    first_rows = jnp.where(here, with_modes[0:half], packed[0:half, :])
    second_rows = jnp.where(here, with_modes[half:two], packed[half:two, :])
    ends = jnp.where(here, with_snaps, packed[two:, :])
    ends = jnp.where((row == place) & (lane >= half), pltpu.roll(late[1:2], half, 1), ends)
    left = lane < half
    eye = (row == lane).astype(jnp.float32)
    eye_right = (row + half == lane).astype(jnp.float32)
    r0, w0 = eliminate([jnp.where(left, ends, eye_right), first_rows], 0)
    d = dot(w0, jnp.concatenate([r0, w0], axis=1), 0, 0)
    r1, m1 = eliminate([second_rows - d[0:half, LANES:], jnp.where(left, eye, -d[0:half, 0:LANES])], 0)
    e = dot(r1, jnp.concatenate([r1, m1], axis=1), 0, 0)[half:two]
    wide = pltpu.roll(w_ref[...], half, 1) * root
    above = jnp.concatenate([jnp.where(left, 0.0, r0) * wide, m1 * wide], axis=0)
    width = basis.shape[1]
    parts = sems.shape[0] - 2
    chunk = width // parts
    for i in range(parts):
        at = slice(i * chunk, (i + 1) * chunk)
        rows = jnp.concatenate([modes_ref[half:two, at], modes_ref[0:half, at], snaps_ref[:, at]], axis=0)
        for k, piece in enumerate(split(rows)):
            pieces[k, :, at] = piece
        basis[0:two, at] = product(above, [pieces[k, 0:two, at] for k in range(3)])
    r2, m2 = eliminate(
        [
            jnp.where(left, eye, ends - d[half:two, LANES:] - e[:, 0:LANES]),
            jnp.where(left, 0.0, -d[half:two, 0:LANES]) - e[:, LANES:],
        ],
        half,
    )
    copies = [pltpu.make_async_copy(basis.at[0:two], basis_ref.at[0:two], sems.at[0])]
    copies[0].start()
    below = jnp.concatenate([m2 * wide, r2[:, 0:half] * root], axis=1)
    zero = jnp.zeros((half, half), jnp.float32)
    scale = 1.0 / root
    factor[0:half, 0:half] = jnp.where(row <= lane, r0, 0.0)[:, 0:half] * scale
    factor[0:half, half:] = w0 * scale
    factor[half:two, 0:half] = zero
    factor[half:two, half:] = jnp.where(row <= lane, r1, 0.0) * scale
    factor[two:, 0:half] = zero
    factor[two:, half:two] = zero
    factor[two:, two:] = jnp.where(row + half <= lane, r2, 0.0)[:, half:] * scale
    copies.append(pltpu.make_async_copy(factor, factor_ref, sems.at[1]))
    copies[1].start()
    for i in range(parts):
        at = slice(i * chunk, (i + 1) * chunk)
        basis[two:, at] = product(below, [pieces[k, :, at] for k in range(3)])
        copies.append(pltpu.make_async_copy(basis.at[two:, at], basis_ref.at[two:, at], sems.at[i + 2]))
        copies[-1].start()
    for copy in copies:
        copy.wait()


def basis_call(root, weights, mine, other, at, modes, snaps):
    k, width = modes.shape
    total = k + snaps.shape[0]
    vmem = pl.BlockSpec(memory_space=pltpu.VMEM)
    hbm = pl.BlockSpec(memory_space=pl.ANY)
    return pl.pallas_call(
        functools.partial(basis_kernel, root),
        in_specs=[vmem] * 6,
        out_specs=[hbm, hbm],
        out_shape=[pltpu.HBM((total, total), jnp.float32), pltpu.HBM((total, width), jnp.float32)],
        scratch_shapes=[
            pltpu.VMEM((total, LANES), jnp.float32),
            pltpu.VMEM((total, total), jnp.float32),
            pltpu.VMEM((total, width), jnp.float32),
            pltpu.VMEM((3, total, width), jnp.bfloat16),
            pltpu.SemaphoreType.DMA((PARTS + 2,)),
        ],
        compiler_params=pltpu.CompilerParams(vmem_limit_bytes=16 * 2**20),
        cost_estimate=pl.CostEstimate(
            flops=12 * total * total * width, bytes_accessed=8 * total * width, transcendentals=0
        ),
        name="factor_and_basis",
    )(*(in_vmem(a) for a in (weights, mine, other, at, modes, snaps)))


def ring(axis):
    count = lax.axis_size(axis)
    forward = [(i, (i + 1) % count) for i in range(count)]
    backward = [(i, (i - 1) % count) for i in range(count)]
    return forward, backward


def swap(array, bits):
    devices = lax.axis_size("tile") * lax.axis_size("grp")
    return lax.ppermute(array, ("tile", "grp"), [(i, i ^ bits) for i in range(devices)])


def per_device(velocity, modes, mode_weights, history, slab_ids, snap_steps):
    ylow, yhigh, xlow, xhigh = faces(velocity)
    up_y, down_y = ring("tile")
    up, down = ring("grp")
    xlo = lax.ppermute(xhigh, "grp", up)
    xhi = lax.ppermute(xlow, "grp", down)
    ylo = lax.ppermute(yhigh, "tile", up_y)
    yhi = lax.ppermute(ylow, "tile", down_y)

    weights = mode_weights.reshape(1, -1)
    comps, nx, ny, nz = velocity.shape
    p1, flat, u2 = inner_call(velocity)
    early, beside, snaps, tall, at, mask = early_gram(
        (nx * ny, nz // LANES), snap_steps, weights, modes, history, slab_ids.reshape(-1, LANES), p1
    )

    clow, chigh = corners(ylo, yhi, early, p1)
    beside = swap(beside, 1)
    clo = lax.ppermute(chigh, "grp", up)
    chi = lax.ppermute(clow, "grp", down)
    p1, flat, u2, advanced = outer_call(velocity, xlo, xhi, ylo, yhi, p1, flat, u2)
    advanced, _, _, snaps, mine = sample_call(
        at, mask, tall, xlo, xhi, clo, chi, clow, chigh, p1, modes, early, beside, advanced, u2, flat, snaps
    )

    devices = lax.axis_size("tile") * lax.axis_size("grp")
    bit = 2
    while bit < devices:
        if 2 * bit < devices:
            far = swap(mine, 3 * bit)
            total = mine + ((far + swap(mine, 2 * bit)) + swap(mine, bit))
        else:
            total = mine + swap(mine, bit)
        mine = total
        bit *= 4
    other = swap(mine, 1)

    root = math.sqrt(modes.shape[1] * devices)
    factor, basis = basis_call(root, weights, mine, other, at, modes, snaps)
    return (advanced, basis, factor)


def solution(mesh):
    return jax.shard_map(
        per_device,
        mesh=mesh,
        in_specs=(
            P(None, "grp", "tile", None),
            P(None, ("tile", "grp")),
            P(),
            P(None, ("tile", "grp")),
            P(("tile", "grp")),
            P(),
        ),
        out_specs=(P(None, "grp", "tile", None), P(None, ("tile", "grp")), P()),
        check_vma=False,
    )
```
